32 devices in a mesh: grp: 4 (over x, core), dev: 8 (over z, y).
Axes of the slice: x: 2, y: 2, z: 4, core: 2. Of those that a mesh axis runs over, the one named last changes fastest.
Arguments:
- key_tokens: bfloat16 [4096, 768], P(('grp', 'dev')), may hold values from -6 to 6
- value_tokens: bfloat16 [4096, 768], P(('grp', 'dev')), may hold values from -6 to 6
- queries: bfloat16 [4096, 768], P(('grp', 'dev')), may hold values from -192 to 192
- token_rate: float32 [4096], P(('grp', 'dev')), may hold values from 0.0005638186 to 0.004510549
- fast_weights: bfloat16 [3, 1536, 768], P(None, ('grp', 'dev')), may hold values from -0.21875 to 0.21875
Outputs:
- target_out: bfloat16 [4096, 768], P(('grp', 'dev'))
The draws below stay inside these ranges and needn't reach their ends.
All inputs are finite; a program needn't handle non-finite values.
Results may differ from the reference program's by a relative error of at most 0.012.
The reference program's roundings to bfloat16 on the way count: a program that leaves them out, or rounds other values in their place, can miss the bound.
Values may be sent and summed in bfloat16 or wider, within the bound.
No kernel may reach another device: no remote copies, remote signals or barrier semaphores. Data moves between devices by JAX's collectives and lax.ppermute only.
A program may use at most 64 MiB of HBM per device.

```python
import math
import jax
import jax.numpy as jnp
from jax import lax

D = 768
HID = 1536
HEADS = 12
HEAD_DIM = 64
TOK_DEV = 128
Q_DEV = 128
TOKENS = 4096
QUERIES = 4096


def drawn_pair(key):
    seeded = jax.random.fold_in(key, 7)
    first, second = jax.random.split(seeded, 2)
    block_count = TOKENS // TOK_DEV
    key_draw = jax.random.truncated_normal(first, -6.0, 6.0, (block_count, TOK_DEV, D), jnp.float32)
    query_draw = jax.random.truncated_normal(second, -6.0, 6.0, (block_count, Q_DEV, D), jnp.float32)
    return (key_draw.reshape(TOKENS, D), query_draw.reshape(QUERIES, D))


def draw_key_tokens(key, part):
    return drawn_pair(key)[0].astype(jnp.bfloat16)


def draw_queries(key, part):
    return drawn_pair(key)[1].astype(jnp.bfloat16)


def block_scale(key, shape, cuts, least, top_value):
    loudness, own = 1.0, jax.random.fold_in(key, 6)
    for axis_at, parts in cuts:
        steps = jnp.exp(jax.random.uniform(jax.random.fold_in(own, axis_at), (parts,), jnp.float32, least / len(cuts), top_value / len(cuts)))
        loudness = loudness * jnp.repeat(steps, shape[axis_at] // parts).reshape([-1 if axis == axis_at else 1 for axis in range(len(shape))])
    return loudness


def scatter_about(own_key, shape, spread, most, pieces=(), held_as=jnp.bfloat16):
    entries = spread * jax.random.normal(own_key, shape, jnp.float32)
    if pieces:
        entries = entries * block_scale(own_key, shape, pieces, -0.22, 0.18)
    return jnp.clip(entries, -most, most).astype(held_as)


def setup_inputs(seed: int = 0) -> dict:
    arg_keys = jax.random.split(jax.random.key(seed), 6)
    return {
        "key_tokens": draw_key_tokens(jax.random.fold_in(arg_keys[5], 71), 0),
        "value_tokens": scatter_about(arg_keys[1], (TOKENS, D), 1.0, 6.0, ((0, 32),)),
        "queries": draw_queries(jax.random.fold_in(arg_keys[5], 71), 0),
        "token_rate": jnp.clip(jnp.exp(math.log(0.004510549) - 2.0794415 * jax.random.uniform(arg_keys[3], (TOKENS,), jnp.float32) ** block_scale(arg_keys[3], (TOKENS,), ((0, 32),), -0.2, 0.2)), 0.0005638186, 0.004510549),
        "fast_weights": scatter_about(arg_keys[4], (3, HID, D), D ** -0.5, 0.21875, ((1, 32),)),
    }


epsilon = 1e-06

def rms_rows(matrix):
    return matrix / jnp.sqrt(lax.optimization_barrier(jnp.mean(matrix * matrix, axis=-1, keepdims=True)) + epsilon)

def gradient_rows(weights, key_normed, signal):
    gate_act = jnp.dot(key_normed, weights[0].T, preferred_element_type=jnp.float32)
    up_act = jnp.dot(key_normed, weights[1].T, preferred_element_type=jnp.float32)
    sigmoid_gate = jax.nn.sigmoid(gate_act)
    silu_gate = gate_act * sigmoid_gate
    hidden_bf = (silu_gate * up_act).astype(jnp.bfloat16)
    down_grad = jnp.dot(hidden_bf.T, signal, preferred_element_type=jnp.float32)
    hidden_grad = jnp.dot(signal, weights[2].T, preferred_element_type=jnp.float32)
    gate_grad = (hidden_grad * up_act * sigmoid_gate * (1.0 + gate_act * (1.0 - sigmoid_gate))).astype(jnp.bfloat16)
    up_grad = (hidden_grad * silu_gate).astype(jnp.bfloat16)
    return jnp.stack([jnp.dot(gate_grad.T, key_normed, preferred_element_type=jnp.float32), jnp.dot(up_grad.T, key_normed, preferred_element_type=jnp.float32), down_grad])

def fast_apply(weights, query_normed):
    gate_act = jnp.dot(query_normed, weights[0].T, preferred_element_type=jnp.float32)
    up_act = jnp.dot(query_normed, weights[1].T, preferred_element_type=jnp.float32)
    hidden_bf = (jax.nn.silu(gate_act) * up_act).astype(jnp.bfloat16)
    return jnp.dot(hidden_bf, weights[2], preferred_element_type=jnp.float32)

def local_attention(query_block, key_block, value_block):
    query_count = query_block.shape[0]
    key_count = key_block.shape[0]
    query_heads = query_block.astype(jnp.float32).reshape(query_count, HEADS, HEAD_DIM)
    key_heads = key_block.astype(jnp.float32).reshape(key_count, HEADS, HEAD_DIM)
    value_heads = value_block.astype(jnp.float32).reshape(key_count, HEADS, HEAD_DIM)
    scores = jnp.einsum('qhe,khe->hqk', query_heads, key_heads) * HEAD_DIM ** (-0.5)
    weights_bf = jax.nn.softmax(scores, axis=-1).astype(jnp.bfloat16)
    mixed = jnp.einsum('hqk,khe->qhe', weights_bf.astype(jnp.float32), value_heads)
    return mixed.reshape(query_count, D)

def reference(key_tokens, value_tokens, queries, token_rate, fast_weights):
    block_count = TOKENS // TOK_DEV
    key_normed = rms_rows(key_tokens.astype(jnp.float32)).astype(jnp.bfloat16)
    signal = (-(token_rate[:, None] * value_tokens.astype(jnp.float32))).astype(jnp.bfloat16)

    def accumulate(running, pair):
        return (running + gradient_rows(fast_weights, pair[0], pair[1]), None)
    gradient, _ = lax.scan(accumulate, jnp.zeros((3, HID, D), jnp.float32), (key_normed.reshape(block_count, TOK_DEV, D), signal.reshape(block_count, TOK_DEV, D)))
    old_rows = fast_weights.astype(jnp.float32)
    stepped = old_rows - gradient
    updated = (stepped * jnp.sqrt(lax.optimization_barrier(jnp.mean(old_rows * old_rows, axis=-1, keepdims=True)) + epsilon) / jnp.sqrt(lax.optimization_barrier(jnp.mean(stepped * stepped, axis=-1, keepdims=True)) + epsilon)).astype(jnp.bfloat16)
    query_normed = rms_rows(queries.astype(jnp.float32)).astype(jnp.bfloat16)

    def per_block(group):
        query_block, key_block, value_block, normed_block = group
        total = fast_apply(updated, normed_block) + local_attention(query_block, key_block, value_block)
        return total.astype(jnp.bfloat16)
    result = lax.map(per_block, (queries.reshape(block_count, Q_DEV, D), key_tokens.reshape(block_count, TOK_DEV, D), value_tokens.reshape(block_count, TOK_DEV, D), query_normed.reshape(block_count, Q_DEV, D)))
    return result.reshape(QUERIES, D)
```

```python
import jax
import jax.numpy as jnp
from jax import lax
from jax.sharding import PartitionSpec as P

D = 768
HEADS = 12
HEAD_DIM = 64
CORES = 2
NEAR = 2

epsilon = 1e-06
AXES = ("grp", "dev")


def rms_rows(matrix):
    return matrix / jnp.sqrt(jnp.mean(matrix * matrix, axis=-1, keepdims=True) + epsilon)


def moves(mesh):
    n_grp, n_dev = mesh.shape["grp"], mesh.shape["dev"]
    n_gx, n_far = n_grp // CORES, n_dev // NEAR

    def build(target):
        pairs = []
        for gx in range(n_gx):
            for core in range(CORES):
                for far in range(n_far):
                    for near in range(NEAR):
                        to = target(gx, core, far, near)
                        source = (gx * CORES + core) * n_dev + far * NEAR + near
                        dest = (to[0] * CORES + to[1]) * n_dev + to[2] * NEAR + to[3]
                        pairs.append((source, dest))
        return pairs

    def along(step):
        return build(lambda gx, core, far, near: (gx, core, (far + step) % n_far, near))

    def layer(dx, dn):
        return build(lambda gx, core, far, near: ((gx + dx) % n_gx, core, far, (near + dn) % NEAR))

    def layer_back(dx, dn):
        return build(lambda gx, core, far, near: ((gx - dx) % n_gx, core, far, (near - dn) % NEAR))

    swap = build(lambda gx, core, far, near: (gx, 1 - core, far, near))
    offsets = [(dx, dn) for dx in range(n_gx) for dn in range(NEAR)]
    return n_far, along, layer, layer_back, swap, offsets


def send(array, pairs):
    return lax.ppermute(array, AXES, pairs)


def local_attention(query_block, key_block, value_block):
    query_count = query_block.shape[0]
    key_count = key_block.shape[0]
    query_heads = query_block.reshape(query_count, HEADS, HEAD_DIM)
    key_heads = key_block.reshape(key_count, HEADS, HEAD_DIM)
    value_heads = value_block.reshape(key_count, HEADS, HEAD_DIM)
    scores = jnp.einsum(
        "qhe,khe->hqk", query_heads, key_heads, preferred_element_type=jnp.float32
    ) * HEAD_DIM ** (-0.5)
    weights_bf = jax.nn.softmax(scores, axis=-1).astype(jnp.bfloat16)
    mixed = jnp.einsum("hqk,khe->qhe", weights_bf, value_heads, preferred_element_type=jnp.float32)
    return mixed.reshape(query_count, D)


def gradient_rows(weights, key_normed, signal):
    gate_act = jnp.dot(key_normed, weights[0].T, preferred_element_type=jnp.float32)
    up_act = jnp.dot(key_normed, weights[1].T, preferred_element_type=jnp.float32)
    sigmoid_gate = jax.nn.sigmoid(gate_act)
    silu_gate = gate_act * sigmoid_gate
    hidden_bf = (silu_gate * up_act).astype(jnp.bfloat16)
    down_grad = jnp.dot(hidden_bf.T, signal, preferred_element_type=jnp.float32)
    hidden_grad = jnp.dot(signal, weights[2].T, preferred_element_type=jnp.float32)
    gate_grad = (
        hidden_grad * up_act * sigmoid_gate * (1.0 + gate_act * (1.0 - sigmoid_gate))
    ).astype(jnp.bfloat16)
    up_grad = (hidden_grad * silu_gate).astype(jnp.bfloat16)
    return jnp.stack(
        [
            jnp.dot(gate_grad.T, key_normed, preferred_element_type=jnp.float32),
            jnp.dot(up_grad.T, key_normed, preferred_element_type=jnp.float32),
            down_grad,
        ]
    )


def normalize_rows(old_bf, grad_rows):
    old_rows = old_bf.astype(jnp.float32)
    stepped = old_rows - grad_rows
    return (
        stepped
        * jnp.sqrt(jnp.mean(old_rows * old_rows, axis=-1, keepdims=True) + epsilon)
        / jnp.sqrt(jnp.mean(stepped * stepped, axis=-1, keepdims=True) + epsilon)
    ).astype(jnp.bfloat16)


def solution(mesh):
    n_far, along, layer, layer_back, swap, offsets = moves(mesh)

    def body(key_tokens, value_tokens, queries, token_rate, fast_weights):
        rows = fast_weights.shape[1]
        count = queries.shape[0]
        line_weights = [fast_weights] + [send(fast_weights, along(-k)) for k in range(1, n_far)]

        key_normed = rms_rows(key_tokens.astype(jnp.float32)).astype(jnp.bfloat16)
        signal = (-(token_rate[:, None] * value_tokens.astype(jnp.float32))).astype(jnp.bfloat16)
        pair = jnp.stack([key_normed, signal])
        here = [pair if o == (0, 0) else send(pair, layer(*o)) for o in offsets]
        there = [send(block, swap) for block in here]
        tokens = jnp.concatenate(here + there, axis=1)

        query_normed = rms_rows(queries.astype(jnp.float32)).astype(jnp.bfloat16)
        q_here = [query_normed if o == (0, 0) else send(query_normed, layer_back(*o)) for o in offsets]
        q_there = [send(block, swap) for block in q_here]
        all_queries = jnp.concatenate(q_here + q_there, axis=0)

        weights = jnp.concatenate(line_weights, axis=1)
        grad = gradient_rows(weights, tokens[0], tokens[1])
        grad_bf = grad.astype(jnp.bfloat16)
        total = grad[:, :rows]
        for k in range(1, n_far):
            total = total + send(grad_bf[:, k * rows:(k + 1) * rows], along(k)).astype(jnp.float32)
        updated = normalize_rows(fast_weights, total)
        stepped = jnp.concatenate(
            [updated] + [send(updated, along(-k)) for k in range(1, n_far)], axis=1
        )

        gate_act = jnp.dot(all_queries, stepped[0].T, preferred_element_type=jnp.float32)
        up_act = jnp.dot(all_queries, stepped[1].T, preferred_element_type=jnp.float32)
        hidden_bf = (jax.nn.silu(gate_act) * up_act).astype(jnp.bfloat16)
        partial = jnp.dot(hidden_bf, stepped[2], preferred_element_type=jnp.float32)
        half = len(offsets) * count
        mine = partial[:half] + send(partial[half:].astype(jnp.bfloat16), swap).astype(jnp.float32)
        result = local_attention(queries, key_tokens, value_tokens)
        for j, o in enumerate(offsets):
            block = mine[j * count:(j + 1) * count]
            if o == (0, 0):
                result = result + block
            else:
                result = result + send(block.astype(jnp.bfloat16), layer(*o)).astype(jnp.float32)
        return result.astype(jnp.bfloat16)

    in_specs = (
        P(("grp", "dev"), None),
        P(("grp", "dev"), None),
        P(("grp", "dev"), None),
        P(("grp", "dev")),
        P(None, ("grp", "dev"), None),
    )
    out_specs = P(("grp", "dev"), None)
    return jax.shard_map(body, mesh=mesh, in_specs=in_specs, out_specs=out_specs, check_vma=False)
```

```python
import jax
import jax.numpy as jnp
from jax import lax
from jax.experimental import pallas as pl
from jax.experimental.pallas import tpu as pltpu
from jax.sharding import PartitionSpec as P

D = 768
HEADS = 12
HEAD_DIM = 64
CORES = 2
NEAR = 2
BF = jnp.bfloat16
F32 = jnp.float32

epsilon = 1e-06
AXES = ("grp", "dev")


def moves(mesh):
    n_grp, n_dev = mesh.shape["grp"], mesh.shape["dev"]
    n_gx, n_far = n_grp // CORES, n_dev // NEAR

    def build(target):
        pairs = []
        for gx in range(n_gx):
            for core in range(CORES):
                for far in range(n_far):
                    for near in range(NEAR):
                        to = target(gx, core, far, near)
                        source = (gx * CORES + core) * n_dev + far * NEAR + near
                        dest = (to[0] * CORES + to[1]) * n_dev + to[2] * NEAR + to[3]
                        pairs.append((source, dest))
        return pairs

    def along(step):
        return build(lambda gx, core, far, near: (gx, core, (far + step) % n_far, near))

    def layer(dx, dn):
        return build(lambda gx, core, far, near: ((gx + dx) % n_gx, core, far, (near + dn) % NEAR))

    swap = build(lambda gx, core, far, near: (gx, 1 - core, far, near))
    offsets = [(dx, dn) for dx in reversed(range(n_gx)) for dn in reversed(range(NEAR))][:-1]
    return n_far, along, layer, swap, offsets


def send(array, pairs):
    return lax.ppermute(array, AXES, pairs)


def after(value, *others):
    return lax.optimization_barrier((value, *others))[0]


def call(kernel, outs, *args, flops=0, scratch=(), name=None):
    vmem = pl.BlockSpec(memory_space=pltpu.VMEM)
    size = sum(a.size * a.dtype.itemsize for a in args) + sum(o.size * o.dtype.itemsize for o in outs)
    result = pl.pallas_call(
        kernel,
        out_shape=list(outs),
        in_specs=[vmem] * len(args),
        out_specs=[vmem] * len(outs),
        scratch_shapes=list(scratch),
        compiler_params=pltpu.CompilerParams(vmem_limit_bytes=32 * 1024 * 1024),
        cost_estimate=pl.CostEstimate(flops=flops, bytes_accessed=size, transcendentals=0),
        name=name,
    )(*args)
    return result


def struct(shape, dtype):
    return jax.ShapeDtypeStruct(shape, dtype)


def nt(a, b):
    return lax.dot_general(a, b, (((1,), (1,)), ((), ())), preferred_element_type=F32)


def nn(a, b):
    return lax.dot_general(a, b, (((1,), (0,)), ((), ())), preferred_element_type=F32)


def rms(matrix):
    return matrix / jnp.sqrt(jnp.mean(matrix * matrix, axis=-1, keepdims=True) + epsilon)


def prep_kernel(key_ref, value_ref, query_ref, rate_ref, pair_ref, query_out):
    count = key_ref.shape[0]
    pair_ref[0] = rms(key_ref[...].astype(F32)).astype(BF)
    spread = jnp.broadcast_to(rate_ref[...], (count, count))
    row = lax.broadcasted_iota(jnp.int32, (count, count), 0)
    col = lax.broadcasted_iota(jnp.int32, (count, count), 1)
    rate = jnp.sum(jnp.where(row == col, spread, 0.0), axis=1, keepdims=True)
    pair_ref[1] = (-(rate * value_ref[...].astype(F32))).astype(BF)
    query_out[...] = rms(query_ref[...].astype(F32)).astype(BF)


def prep(key_tokens, value_tokens, queries, token_rate):
    count = key_tokens.shape[0]
    return call(
        prep_kernel,
        [struct((2, count, D), BF), struct((count, D), BF)],
        key_tokens, value_tokens, queries, token_rate.reshape(1, count),
        name="prep",
    )


def gradient(pairs, blocks):
    count = pairs[0].shape[1]
    sizes = [b.shape[1] for b in blocks]
    starts = [sum(sizes[:i]) for i in range(len(sizes))]
    units = sum(sizes)
    group = 2 if len(pairs) % 2 == 0 else 1

    def kernel(*refs):
        pair_refs = refs[:len(pairs)]
        block_refs = refs[len(pairs):len(pairs) + len(blocks)]
        out_refs = refs[len(pairs) + len(blocks):-2]
        weights, total = refs[-2:]
        for ref, start, size in zip(block_refs, starts, sizes):
            for m in range(3):
                weights[m * units + start:m * units + start + size] = ref[m]
        for j in range(0, len(pairs), group):
            keys = jnp.concatenate([pair_refs[j + i][0] for i in range(group)], axis=0)
            signal = jnp.concatenate([pair_refs[j + i][1] for i in range(group)], axis=0)
            acts = nt(weights[:2 * units], keys)
            gate_act, up_act = acts[:units], acts[units:]
            sg = jax.nn.sigmoid(gate_act)
            silu = gate_act * sg
            hidden = (silu * up_act).astype(BF)
            hidden_grad = nt(weights[2 * units:], signal)
            gate_grad = (hidden_grad * up_act * sg * (1.0 + gate_act * (1.0 - sg))).astype(BF)
            up_grad = (hidden_grad * silu).astype(BF)
            first = nn(jnp.concatenate([gate_grad, up_grad], axis=0), keys)
            last = nn(hidden, signal)
            if j == 0:
                total[:2 * units] = first
                total[2 * units:] = last
            else:
                total[:2 * units] += first
                total[2 * units:] += last
        for out, start, size in zip(out_refs, starts, sizes):
            for m in range(3):
                out[m] = total[m * units + start:m * units + start + size].astype(out.dtype)

    outs = [struct((3, s, D), F32 if i == 0 else BF) for i, s in enumerate(sizes)]
    return call(
        kernel, outs, *pairs, *blocks,
        flops=12 * count * len(pairs) * units * D,
        scratch=[pltpu.VMEM((3 * units, D), BF), pltpu.VMEM((3 * units, D), F32)],
        name="gradient",
    )


def step(old, own, others):
    def kernel(old_ref, own_ref, *refs):
        for m in range(3):
            grad = own_ref[m]
            for ref in refs[:-1]:
                grad = grad + ref[m].astype(F32)
            old_rows = old_ref[m].astype(F32)
            stepped = old_rows - grad
            refs[-1][m] = (
                stepped
                * jnp.sqrt(jnp.mean(old_rows * old_rows, axis=-1, keepdims=True) + epsilon)
                / jnp.sqrt(jnp.mean(stepped * stepped, axis=-1, keepdims=True) + epsilon)
            ).astype(BF)

    return call(kernel, [struct(old.shape, BF)], old, own, *others, name="step")[0]


def attention_kernel(query_ref, key_ref, value_ref, out_ref):
    count = key_ref.shape[0]
    width = 2 * HEAD_DIM
    low = lax.broadcasted_iota(jnp.int32, (count, width), 1) < HEAD_DIM
    zero = jnp.zeros((count, width), BF)
    for h in range(HEADS // 2):
        cols = slice(h * width, (h + 1) * width)
        query, key, value = query_ref[:, cols], key_ref[:, cols], value_ref[:, cols]
        probs = []
        for keep in (low, ~low):
            scores = nt(query, jnp.where(keep, key, zero)) * HEAD_DIM ** (-0.5)
            weights = jnp.exp(scores - jnp.max(scores, axis=-1, keepdims=True))
            probs.append((weights / jnp.sum(weights, axis=-1, keepdims=True)).astype(BF))
        values = jnp.concatenate([jnp.where(low, value, zero), jnp.where(low, zero, value)], axis=0)
        out_ref[:, cols] = nn(jnp.concatenate(probs, axis=1), values)


def attention(queries, key_tokens, value_tokens):
    return call(
        attention_kernel, [struct(queries.shape, F32)], queries, key_tokens, value_tokens,
        flops=4 * queries.shape[0] * key_tokens.shape[0] * D, name="attention",
    )[0]


def apply_rows(queries, blocks):
    count = queries[0].shape[0]
    sizes = [b.shape[1] for b in blocks]
    starts = [sum(sizes[:i]) for i in range(len(sizes))]
    units = sum(sizes)

    def kernel(*refs):
        query_refs = refs[:len(queries)]
        block_refs = refs[len(queries):len(queries) + len(blocks)]
        out_refs = refs[len(queries) + len(blocks):-1]
        weights = refs[-1]
        for ref, start, size in zip(block_refs, starts, sizes):
            for m in range(3):
                weights[m * units + start:m * units + start + size] = ref[m]
        rows = jnp.concatenate([ref[...] for ref in query_refs], axis=0)
        gate_act = nt(rows, weights[:units])
        up_act = nt(rows, weights[units:2 * units])
        hidden = (jax.nn.silu(gate_act) * up_act).astype(BF)
        result = nn(hidden, weights[2 * units:])
        for i, out in enumerate(out_refs):
            out[...] = result[i * count:(i + 1) * count].astype(out.dtype)

    outs = [struct((count, D), BF) for _ in queries[:-1]] + [struct((count, D), F32)]
    return call(
        kernel, outs, *queries, *blocks,
        flops=6 * count * len(queries) * units * D,
        scratch=[pltpu.VMEM((3 * units, D), BF)],
        name="apply",
    )


def total_kernel(*refs):
    result = refs[0][...] + refs[1][...]
    for ref in refs[2:-1]:
        result = result + ref[...].astype(F32)
    refs[-1][...] = result.astype(BF)


def solution(mesh):
    n_far, along, layer, swap, offsets = moves(mesh)
    steps = sorted(range(1, n_far), key=lambda k: (k != 2, k))

    def joined(blocks):
        if blocks[0].shape[1] % 16 == 0:
            return blocks
        return [jnp.concatenate(blocks, axis=1)]

    def body(key_tokens, value_tokens, queries, token_rate, fast_weights):
        rows = fast_weights.shape[1]
        line = {}
        for i, k in enumerate(steps):
            source = fast_weights if i < 2 else after(fast_weights, line[steps[i - 1]])
            line[k] = send(source, along(-k))

        pair, query_normed = prep(key_tokens, value_tokens, queries, token_rate)
        here = [send(pair, layer(*o)) for o in offsets]
        own_there = send(pair, swap)
        there = [send(block, swap) for block in here]

        blocks = joined([fast_weights] + [line[k] for k in steps])
        grads = gradient([pair, own_there] + here + there, blocks)
        if len(blocks) > 1:
            own_grad, parts = grads[0], grads[1:]
        else:
            own_grad = grads[0][:, :rows]
            parts = [grads[0][:, i * rows:(i + 1) * rows].astype(BF) for i in range(1, n_far)]
        arrived = [send(part, along(k)) for part, k in zip(parts, steps)]

        queries_late, keys_late, values_late, query_normed = lax.optimization_barrier(
            (queries, key_tokens, value_tokens, query_normed, own_grad)
        )[:4]
        all_queries = [send(query_normed, layer(-o[0], -o[1])) for o in offsets] + [query_normed]
        mixed = attention(queries_late, keys_late, values_late)

        own_grad = after(own_grad, *all_queries)
        updated = step(fast_weights, own_grad, arrived)
        updated, mixed = lax.optimization_barrier((updated, mixed))
        stepped = [send(updated, along(-k)) for k in steps]
        stepped_there = [send(block, swap) for block in [updated] + stepped]

        outs = apply_rows(all_queries, joined([updated] + stepped + stepped_there))
        back = [send(part, layer(*o)) for part, o in zip(outs[:-1], offsets)]
        return call(total_kernel, [struct(queries.shape, BF)], outs[-1], mixed, *back, name="total")[0]

    in_specs = (
        P(("grp", "dev"), None),
        P(("grp", "dev"), None),
        P(("grp", "dev"), None),
        P(("grp", "dev")),
        P(None, ("grp", "dev"), None),
    )
    out_specs = P(("grp", "dev"), None)
    return jax.shard_map(body, mesh=mesh, in_specs=in_specs, out_specs=out_specs, check_vma=False)
```

```python
import jax
import jax.numpy as jnp
from jax import lax
from jax.experimental import pallas as pl
from jax.experimental.pallas import tpu as pltpu
from jax.sharding import PartitionSpec as P

D = 768
HEADS = 12
HEAD_DIM = 64
CORES = 2
NEAR = 2
BF = jnp.bfloat16
F32 = jnp.float32

WEIGHT_FLOPS = 20_000_000_000

epsilon = 1e-06
AXES = ("grp", "dev")


def moves(mesh):
    n_grp, n_dev = mesh.shape["grp"], mesh.shape["dev"]
    n_gx, n_far = n_grp // CORES, n_dev // NEAR

    def build(target):
        pairs = []
        for gx in range(n_gx):
            for core in range(CORES):
                for far in range(n_far):
                    for near in range(NEAR):
                        to = target(gx, core, far, near)
                        source = (gx * CORES + core) * n_dev + far * NEAR + near
                        dest = (to[0] * CORES + to[1]) * n_dev + to[2] * NEAR + to[3]
                        pairs.append((source, dest))
        return pairs

    def along(step):
        return build(lambda gx, core, far, near: (gx, core, (far + step) % n_far, near))

    def layer(dx, dn):
        return build(lambda gx, core, far, near: ((gx + dx) % n_gx, core, far, (near + dn) % NEAR))

    swap = build(lambda gx, core, far, near: (gx, 1 - core, far, near))
    offsets = [(dx, dn) for dx in reversed(range(n_gx)) for dn in reversed(range(NEAR))][:-1]
    return n_far, along, layer, swap, offsets


def send(array, pairs):
    return lax.ppermute(array, AXES, pairs)


def after(value, *others):
    return lax.optimization_barrier((value, *others))[0]


def call(kernel, outs, *args, flops=0, scratch=(), space=pltpu.VMEM, limit=32 * 1024 * 1024, name=None):
    vmem = pl.BlockSpec(memory_space=pltpu.VMEM)
    size = sum(a.size * a.dtype.itemsize for a in args) + sum(o.size * o.dtype.itemsize for o in outs)
    result = pl.pallas_call(
        kernel,
        out_shape=list(outs),
        in_specs=[pl.BlockSpec(memory_space=space)] * len(args),
        out_specs=[vmem] * len(outs),
        scratch_shapes=list(scratch),
        compiler_params=pltpu.CompilerParams(vmem_limit_bytes=limit),
        cost_estimate=pl.CostEstimate(flops=flops, bytes_accessed=size, transcendentals=0),
        name=name,
    )(*args)
    return result


def struct(shape, dtype):
    return jax.ShapeDtypeStruct(shape, dtype)


def nt(a, b):
    return lax.dot_general(a, b, (((1,), (1,)), ((), ())), preferred_element_type=F32)


def nn(a, b):
    return lax.dot_general(a, b, (((1,), (0,)), ((), ())), preferred_element_type=F32)


def rms(matrix):
    return matrix / jnp.sqrt(jnp.mean(matrix * matrix, axis=-1, keepdims=True) + epsilon)


def prep_kernel(key_hbm, value_hbm, query_hbm, rate_hbm, pair_ref, query_out, key_ref, value_ref, query_ref, rate_ref, sems):
    count = key_ref.shape[0]
    sources = (key_hbm, rate_hbm, value_hbm, query_hbm)
    targets = (key_ref, rate_ref, value_ref, query_ref)
    copies = [pltpu.make_async_copy(a, b, sems.at[i]) for i, (a, b) in enumerate(zip(sources, targets))]
    for copy in copies:
        copy.start()
    copies[0].wait()
    pair_ref[0] = rms(key_ref[...].astype(F32)).astype(BF)
    copies[1].wait()
    copies[2].wait()
    spread = jnp.broadcast_to(rate_ref[...], (count, count))
    row = lax.broadcasted_iota(jnp.int32, (count, count), 0)
    col = lax.broadcasted_iota(jnp.int32, (count, count), 1)
    rate = jnp.sum(jnp.where(row == col, spread, 0.0), axis=1, keepdims=True)
    pair_ref[1] = (-(rate * value_ref[...].astype(F32))).astype(BF)
    copies[3].wait()
    query_out[...] = rms(query_ref[...].astype(F32)).astype(BF)


def prep(key_tokens, value_tokens, queries, token_rate):
    count = key_tokens.shape[0]
    return call(
        prep_kernel,
        [struct((2, count, D), BF), struct((count, D), BF)],
        key_tokens, value_tokens, queries, token_rate.reshape(1, count),
        scratch=[pltpu.VMEM((count, D), BF)] * 3 + [pltpu.VMEM((1, count), F32), pltpu.SemaphoreType.DMA((4,))],
        space=pltpu.HBM,
        limit=62 * 1024 * 1024,
        name="prep",
    )


def assemble(blocks):
    sizes = [b.shape[1] for b in blocks]
    starts = [sum(sizes[:i]) for i in range(len(sizes))]
    units = sum(sizes)

    def kernel(*refs):
        for ref, start, size in zip(refs, starts, sizes):
            for m in range(3):
                refs[-1][m * units + start:m * units + start + size] = ref[m]

    return call(kernel, [struct((3 * units, D), BF)], *blocks, flops=WEIGHT_FLOPS, name="assemble")[0]


def gradient(pairs, weights, sizes):
    count = pairs[0].shape[1]
    starts = [sum(sizes[:i]) for i in range(len(sizes))]
    units = sum(sizes)
    group = 2 if len(pairs) % 2 == 0 else 1

    def kernel(*refs):
        pair_refs = refs[:len(pairs)]
        weights = refs[len(pairs)]
        out_refs = refs[len(pairs) + 1:-1]
        total = refs[-1]
        for j in range(0, len(pairs), group):
            keys = jnp.concatenate([pair_refs[j + i][0] for i in range(group)], axis=0)
            signal = jnp.concatenate([pair_refs[j + i][1] for i in range(group)], axis=0)
            acts = nt(weights[:2 * units], keys)
            gate_act, up_act = acts[:units], acts[units:]
            sg = jax.nn.sigmoid(gate_act)
            silu = gate_act * sg
            hidden = (silu * up_act).astype(BF)
            hidden_grad = nt(weights[2 * units:], signal)
            gate_grad = (hidden_grad * up_act * sg * (1.0 + gate_act * (1.0 - sg))).astype(BF)
            up_grad = (hidden_grad * silu).astype(BF)
            first = nn(jnp.concatenate([gate_grad, up_grad], axis=0), keys)
            last = nn(hidden, signal)
            if j == 0:
                total[:2 * units] = first
                total[2 * units:] = last
            else:
                total[:2 * units] += first
                total[2 * units:] += last
        for out, start, size in zip(out_refs, starts, sizes):
            for m in range(3):
                out[m] = total[m * units + start:m * units + start + size].astype(out.dtype)

    outs = [struct((3, s, D), F32 if i == 0 else BF) for i, s in enumerate(sizes)]
    return call(
        kernel, outs, *pairs, weights,
        flops=12 * count * len(pairs) * units * D,
        scratch=[pltpu.VMEM((3 * units, D), F32)],
        name="gradient",
    )


def step(old, own, others):
    def kernel(old_ref, own_ref, *refs):
        for m in range(3):
            grad = own_ref[m]
            for ref in refs[:-1]:
                grad = grad + ref[m].astype(F32)
            old_rows = old_ref[m].astype(F32)
            stepped = old_rows - grad
            refs[-1][m] = (
                stepped
                * jnp.sqrt(jnp.mean(old_rows * old_rows, axis=-1, keepdims=True) + epsilon)
                / jnp.sqrt(jnp.mean(stepped * stepped, axis=-1, keepdims=True) + epsilon)
            ).astype(BF)

    return call(kernel, [struct(old.shape, BF)], old, own, *others, name="step")[0]


def attention_kernel(query_ref, key_ref, value_ref, out_ref):
    count = key_ref.shape[0]
    width = 2 * HEAD_DIM
    low = lax.broadcasted_iota(jnp.int32, (count, width), 1) < HEAD_DIM
    zero = jnp.zeros((count, width), BF)
    for h in range(HEADS // 2):
        cols = slice(h * width, (h + 1) * width)
        query, key, value = query_ref[:, cols], key_ref[:, cols], value_ref[:, cols]
        probs = []
        for keep in (low, ~low):
            scores = nt(query, jnp.where(keep, key, zero)) * HEAD_DIM ** (-0.5)
            weights = jnp.exp(scores - jnp.max(scores, axis=-1, keepdims=True))
            probs.append((weights / jnp.sum(weights, axis=-1, keepdims=True)).astype(BF))
        values = jnp.concatenate([jnp.where(low, value, zero), jnp.where(low, zero, value)], axis=0)
        out_ref[:, cols] = nn(jnp.concatenate(probs, axis=1), values)


def attention(queries, key_tokens, value_tokens):
    return call(
        attention_kernel, [struct(queries.shape, F32)], queries, key_tokens, value_tokens,
        flops=4 * queries.shape[0] * key_tokens.shape[0] * D, name="attention",
    )[0]


def apply_rows(queries, blocks):
    count = queries[0].shape[0]
    sizes = [b.shape[1] for b in blocks]
    starts = [sum(sizes[:i]) for i in range(len(sizes))]
    units = sum(sizes)

    def kernel(*refs):
        query_refs = refs[:len(queries)]
        block_refs = refs[len(queries):len(queries) + len(blocks)]
        out_refs = refs[len(queries) + len(blocks):-1]
        weights = refs[-1]
        for ref, start, size in zip(block_refs, starts, sizes):
            for m in range(3):
                weights[m * units + start:m * units + start + size] = ref[m]
        rows = jnp.concatenate([ref[...] for ref in query_refs], axis=0)
        gate_act = nt(rows, weights[:units])
        up_act = nt(rows, weights[units:2 * units])
        hidden = (jax.nn.silu(gate_act) * up_act).astype(BF)
        result = nn(hidden, weights[2 * units:])
        for i, out in enumerate(out_refs):
            out[...] = result[i * count:(i + 1) * count].astype(out.dtype)

    outs = [struct((count, D), BF) for _ in queries[:-1]] + [struct((count, D), F32)]
    return call(
        kernel, outs, *queries, *blocks,
        flops=6 * count * len(queries) * units * D,
        scratch=[pltpu.VMEM((3 * units, D), BF)],
        name="apply",
    )


def total_kernel(*refs):
    result = refs[0][...] + refs[1][...]
    for ref in refs[2:-1]:
        result = result + ref[...].astype(F32)
    refs[-1][...] = result.astype(BF)


def solution(mesh):
    n_far, along, layer, swap, offsets = moves(mesh)
    steps = sorted(range(1, n_far), key=lambda k: (k != 2, k))

    def joined(blocks):
        if blocks[0].shape[1] % 16 == 0:
            return blocks
        return [jnp.concatenate(blocks, axis=1)]

    def body(key_tokens, value_tokens, queries, token_rate, fast_weights):
        rows = fast_weights.shape[1]
        line = {}
        for i, k in enumerate(steps):
            source = fast_weights if i < 2 else after(fast_weights, line[steps[i - 1]])
            line[k] = send(source, along(-k))

        pair, query_normed = prep(key_tokens, value_tokens, queries, token_rate)
        here = [send(pair, layer(*o)) for o in offsets]
        own_there = send(pair, swap)
        there = [send(block, swap) for block in here]

        blocks = joined([fast_weights] + [line[k] for k in steps])
        weights = assemble(blocks)
        grads = gradient([pair, own_there] + here + there, weights, [b.shape[1] for b in blocks])
        if len(blocks) > 1:
            own_grad, parts = grads[0], grads[1:]
        else:
            own_grad = grads[0][:, :rows]
            parts = [grads[0][:, i * rows:(i + 1) * rows].astype(BF) for i in range(1, n_far)]
        arrived = [send(part, along(k)) for part, k in zip(parts, steps)]

        queries_late, keys_late, values_late = lax.optimization_barrier(
            (queries, key_tokens, value_tokens, own_grad)
        )[:3]
        all_queries, last = [], weights
        for o in offsets:
            all_queries.append(send(after(query_normed, last), layer(-o[0], -o[1])))
            last = all_queries[0]
        own_grad = after(own_grad, *all_queries)
        all_queries.append(query_normed)
        mixed = attention(queries_late, keys_late, values_late)

        updated = step(fast_weights, own_grad, arrived)
        updated, mixed = lax.optimization_barrier((updated, mixed))
        stepped = [send(updated, along(-k)) for k in steps]
        stepped_there = [send(block, swap) for block in [updated] + stepped]

        outs = apply_rows(all_queries, joined([updated] + stepped + stepped_there))
        back = [send(part, layer(*o)) for part, o in zip(outs[:-1], offsets)]
        return call(total_kernel, [struct(queries.shape, BF)], outs[-1], mixed, *back, name="total")[0]

    in_specs = (
        P(("grp", "dev"), None),
        P(("grp", "dev"), None),
        P(("grp", "dev"), None),
        P(("grp", "dev")),
        P(None, ("grp", "dev"), None),
    )
    out_specs = P(("grp", "dev"), None)
    return jax.shard_map(body, mesh=mesh, in_specs=in_specs, out_specs=out_specs, check_vma=False)
```

```python
import jax
import jax.numpy as jnp
from jax import lax
from jax.experimental import pallas as pl
from jax.experimental.pallas import tpu as pltpu
from jax.sharding import PartitionSpec as P

D = 768
HEADS = 12
HEAD_DIM = 64
CORES = 2
FAR = 4
BF = jnp.bfloat16
F32 = jnp.float32

epsilon = 1e-06
AXES = ("grp", "dev")


def moves(mesh):
    n_grp, n_dev = mesh.shape["grp"], mesh.shape["dev"]
    n_gx, n_near = n_grp // CORES, n_dev // FAR

    def build(target):
        pairs = []
        for gx in range(n_gx):
            for core in range(CORES):
                for far in range(FAR):
                    for near in range(n_near):
                        to = target(gx, core, far, near)
                        if to is None:
                            continue
                        source = (gx * CORES + core) * n_dev + far * n_near + near
                        dest = (to[0] * CORES + to[1]) * n_dev + to[2] * n_near + to[3]
                        pairs.append((source, dest))
        return pairs

    def along(table):
        return build(lambda gx, core, far, near: (gx, core, table[far], near) if far in table else None)

    def layer(dx, dn):
        return build(lambda gx, core, far, near: ((gx + dx) % n_gx, core, far, (near + dn) % n_near))

    swap = build(lambda gx, core, far, near: (gx, 1 - core, far, near))
    offsets = [(dx, dn) for dx in reversed(range(n_gx)) for dn in reversed(range(n_near))][:-1]
    return along, layer, swap, offsets


def send(array, pairs):
    return lax.ppermute(array, AXES, pairs)


def after(value, *others):
    return lax.optimization_barrier((value, *others))[0]


def call(kernel, outs, *args, flops=0, scratch=(), space=pltpu.VMEM, limit=32 * 1024 * 1024, name=None):
    vmem = pl.BlockSpec(memory_space=pltpu.VMEM)
    size = sum(a.size * a.dtype.itemsize for a in args) + sum(o.size * o.dtype.itemsize for o in outs)
    result = pl.pallas_call(
        kernel,
        out_shape=list(outs),
        in_specs=[pl.BlockSpec(memory_space=space)] * len(args),
        out_specs=[vmem] * len(outs),
        scratch_shapes=list(scratch),
        compiler_params=pltpu.CompilerParams(vmem_limit_bytes=limit),
        cost_estimate=pl.CostEstimate(flops=flops, bytes_accessed=size, transcendentals=0),
        name=name,
    )(*args)
    return result


def struct(shape, dtype):
    return jax.ShapeDtypeStruct(shape, dtype)


def nt(a, b):
    return lax.dot_general(a, b, (((1,), (1,)), ((), ())), preferred_element_type=F32)


def nn(a, b):
    return lax.dot_general(a, b, (((1,), (0,)), ((), ())), preferred_element_type=F32)


def rms(matrix):
    return matrix / jnp.sqrt(jnp.mean(matrix * matrix, axis=-1, keepdims=True) + epsilon)


def prep_kernel(key_hbm, value_hbm, query_hbm, rate_hbm, pair_ref, query_out, key_ref, value_ref, query_ref, rate_ref, sems):
    count = key_ref.shape[0]
    sources = (key_hbm, rate_hbm, value_hbm, query_hbm)
    targets = (key_ref, rate_ref, value_ref, query_ref)
    copies = [pltpu.make_async_copy(a, b, sems.at[i]) for i, (a, b) in enumerate(zip(sources, targets))]
    for copy in copies:
        copy.start()
    copies[0].wait()
    pair_ref[0] = rms(key_ref[...].astype(F32)).astype(BF)
    copies[1].wait()
    copies[2].wait()
    spread = jnp.broadcast_to(rate_ref[...], (count, count))
    row = lax.broadcasted_iota(jnp.int32, (count, count), 0)
    col = lax.broadcasted_iota(jnp.int32, (count, count), 1)
    rate = jnp.sum(jnp.where(row == col, spread, 0.0), axis=1, keepdims=True)
    pair_ref[1] = (-(rate * value_ref[...].astype(F32))).astype(BF)
    copies[3].wait()
    query_out[...] = rms(query_ref[...].astype(F32)).astype(BF)


def prep(key_tokens, value_tokens, queries, token_rate):
    count = key_tokens.shape[0]
    return call(
        prep_kernel,
        [struct((2, count, D), BF), struct((count, D), BF)],
        key_tokens, value_tokens, queries, token_rate.reshape(1, count),
        scratch=[pltpu.VMEM((count, D), BF)] * 3 + [pltpu.VMEM((1, count), F32), pltpu.SemaphoreType.DMA((4,))],
        space=pltpu.HBM,
        limit=62 * 1024 * 1024,
        name="prep",
    )


def assemble(blocks):
    sizes = [b.shape[1] for b in blocks]
    starts = [sum(sizes[:i]) for i in range(len(sizes))]
    units = sum(sizes)

    def kernel(*refs):
        for ref, start, size in zip(refs, starts, sizes):
            for m in range(3):
                refs[-1][m * units + start:m * units + start + size] = ref[m]

    return call(kernel, [struct((3 * units, D), BF)], *blocks, name="assemble")[0]


def gradient(pairs, weights, sizes, before=None):
    count = pairs[0].shape[1]
    starts = [sum(sizes[:i]) for i in range(len(sizes))]
    units = sum(sizes)
    group = 2 if len(pairs) % 2 == 0 else 1
    given = 0 if before is None else 1

    def kernel(*refs):
        pair_refs = refs[:len(pairs)]
        weights = refs[len(pairs)]
        out_refs = refs[len(pairs) + 1 + given:]
        total = refs[-1]
        for j in range(0, len(pairs), group):
            keys = jnp.concatenate([pair_refs[j + i][0] for i in range(group)], axis=0)
            signal = jnp.concatenate([pair_refs[j + i][1] for i in range(group)], axis=0)
            acts = nt(weights[:2 * units], keys)
            gate_act, up_act = acts[:units], acts[units:]
            sg = jax.nn.sigmoid(gate_act)
            silu = gate_act * sg
            hidden = (silu * up_act).astype(BF)
            hidden_grad = nt(weights[2 * units:], signal)
            gate_grad = (hidden_grad * up_act * sg * (1.0 + gate_act * (1.0 - sg))).astype(BF)
            up_grad = (hidden_grad * silu).astype(BF)
            first = nn(jnp.concatenate([gate_grad, up_grad], axis=0), keys)
            last = nn(hidden, signal)
            if j == 0 and given:
                total[:2 * units] = refs[len(pairs) + 1][:2 * units] + first
                total[2 * units:] = refs[len(pairs) + 1][2 * units:] + last
            elif j == 0:
                total[:2 * units] = first
                total[2 * units:] = last
            else:
                total[:2 * units] += first
                total[2 * units:] += last
        if given:
            for out, start, size in zip(out_refs, starts, sizes):
                for m in range(3):
                    out[m] = total[m * units + start:m * units + start + size].astype(out.dtype)

    flops = 12 * count * len(pairs) * units * D
    if not given:
        return call(kernel, [struct((3 * units, D), F32)], *pairs, weights, flops=flops, name="gradient_part")[0]
    outs = [struct((3, s, D), F32 if i == 0 else BF) for i, s in enumerate(sizes)]
    return call(
        kernel, outs, *pairs, weights, before,
        flops=flops,
        scratch=[pltpu.VMEM((3 * units, D), F32)],
        name="gradient",
    )


def step(old, own, others):
    def kernel(old_ref, own_ref, *refs):
        for m in range(3):
            grad = own_ref[m]
            for ref in refs[:-1]:
                grad = grad + ref[m].astype(F32)
            old_rows = old_ref[m].astype(F32)
            stepped = old_rows - grad
            refs[-1][m] = (
                stepped
                * jnp.sqrt(jnp.mean(old_rows * old_rows, axis=-1, keepdims=True) + epsilon)
                / jnp.sqrt(jnp.mean(stepped * stepped, axis=-1, keepdims=True) + epsilon)
            ).astype(BF)

    return call(kernel, [struct(old.shape, BF)], old, own, *others, name="step")[0]


def attention_kernel(query_ref, key_ref, value_ref, out_ref):
    count = key_ref.shape[0]
    width = 2 * HEAD_DIM
    low = lax.broadcasted_iota(jnp.int32, (count, width), 1) < HEAD_DIM
    zero = jnp.zeros((count, width), BF)
    for h in range(HEADS // 2):
        cols = slice(h * width, (h + 1) * width)
        query, key, value = query_ref[:, cols], key_ref[:, cols], value_ref[:, cols]
        probs = []
        for keep in (low, ~low):
            scores = nt(query, jnp.where(keep, key, zero)) * HEAD_DIM ** (-0.5)
            weights = jnp.exp(scores - jnp.max(scores, axis=-1, keepdims=True))
            probs.append((weights / jnp.sum(weights, axis=-1, keepdims=True)).astype(BF))
        values = jnp.concatenate([jnp.where(low, value, zero), jnp.where(low, zero, value)], axis=0)
        out_ref[:, cols] = nn(jnp.concatenate(probs, axis=1), values)


def attention(queries, key_tokens, value_tokens):
    return call(
        attention_kernel, [struct(queries.shape, F32)], queries, key_tokens, value_tokens,
        flops=4 * queries.shape[0] * key_tokens.shape[0] * D, name="attention",
    )[0]


def apply_rows(queries, blocks):
    count = queries[0].shape[0]
    sizes = [b.shape[1] for b in blocks]
    starts = [sum(sizes[:i]) for i in range(len(sizes))]
    units = sum(sizes)

    def kernel(*refs):
        query_refs = refs[:len(queries)]
        block_refs = refs[len(queries):len(queries) + len(blocks)]
        out_refs = refs[len(queries) + len(blocks):-1]
        weights = refs[-1]
        for ref, start, size in zip(block_refs, starts, sizes):
            for m in range(3):
                weights[m * units + start:m * units + start + size] = ref[m]
        rows = jnp.concatenate([ref[...] for ref in query_refs], axis=0)
        gate_act = nt(rows, weights[:units])
        up_act = nt(rows, weights[units:2 * units])
        hidden = (jax.nn.silu(gate_act) * up_act).astype(BF)
        result = nn(hidden, weights[2 * units:])
        for i, out in enumerate(out_refs):
            out[...] = result[i * count:(i + 1) * count].astype(out.dtype)

    outs = [struct((count, D), BF) for _ in queries[:-1]] + [struct((count, D), F32)]
    return call(
        kernel, outs, *queries, *blocks,
        flops=6 * count * len(queries) * units * D,
        scratch=[pltpu.VMEM((3 * units, D), BF)],
        name="apply",
    )


def total_kernel(*refs):
    result = refs[0][...] + refs[1][...]
    for ref in refs[2:-1]:
        result = result + ref[...].astype(F32)
    refs[-1][...] = result.astype(BF)


def solution(mesh):
    along, layer, swap, offsets = moves(mesh)

    def line_gather(block, *beside):
        two = send(block, along({0: 2, 1: 3, 2: 0, 3: 1}))
        near = send(block, along({0: 1, 1: 0, 2: 3, 3: 2}))
        block, two, near, *beside = lax.optimization_barrier((block, two, near, *beside))
        middle = send(block, along({1: 2, 2: 1}))
        relayed = send(two, along({2: 3, 1: 0}))
        return (near, two, middle, relayed), beside

    def joined(blocks):
        if blocks[0].shape[1] % 16 == 0:
            return blocks
        return [jnp.concatenate(blocks, axis=1)]

    def body(key_tokens, value_tokens, queries, token_rate, fast_weights):
        rows = fast_weights.shape[1]
        pair, query_normed = prep(key_tokens, value_tokens, queries, token_rate)
        mixed = attention(queries, key_tokens, value_tokens)
        first_weights = after(fast_weights, pair)
        blocks = [fast_weights] + [send(first_weights, layer(-o[0], -o[1])) for o in offsets]
        (near, two, middle, relayed), beside = line_gather(pair, query_normed, mixed, *blocks)
        query_normed, mixed, *blocks = beside
        blocks = joined(blocks)
        weights = assemble(blocks)
        sizes = [b.shape[1] for b in blocks]

        part = gradient([pair, send(pair, swap), near, send(near, swap), two, send(two, swap)], weights, sizes)
        part, middle, relayed = lax.optimization_barrier((part, middle, relayed))
        rest = middle + relayed
        grads = gradient([rest, send(rest, swap)], weights, sizes, part)
        if len(blocks) > 1:
            own_grad, parts = grads[0], grads[1:]
        else:
            own_grad = grads[0][:, :rows]
            parts = [grads[0][:, i * rows:(i + 1) * rows].astype(BF) for i in range(1, len(offsets) + 1)]
        arrived = [send(part, layer(*o)) for part, o in zip(parts, offsets)]

        updated = step(fast_weights, own_grad, arrived)
        query_normed = after(query_normed, updated)
        all_queries = [send(query_normed, layer(-o[0], -o[1])) for o in offsets[:-1]]
        (near, two, middle, relayed), beside = line_gather(updated, query_normed, send(updated, swap), *all_queries)
        query_normed, own_there, *all_queries = beside
        last_query = send(query_normed, layer(-offsets[-1][0], -offsets[-1][1]))
        middle, relayed, last_query = lax.optimization_barrier((middle, relayed, last_query))
        all_queries += [last_query, query_normed]
        stepped = [updated, near, two, middle + relayed]
        stepped_there = [own_there] + [send(block, swap) for block in stepped[1:]]

        outs = apply_rows(all_queries, joined(stepped + stepped_there))
        back = [send(part, layer(*o)) for part, o in zip(outs[:-1], offsets)]
        return call(total_kernel, [struct(queries.shape, BF)], outs[-1], mixed, *back, name="total")[0]

    in_specs = (
        P(("grp", "dev"), None),
        P(("grp", "dev"), None),
        P(("grp", "dev"), None),
        P(("grp", "dev")),
        P(None, ("grp", "dev"), None),
    )
    out_specs = P(("grp", "dev"), None)
    return jax.shard_map(body, mesh=mesh, in_specs=in_specs, out_specs=out_specs, check_vma=False)
```

```python
import jax
import jax.numpy as jnp
from jax import lax
from jax.experimental import pallas as pl
from jax.experimental.pallas import tpu as pltpu
from jax.sharding import PartitionSpec as P

D = 768
HEADS = 12
HEAD_DIM = 64
CORES = 2
NEAR = 2
BF = jnp.bfloat16
F32 = jnp.float32

WEIGHT_FLOPS = 20_000_000_000

epsilon = 1e-06
AXES = ("grp", "dev")


def moves(mesh):
    n_grp, n_dev = mesh.shape["grp"], mesh.shape["dev"]
    n_gx, n_far = n_grp // CORES, n_dev // NEAR

    def build(target):
        pairs = []
        for gx in range(n_gx):
            for core in range(CORES):
                for far in range(n_far):
                    for near in range(NEAR):
                        to = target(gx, core, far, near)
                        source = (gx * CORES + core) * n_dev + far * NEAR + near
                        dest = (to[0] * CORES + to[1]) * n_dev + to[2] * NEAR + to[3]
                        pairs.append((source, dest))
        return pairs

    def along(step):
        return build(lambda gx, core, far, near: (gx, core, far ^ step, near))

    def layer(dx, dn):
        return build(lambda gx, core, far, near: ((gx + dx) % n_gx, core, far, (near + dn) % NEAR))

    swap = build(lambda gx, core, far, near: (gx, 1 - core, far, near))
    offsets = [(dx, dn) for dx in reversed(range(n_gx)) for dn in reversed(range(NEAR))][:-1]
    return n_far, along, layer, swap, offsets


def send(array, pairs):
    return lax.ppermute(array, AXES, pairs)


def after(value, *others):
    return lax.optimization_barrier((value, *others))[0]


def call(kernel, outs, *args, flops=0, scratch=(), space=pltpu.VMEM, limit=32 * 1024 * 1024, name=None):
    vmem = pl.BlockSpec(memory_space=pltpu.VMEM)
    size = sum(a.size * a.dtype.itemsize for a in args) + sum(o.size * o.dtype.itemsize for o in outs)
    result = pl.pallas_call(
        kernel,
        out_shape=list(outs),
        in_specs=[pl.BlockSpec(memory_space=space)] * len(args),
        out_specs=[vmem] * len(outs),
        scratch_shapes=list(scratch),
        compiler_params=pltpu.CompilerParams(vmem_limit_bytes=limit),
        cost_estimate=pl.CostEstimate(flops=flops, bytes_accessed=size, transcendentals=0),
        name=name,
    )(*args)
    return result


def struct(shape, dtype):
    return jax.ShapeDtypeStruct(shape, dtype)


def nt(a, b):
    return lax.dot_general(a, b, (((1,), (1,)), ((), ())), preferred_element_type=F32)


def nn(a, b):
    return lax.dot_general(a, b, (((1,), (0,)), ((), ())), preferred_element_type=F32)


def rms(matrix):
    return matrix / jnp.sqrt(jnp.mean(matrix * matrix, axis=-1, keepdims=True) + epsilon)


def prep_kernel(key_hbm, value_hbm, query_hbm, rate_hbm, pair_ref, query_out, key_ref, value_ref, query_ref, rate_ref, sems):
    count = key_ref.shape[0]
    sources = (key_hbm, rate_hbm, value_hbm, query_hbm)
    targets = (key_ref, rate_ref, value_ref, query_ref)
    copies = [pltpu.make_async_copy(a, b, sems.at[i]) for i, (a, b) in enumerate(zip(sources, targets))]
    for copy in copies:
        copy.start()
    copies[0].wait()
    pair_ref[0] = rms(key_ref[...].astype(F32)).astype(BF)
    copies[1].wait()
    copies[2].wait()
    spread = jnp.broadcast_to(rate_ref[...], (count, count))
    row = lax.broadcasted_iota(jnp.int32, (count, count), 0)
    col = lax.broadcasted_iota(jnp.int32, (count, count), 1)
    rate = jnp.sum(jnp.where(row == col, spread, 0.0), axis=1, keepdims=True)
    pair_ref[1] = (-(rate * value_ref[...].astype(F32))).astype(BF)
    copies[3].wait()
    query_out[...] = rms(query_ref[...].astype(F32)).astype(BF)


def prep(key_tokens, value_tokens, queries, token_rate):
    count = key_tokens.shape[0]
    return call(
        prep_kernel,
        [struct((2, count, D), BF), struct((count, D), BF)],
        key_tokens, value_tokens, queries, token_rate.reshape(1, count),
        scratch=[pltpu.VMEM((count, D), BF)] * 3 + [pltpu.VMEM((1, count), F32), pltpu.SemaphoreType.DMA((4,))],
        space=pltpu.HBM,
        limit=62 * 1024 * 1024,
        name="prep",
    )


def assemble(blocks):
    sizes = [b.shape[1] for b in blocks]
    starts = [sum(sizes[:i]) for i in range(len(sizes))]
    units = sum(sizes)

    def kernel(*refs):
        for ref, start, size in zip(refs, starts, sizes):
            for m in range(3):
                refs[-1][m * units + start:m * units + start + size] = ref[m]

    return call(kernel, [struct((3 * units, D), BF)], *blocks, flops=WEIGHT_FLOPS, name="assemble")[0]


def gradient(pairs, weights, sizes, kinds):
    count = pairs[0].shape[1]
    starts = [sum(sizes[:i]) for i in range(len(sizes))]
    units = sum(sizes)
    group = 2 if len(pairs) % 2 == 0 else 1

    def kernel(*refs):
        pair_refs = refs[:len(pairs)]
        weights = refs[len(pairs)]
        out_refs = refs[len(pairs) + 1:-1]
        total = refs[-1]
        for j in range(0, len(pairs), group):
            keys = jnp.concatenate([pair_refs[j + i][0] for i in range(group)], axis=0)
            signal = jnp.concatenate([pair_refs[j + i][1] for i in range(group)], axis=0)
            acts = nt(weights[:2 * units], keys)
            gate_act, up_act = acts[:units], acts[units:]
            sg = jax.nn.sigmoid(gate_act)
            silu = gate_act * sg
            hidden = (silu * up_act).astype(BF)
            hidden_grad = nt(weights[2 * units:], signal)
            gate_grad = (hidden_grad * up_act * sg * (1.0 + gate_act * (1.0 - sg))).astype(BF)
            up_grad = (hidden_grad * silu).astype(BF)
            first = nn(jnp.concatenate([gate_grad, up_grad], axis=0), keys)
            last = nn(hidden, signal)
            if j == 0:
                total[:2 * units] = first
                total[2 * units:] = last
            else:
                total[:2 * units] += first
                total[2 * units:] += last
        for out, start, size in zip(out_refs, starts, sizes):
            for m in range(3):
                out[m] = total[m * units + start:m * units + start + size].astype(out.dtype)

    outs = [struct((3, s, D), kind) for s, kind in zip(sizes, kinds)]
    return call(
        kernel, outs, *pairs, weights,
        flops=12 * count * len(pairs) * units * D,
        scratch=[pltpu.VMEM((3 * units, D), F32)],
        name="gradient",
    )


def add_up(blocks):
    def kernel(*refs):
        if len(refs) == 2:
            refs[1][...] = refs[0][...]
            return
        total = refs[0][...].astype(F32)
        for ref in refs[1:-1]:
            total = total + ref[...].astype(F32)
        refs[-1][...] = total

    return call(kernel, [struct(blocks[0].shape, F32 if len(blocks) > 1 else BF)], *blocks, flops=WEIGHT_FLOPS, name="add_up")[0]


def step(old, own, others):
    def kernel(old_ref, own_ref, *refs):
        for m in range(3):
            grad = own_ref[m]
            for ref in refs[:-1]:
                grad = grad + ref[m].astype(F32)
            old_rows = old_ref[m].astype(F32)
            stepped = old_rows - grad
            refs[-1][m] = (
                stepped
                * jnp.sqrt(jnp.mean(old_rows * old_rows, axis=-1, keepdims=True) + epsilon)
                / jnp.sqrt(jnp.mean(stepped * stepped, axis=-1, keepdims=True) + epsilon)
            ).astype(BF)

    return call(kernel, [struct(old.shape, BF)], old, own, *others, name="step")[0]


def attention_kernel(query_ref, key_ref, value_ref, out_ref):
    count = key_ref.shape[0]
    width = 2 * HEAD_DIM
    low = lax.broadcasted_iota(jnp.int32, (count, width), 1) < HEAD_DIM
    zero = jnp.zeros((count, width), BF)
    for h in range(HEADS // 2):
        cols = slice(h * width, (h + 1) * width)
        query, key, value = query_ref[:, cols], key_ref[:, cols], value_ref[:, cols]
        probs = []
        for keep in (low, ~low):
            scores = nt(query, jnp.where(keep, key, zero)) * HEAD_DIM ** (-0.5)
            weights = jnp.exp(scores - jnp.max(scores, axis=-1, keepdims=True))
            probs.append((weights / jnp.sum(weights, axis=-1, keepdims=True)).astype(BF))
        values = jnp.concatenate([jnp.where(low, value, zero), jnp.where(low, zero, value)], axis=0)
        out_ref[:, cols] = nn(jnp.concatenate(probs, axis=1), values)


def attention(queries, key_tokens, value_tokens):
    return call(
        attention_kernel, [struct(queries.shape, F32)], queries, key_tokens, value_tokens,
        flops=4 * queries.shape[0] * key_tokens.shape[0] * D, name="attention",
    )[0]


def apply_rows(queries, blocks, before=None):
    count = queries[0].shape[0]
    sizes = [b.shape[1] for b in blocks]
    starts = [sum(sizes[:i]) for i in range(len(sizes))]
    units = sum(sizes)
    given = 0 if before is None else 1

    def kernel(*refs):
        query_refs = refs[:len(queries)]
        block_refs = refs[len(queries):len(queries) + len(blocks)]
        out_refs = refs[len(queries) + len(blocks) + given:-1]
        weights = refs[-1]
        for ref, start, size in zip(block_refs, starts, sizes):
            for m in range(3):
                weights[m * units + start:m * units + start + size] = ref[m]
        rows = jnp.concatenate([ref[...] for ref in query_refs], axis=0)
        gate_act = nt(rows, weights[:units])
        up_act = nt(rows, weights[units:2 * units])
        hidden = (jax.nn.silu(gate_act) * up_act).astype(BF)
        result = nn(hidden, weights[2 * units:])
        if given:
            result = result + refs[len(queries) + len(blocks)][...]
            for i, out in enumerate(out_refs):
                out[...] = result[i * count:(i + 1) * count].astype(out.dtype)
        else:
            out_refs[0][...] = result

    if given:
        outs = [struct((count, D), BF) for _ in queries[:-1]] + [struct((count, D), F32)]
    else:
        outs = [struct((len(queries) * count, D), F32)]
    result = call(
        kernel, outs, *queries, *blocks, *([before] if given else []),
        flops=6 * count * len(queries) * units * D,
        scratch=[pltpu.VMEM((3 * units, D), BF)],
        name="apply" if given else "apply_part",
    )
    return result if given else result[0]


def total_kernel(*refs):
    result = refs[0][...] + refs[1][...]
    for ref in refs[2:-1]:
        result = result + ref[...].astype(F32)
    refs[-1][...] = result.astype(BF)


def solution(mesh):
    n_far, along, layer, swap, offsets = moves(mesh)
    steps = [*range(2, n_far), 1]
    far_steps, near_steps = steps[:n_far // 2], steps[n_far // 2:]

    def joined(blocks):
        if blocks[0].shape[1] % 16 == 0:
            return blocks
        return [jnp.concatenate(blocks, axis=1)]

    def split(grad, number):
        rows = grad.shape[1] // number
        return [grad[:, i * rows:(i + 1) * rows] for i in range(number)]

    def body(key_tokens, value_tokens, queries, token_rate, fast_weights):
        line = {}
        for i, k in enumerate(steps):
            source = after(fast_weights, line[steps[0]]) if i == n_far - 2 else fast_weights
            line[k] = send(source, along(k))

        pair, query_normed = prep(key_tokens, value_tokens, queries, token_rate)
        here = [send(pair, layer(*o)) for o in offsets]
        own_there = send(after(pair, line[steps[1]]), swap)
        there = [send(block, swap) for block in here]
        tokens = [pair, own_there] + here + there

        line[steps[0]] = add_up([line[steps[0]]])
        blocks = joined([line[k] for k in far_steps])
        parts = gradient(tokens, assemble(blocks), [b.shape[1] for b in blocks], [BF] * len(blocks))
        far_sent = parts[0]
        if len(blocks) == 1:
            parts = split(parts[0], len(far_steps))
        far_sum = add_up([send(part, along(k)) for part, k in zip(parts, far_steps)])

        blocks = joined([fast_weights] + [after(line[k], far_sent) for k in near_steps])
        kinds = [F32] + [BF] * (len(blocks) - 1)
        own_grad, *parts = gradient(tokens, assemble(blocks), [b.shape[1] for b in blocks], kinds)
        if len(blocks) == 1:
            own_grad, *parts = split(own_grad, len(near_steps) + 1)
            parts = [part.astype(BF) for part in parts]
        arrived = [far_sum] + [send(part, along(k)) for part, k in zip(parts, near_steps)]

        queries_late, keys_late, values_late, query_normed = lax.optimization_barrier(
            (queries, key_tokens, value_tokens, query_normed, far_sent)
        )[:4]
        all_queries, last = [], far_sent
        for o in offsets:
            all_queries.append(send(after(query_normed, last), layer(-o[0], -o[1])))
            last = all_queries[0]
        own_grad = after(own_grad, *all_queries)
        all_queries.append(query_normed)
        mixed = attention(queries_late, keys_late, values_late)

        updated = step(fast_weights, own_grad, arrived)
        updated, mixed = lax.optimization_barrier((updated, mixed))
        stepped = {k: send(updated, along(k)) for k in steps}
        stepped[0] = updated
        stepped_there = {k: send(stepped[k], swap) for k in [0, *steps]}

        late = steps[(n_far - 2) // 2]
        early = [k for k in [0, *steps] if k != late]
        part = apply_rows(all_queries, joined([stepped[k] for k in early] + [stepped_there[k] for k in early]))
        outs = apply_rows(all_queries, joined([stepped[late], stepped_there[late]]), part)
        back = [send(part, layer(*o)) for part, o in zip(outs[:-1], offsets)]
        return call(total_kernel, [struct(queries.shape, BF)], outs[-1], mixed, *back, name="total")[0]

    in_specs = (
        P(("grp", "dev"), None),
        P(("grp", "dev"), None),
        P(("grp", "dev"), None),
        P(("grp", "dev")),
        P(None, ("grp", "dev"), None),
    )
    out_specs = P(("grp", "dev"), None)
    return jax.shard_map(body, mesh=mesh, in_specs=in_specs, out_specs=out_specs, check_vma=False)
```

```python
import jax
import jax.numpy as jnp
from jax import lax
from jax.experimental import pallas as pl
from jax.experimental.pallas import tpu as pltpu
from jax.sharding import PartitionSpec as P

D = 768
HEADS = 12
HEAD_DIM = 64
CORES = 2
NEAR = 2
BF = jnp.bfloat16
F32 = jnp.float32

epsilon = 1e-06
AXES = ("grp", "dev")


def moves(mesh):
    n_grp, n_dev = mesh.shape["grp"], mesh.shape["dev"]
    n_gx, n_far = n_grp // CORES, n_dev // NEAR

    def build(target):
        pairs = []
        for gx in range(n_gx):
            for core in range(CORES):
                for far in range(n_far):
                    for near in range(NEAR):
                        to = target(gx, core, far, near)
                        source = (gx * CORES + core) * n_dev + far * NEAR + near
                        dest = (to[0] * CORES + to[1]) * n_dev + to[2] * NEAR + to[3]
                        pairs.append((source, dest))
        return pairs

    def along(step):
        return build(lambda gx, core, far, near: (gx, core, far ^ step, near))

    def layer(dx, dn):
        return build(lambda gx, core, far, near: ((gx + dx) % n_gx, core, far, (near + dn) % NEAR))

    swap = build(lambda gx, core, far, near: (gx, 1 - core, far, near))
    offsets = [(dx, dn) for dx in reversed(range(n_gx)) for dn in reversed(range(NEAR))][:-1]
    return n_far, along, layer, swap, offsets


def send(array, pairs):
    return lax.ppermute(array, AXES, pairs)


def after(value, *others):
    return lax.optimization_barrier((value, *others))[0]


def call(kernel, outs, *args, flops=0, scratch=(), space=pltpu.VMEM, limit=32 * 1024 * 1024, name=None):
    vmem = pl.BlockSpec(memory_space=pltpu.VMEM)
    size = sum(a.size * a.dtype.itemsize for a in args) + sum(o.size * o.dtype.itemsize for o in outs)
    result = pl.pallas_call(
        kernel,
        out_shape=list(outs),
        in_specs=[pl.BlockSpec(memory_space=space)] * len(args),
        out_specs=[vmem] * len(outs),
        scratch_shapes=list(scratch),
        compiler_params=pltpu.CompilerParams(vmem_limit_bytes=limit),
        cost_estimate=pl.CostEstimate(flops=flops, bytes_accessed=size, transcendentals=0),
        name=name,
    )(*args)
    return result


def struct(shape, dtype):
    return jax.ShapeDtypeStruct(shape, dtype)


def nt(a, b):
    return lax.dot_general(a, b, (((1,), (1,)), ((), ())), preferred_element_type=F32)


def nn(a, b):
    return lax.dot_general(a, b, (((1,), (0,)), ((), ())), preferred_element_type=F32)


def rms(matrix):
    return matrix / jnp.sqrt(jnp.mean(matrix * matrix, axis=-1, keepdims=True) + epsilon)


def prep_kernel(key_hbm, value_hbm, query_hbm, rate_hbm, pair_ref, query_out, key_ref, value_ref, query_ref, rate_ref, sems):
    count = key_ref.shape[0]
    sources = (key_hbm, rate_hbm, value_hbm, query_hbm)
    targets = (key_ref, rate_ref, value_ref, query_ref)
    copies = [pltpu.make_async_copy(a, b, sems.at[i]) for i, (a, b) in enumerate(zip(sources, targets))]
    for copy in copies:
        copy.start()
    copies[0].wait()
    pair_ref[0] = rms(key_ref[...].astype(F32)).astype(BF)
    copies[1].wait()
    copies[2].wait()
    spread = jnp.broadcast_to(rate_ref[...], (count, count))
    row = lax.broadcasted_iota(jnp.int32, (count, count), 0)
    col = lax.broadcasted_iota(jnp.int32, (count, count), 1)
    rate = jnp.sum(jnp.where(row == col, spread, 0.0), axis=1, keepdims=True)
    pair_ref[1] = (-(rate * value_ref[...].astype(F32))).astype(BF)
    copies[3].wait()
    query_out[...] = rms(query_ref[...].astype(F32)).astype(BF)


def prep(key_tokens, value_tokens, queries, token_rate):
    count = key_tokens.shape[0]
    return call(
        prep_kernel,
        [struct((2, count, D), BF), struct((count, D), BF)],
        key_tokens, value_tokens, queries, token_rate.reshape(1, count),
        scratch=[pltpu.VMEM((count, D), BF)] * 3 + [pltpu.VMEM((1, count), F32), pltpu.SemaphoreType.DMA((4,))],
        space=pltpu.HBM,
        limit=62 * 1024 * 1024,
        name="prep",
    )


def cut(rows):
    return 16 * ((3 * rows + 31) // 32)


def pieces(rows):
    edge = cut(rows)
    found = []
    for m in range(3):
        for low, high, chunk in ((0, edge, 0), (edge, 3 * rows, 1)):
            first, last = max(low, m * rows), min(high, (m + 1) * rows)
            if first < last:
                found.append((m, first - m * rows, last - first, chunk, first - low))
    return found


def gradient(pairs, blocks):
    count = pairs[0].shape[1]
    number, rows = len(blocks), blocks[0].shape[1]
    aligned = rows % 16 == 0
    if not aligned:
        blocks = [jnp.concatenate(blocks, axis=1)]
    sizes = [b.shape[1] for b in blocks]
    units = number * rows
    group = 2 if len(pairs) % 2 == 0 else 1

    def kernel(*refs):
        pair_refs = refs[:len(pairs)]
        block_refs = refs[len(pairs):len(pairs) + len(blocks)]
        out_refs = refs[len(pairs) + len(blocks):-2]
        weights, total = refs[-2:]
        for i, ref in enumerate(block_refs):
            for m in range(3):
                weights[m * units + i * sizes[0]:m * units + (i + 1) * sizes[0]] = ref[m]
        for j in range(0, len(pairs), group):
            keys = jnp.concatenate([pair_refs[j + i][0] for i in range(group)], axis=0)
            signal = jnp.concatenate([pair_refs[j + i][1] for i in range(group)], axis=0)
            acts = nt(weights[:2 * units], keys)
            gate_act, up_act = acts[:units], acts[units:]
            sg = jax.nn.sigmoid(gate_act)
            silu = gate_act * sg
            hidden = (silu * up_act).astype(BF)
            hidden_grad = nt(weights[2 * units:], signal)
            gate_grad = (hidden_grad * up_act * sg * (1.0 + gate_act * (1.0 - sg))).astype(BF)
            up_grad = (hidden_grad * silu).astype(BF)
            first = nn(jnp.concatenate([gate_grad, up_grad], axis=0), keys)
            last = nn(hidden, signal)
            if j == 0:
                total[:2 * units] = first
                total[2 * units:] = last
            else:
                total[:2 * units] += first
                total[2 * units:] += last
        if not aligned:
            out_refs[0][...] = total[...]
            return
        for m, row, size, chunk, place in pieces(rows):
            for k in range(number):
                source = total[m * units + k * rows + row:m * units + k * rows + row + size]
                out = out_refs[2 * chunk + (k + 1) % 2]
                out[k // 2, place:place + size] = source.astype(out.dtype)

    edges = (cut(rows), 3 * rows - cut(rows))
    if aligned:
        outs = [struct((number // 2, edge, D), kind) for edge in edges for kind in (BF, F32)]
    else:
        outs = [struct((3 * units, D), F32)]
    outs = call(
        kernel, outs, *pairs, *blocks,
        flops=12 * count * len(pairs) * units * D,
        scratch=[pltpu.VMEM((3 * units, D), BF), pltpu.VMEM((3 * units, D), F32)],
        name="gradient",
    )
    if aligned:
        return outs[:2], outs[2:]
    total = outs[0].reshape(3, number, rows, D).swapaxes(0, 1).reshape(number, 3 * rows, D)
    parts = total[:, :edges[0]], total[:, edges[0]:]
    return [(part[1::2].astype(BF), part[::2]) for part in parts]


def fold(keep, arrived):
    number, rows = keep.shape[:2]

    def kernel(keep_ref, arrived_ref, send_ref, kept_ref):
        for k in range(number):
            total = keep_ref[k] + arrived_ref[k].astype(F32)
            out = send_ref if k % 2 else kept_ref
            out[k // 2] = total.astype(out.dtype)

    shape = (number // 2, rows, D)
    return call(kernel, [struct(shape, BF), struct(shape, F32)], keep, arrived, name="fold")


def step(old, keep, arrived):
    def kernel(old_ref, keep_ref, arrived_ref, out_ref):
        old_rows = old_ref[...].astype(F32)
        stepped = old_rows - (keep_ref[0] + arrived_ref[0].astype(F32))
        out_ref[...] = (
            stepped
            * jnp.sqrt(jnp.mean(old_rows * old_rows, axis=-1, keepdims=True) + epsilon)
            / jnp.sqrt(jnp.mean(stepped * stepped, axis=-1, keepdims=True) + epsilon)
        ).astype(BF)

    return call(kernel, [struct(old.shape, BF)], old, keep, arrived, name="step")[0]


def attention_kernel(query_ref, key_ref, value_ref, out_ref):
    count = key_ref.shape[0]
    width = 2 * HEAD_DIM
    low = lax.broadcasted_iota(jnp.int32, (count, width), 1) < HEAD_DIM
    zero = jnp.zeros((count, width), BF)
    for h in range(HEADS // 2):
        cols = slice(h * width, (h + 1) * width)
        query, key, value = query_ref[:, cols], key_ref[:, cols], value_ref[:, cols]
        probs = []
        for keep in (low, ~low):
            scores = nt(query, jnp.where(keep, key, zero)) * HEAD_DIM ** (-0.5)
            weights = jnp.exp(scores - jnp.max(scores, axis=-1, keepdims=True))
            probs.append((weights / jnp.sum(weights, axis=-1, keepdims=True)).astype(BF))
        values = jnp.concatenate([jnp.where(low, value, zero), jnp.where(low, zero, value)], axis=0)
        out_ref[:, cols] = nn(jnp.concatenate(probs, axis=1), values)


def attention(queries, key_tokens, value_tokens):
    return call(
        attention_kernel, [struct(queries.shape, F32)], queries, key_tokens, value_tokens,
        flops=4 * queries.shape[0] * key_tokens.shape[0] * D, name="attention",
    )[0]


def apply_rows(queries, blocks, rows):
    count = queries[0].shape[0]
    number = len(blocks)
    aligned = rows % 16 == 0
    if not aligned:
        whole = [jnp.concatenate(chunks, axis=0).reshape(3, rows, D) for chunks in blocks]
        blocks = [[jnp.concatenate(whole, axis=1).reshape(3 * number * rows, D)]]
    chunks = [chunk for block in blocks for chunk in block]
    units = number * rows

    def kernel(*refs):
        query_refs = refs[:len(queries)]
        chunk_refs = refs[len(queries):len(queries) + len(chunks)]
        out_refs = refs[len(queries) + len(chunks):-1]
        weights = refs[-1]
        if aligned:
            for i in range(number):
                for m, row, size, chunk, place in pieces(rows):
                    start = m * units + i * rows + row
                    weights[start:start + size] = chunk_refs[2 * i + chunk][place:place + size]
        else:
            weights[...] = chunk_refs[0][...]
        stacked = jnp.concatenate([ref[...] for ref in query_refs], axis=0)
        gate_act = nt(stacked, weights[:units])
        up_act = nt(stacked, weights[units:2 * units])
        hidden = (jax.nn.silu(gate_act) * up_act).astype(BF)
        result = nn(hidden, weights[2 * units:])
        for i, out in enumerate(out_refs):
            out[...] = result[i * count:(i + 1) * count].astype(out.dtype)

    outs = [struct((count, D), BF) for _ in queries[:-1]] + [struct((count, D), F32)]
    return call(
        kernel, outs, *queries, *chunks,
        flops=6 * count * len(queries) * units * D,
        scratch=[pltpu.VMEM((3 * units, D), BF)],
        name="apply",
    )


def total_kernel(*refs):
    result = refs[0][...] + refs[1][...]
    for ref in refs[2:-1]:
        result = result + ref[...].astype(F32)
    refs[-1][...] = result.astype(BF)


def solution(mesh):
    n_far, along, layer, swap, offsets = moves(mesh)
    bits = [1 << i for i in range(n_far.bit_length() - 1)]

    def line_gather(block):
        blocks = {0: block}
        for bit in reversed(bits):
            for k in list(blocks):
                blocks[k ^ bit] = send(blocks[k], along(bit))
        return [blocks[k] for k in range(n_far)]

    def body(key_tokens, value_tokens, queries, token_rate, fast_weights):
        rows = fast_weights.shape[1]
        blocks = line_gather(fast_weights)

        pair, query_normed = prep(key_tokens, value_tokens, queries, token_rate)
        here = [send(pair, layer(*o)) for o in offsets]
        own_there = send(pair, swap)
        there = [send(block, swap) for block in here]

        chunks = gradient([pair, own_there] + here + there, blocks)
        queries_late, keys_late, values_late, query_normed = lax.optimization_barrier(
            (queries, key_tokens, value_tokens, query_normed, chunks[0][0])
        )[:4]
        all_queries, last = [], query_normed
        for o in offsets:
            all_queries.append(send(after(query_normed, last), layer(-o[0], -o[1])))
            last = all_queries[0]
        mixed = attention(queries_late, keys_late, values_late)

        flat = fast_weights.reshape(3 * rows, D)
        olds = flat[:cut(rows)], flat[cut(rows):]
        stepped = []
        for old, (part, keep) in zip(olds, chunks):
            for bit in bits[:-1]:
                part, keep = fold(keep, send(part, along(bit)))
            updated = step(old, keep, send(part, along(bits[-1])))
            stepped.append(line_gather(updated))
        pairs = list(zip(*stepped))
        pairs += [[send(chunk, swap) for chunk in block] for block in pairs]

        outs = apply_rows(all_queries + [query_normed], pairs, rows)
        back = [send(part, layer(*o)) for part, o in zip(outs[:-1], offsets)]
        return call(total_kernel, [struct(queries.shape, BF)], outs[-1], mixed, *back, name="total")[0]

    in_specs = (
        P(("grp", "dev"), None),
        P(("grp", "dev"), None),
        P(("grp", "dev"), None),
        P(("grp", "dev")),
        P(None, ("grp", "dev"), None),
    )
    out_specs = P(("grp", "dev"), None)
    return jax.shard_map(body, mesh=mesh, in_specs=in_specs, out_specs=out_specs, check_vma=False)
```

```python
import jax
import jax.numpy as jnp
from jax import lax
from jax.experimental import pallas as pl
from jax.experimental.pallas import tpu as pltpu
from jax.sharding import Mesh, PartitionSpec as P

D = 768
HEADS = 12
HEAD_DIM = 64
CORES = 2
NEAR = 2
BF = jnp.bfloat16
F32 = jnp.float32

epsilon = 1e-06
AXES = ("gx", "core", "far", "near")


def moves(mesh):
    n_grp, n_dev = mesh.shape["grp"], mesh.shape["dev"]
    n_gx, n_far = n_grp // CORES, n_dev // NEAR

    def build(target):
        pairs = []
        for gx in range(n_gx):
            for core in range(CORES):
                for far in range(n_far):
                    for near in range(NEAR):
                        to = target(gx, core, far, near)
                        source = (gx * CORES + core) * n_dev + far * NEAR + near
                        dest = (to[0] * CORES + to[1]) * n_dev + to[2] * NEAR + to[3]
                        pairs.append((source, dest))
        return pairs

    def along(step):
        return build(lambda gx, core, far, near: (gx, core, far ^ step, near))

    def layer(dx, dn):
        return build(lambda gx, core, far, near: ((gx + dx) % n_gx, core, far, (near + dn) % NEAR))

    swap = build(lambda gx, core, far, near: (gx, 1 - core, far, near))
    offsets = [(dx, dn) for dx in reversed(range(n_gx)) for dn in reversed(range(NEAR))][:-1]
    return n_far, along, layer, swap, offsets


def send(array, pairs):
    return lax.ppermute(array, AXES, pairs)


def after(value, *others):
    return lax.optimization_barrier((value, *others))[0]


def call(kernel, outs, *args, flops=0, scratch=(), in_hbm=(), limit=32 * 1024 * 1024, name=None):
    vmem = pl.BlockSpec(memory_space=pltpu.VMEM)
    size = sum(a.size * a.dtype.itemsize for a in args) + sum(o.size * o.dtype.itemsize for o in outs)
    result = pl.pallas_call(
        kernel,
        out_shape=list(outs),
        in_specs=[pl.BlockSpec(memory_space=pltpu.HBM) if i in in_hbm else vmem for i in range(len(args))],
        out_specs=[vmem] * len(outs),
        scratch_shapes=list(scratch),
        compiler_params=pltpu.CompilerParams(vmem_limit_bytes=limit),
        cost_estimate=pl.CostEstimate(flops=flops, bytes_accessed=size, transcendentals=0),
        name=name,
    )(*args)
    return result


def struct(shape, dtype):
    return jax.ShapeDtypeStruct(shape, dtype)


def nt(a, b):
    return lax.dot_general(a, b, (((1,), (1,)), ((), ())), preferred_element_type=F32)


def nn(a, b):
    return lax.dot_general(a, b, (((1,), (0,)), ((), ())), preferred_element_type=F32)


def rms(matrix):
    return matrix / jnp.sqrt(jnp.mean(matrix * matrix, axis=-1, keepdims=True) + epsilon)


def prep_kernel(key_hbm, value_hbm, query_hbm, rate_hbm, pair_ref, query_out, key_ref, value_ref, query_ref, rate_ref, sems):
    count = key_ref.shape[0]
    sources = (key_hbm, rate_hbm, value_hbm, query_hbm)
    targets = (key_ref, rate_ref, value_ref, query_ref)
    copies = [pltpu.make_async_copy(a, b, sems.at[i]) for i, (a, b) in enumerate(zip(sources, targets))]
    for copy in copies:
        copy.start()
    copies[0].wait()
    pair_ref[0] = rms(key_ref[...].astype(F32)).astype(BF)
    copies[1].wait()
    copies[2].wait()
    spread = jnp.broadcast_to(rate_ref[...], (count, count))
    row = lax.broadcasted_iota(jnp.int32, (count, count), 0)
    col = lax.broadcasted_iota(jnp.int32, (count, count), 1)
    rate = jnp.sum(jnp.where(row == col, spread, 0.0), axis=1, keepdims=True)
    pair_ref[1] = (-(rate * value_ref[...].astype(F32))).astype(BF)
    copies[3].wait()
    query_out[...] = rms(query_ref[...].astype(F32)).astype(BF)


def prep(key_tokens, value_tokens, queries, token_rate):
    count = key_tokens.shape[0]
    return call(
        prep_kernel,
        [struct((2, count, D), BF), struct((count, D), BF)],
        key_tokens, value_tokens, queries, token_rate.reshape(1, count),
        scratch=[pltpu.VMEM((count, D), BF)] * 3 + [pltpu.VMEM((1, count), F32), pltpu.SemaphoreType.DMA((4,))],
        in_hbm=(0, 1, 2, 3),
        limit=62 * 1024 * 1024,
        name="prep",
    )


def cut(rows):
    return 16 * ((3 * rows + 31) // 32)


def pieces(rows):
    edge = cut(rows)
    found = []
    for m in range(3):
        for low, high, chunk in ((0, edge, 0), (edge, 3 * rows, 1)):
            first, last = max(low, m * rows), min(high, (m + 1) * rows)
            if first < last:
                found.append((m, first - m * rows, last - first, chunk, first - low))
    return found


def gradient(pairs, blocks):
    count = pairs[0].shape[1]
    number, rows = len(blocks), blocks[0].shape[1]
    aligned = rows % 16 == 0
    if not aligned:
        blocks = [jnp.concatenate(blocks, axis=1)]
    sizes = [b.shape[1] for b in blocks]
    units = number * rows
    group = 2 if len(pairs) % 2 == 0 else 1

    def kernel(*refs):
        pair_refs = refs[:len(pairs)]
        block_refs = refs[len(pairs):len(pairs) + len(blocks)]
        out_refs = refs[len(pairs) + len(blocks):-4]
        weights, total, own, sem = refs[-4:]
        fetch = pltpu.make_async_copy(pair_refs[-1], own, sem)
        fetch.start()
        pair_refs = [*pair_refs[:-1], own]
        for i, ref in enumerate(block_refs):
            for m in range(3):
                weights[m * units + i * sizes[0]:m * units + (i + 1) * sizes[0]] = ref[m]
        for j in range(0, len(pairs), group):
            if j + group == len(pairs):
                fetch.wait()
            keys = jnp.concatenate([pair_refs[j + i][0] for i in range(group)], axis=0)
            signal = jnp.concatenate([pair_refs[j + i][1] for i in range(group)], axis=0)
            acts = nt(weights[:2 * units], keys)
            gate_act, up_act = acts[:units], acts[units:]
            sg = jax.nn.sigmoid(gate_act)
            silu = gate_act * sg
            hidden = (silu * up_act).astype(BF)
            hidden_grad = nt(weights[2 * units:], signal)
            gate_grad = (hidden_grad * up_act * sg * (1.0 + gate_act * (1.0 - sg))).astype(BF)
            up_grad = (hidden_grad * silu).astype(BF)
            first = nn(jnp.concatenate([gate_grad, up_grad], axis=0), keys)
            last = nn(hidden, signal)
            if j == 0:
                total[:2 * units] = first
                total[2 * units:] = last
            else:
                total[:2 * units] += first
                total[2 * units:] += last
        if not aligned:
            out_refs[0][...] = total[...]
            return
        for m, row, size, chunk, place in pieces(rows):
            for k in range(number):
                source = total[m * units + k * rows + row:m * units + k * rows + row + size]
                out = out_refs[2 * chunk + (k + 1) % 2]
                out[k // 2, place:place + size] = source.astype(out.dtype)

    edges = (cut(rows), 3 * rows - cut(rows))
    if aligned:
        outs = [struct((number // 2, edge, D), kind) for edge in edges for kind in (BF, F32)]
    else:
        outs = [struct((3 * units, D), F32)]
    outs = call(
        kernel, outs, *pairs, *blocks,
        flops=12 * count * len(pairs) * units * D,
        scratch=[
            pltpu.VMEM((3 * units, D), BF),
            pltpu.VMEM((3 * units, D), F32),
            pltpu.VMEM(pairs[-1].shape, BF),
            pltpu.SemaphoreType.DMA(()),
        ],
        in_hbm=(len(pairs) - 1,),
        name="gradient",
    )
    if aligned:
        return outs[:2], outs[2:]
    total = outs[0].reshape(3, number, rows, D).swapaxes(0, 1).reshape(number, 3 * rows, D)
    parts = total[:, :edges[0]], total[:, edges[0]:]
    return [(part[1::2].astype(BF), part[::2]) for part in parts]


def fold(keep, arrived):
    number, rows = keep.shape[:2]

    def kernel(keep_ref, arrived_ref, send_ref, kept_ref):
        for k in range(number):
            total = keep_ref[k] + arrived_ref[k].astype(F32)
            out = send_ref if k % 2 else kept_ref
            out[k // 2] = total.astype(out.dtype)

    shape = (number // 2, rows, D)
    return call(kernel, [struct(shape, BF), struct(shape, F32)], keep, arrived, name="fold")


def step(old, keep, arrived):
    def kernel(old_ref, keep_ref, arrived_ref, out_ref):
        old_rows = old_ref[...].astype(F32)
        stepped = old_rows - (keep_ref[0] + arrived_ref[0].astype(F32))
        out_ref[...] = (
            stepped
            * jnp.sqrt(jnp.mean(old_rows * old_rows, axis=-1, keepdims=True) + epsilon)
            / jnp.sqrt(jnp.mean(stepped * stepped, axis=-1, keepdims=True) + epsilon)
        ).astype(BF)

    return call(kernel, [struct(old.shape, BF)], old, keep, arrived, name="step")[0]


def attention_kernel(query_ref, key_ref, value_ref, out_ref):
    count = key_ref.shape[0]
    width = 2 * HEAD_DIM
    low = lax.broadcasted_iota(jnp.int32, (count, width), 1) < HEAD_DIM
    zero = jnp.zeros((count, width), BF)
    for h in range(HEADS // 2):
        cols = slice(h * width, (h + 1) * width)
        query, key, value = query_ref[:, cols], key_ref[:, cols], value_ref[:, cols]
        probs = []
        for keep in (low, ~low):
            scores = nt(query, jnp.where(keep, key, zero)) * HEAD_DIM ** (-0.5)
            weights = jnp.exp(scores - jnp.max(scores, axis=-1, keepdims=True))
            probs.append((weights / jnp.sum(weights, axis=-1, keepdims=True)).astype(BF))
        values = jnp.concatenate([jnp.where(low, value, zero), jnp.where(low, zero, value)], axis=0)
        out_ref[:, cols] = nn(jnp.concatenate(probs, axis=1), values)


def attention(queries, key_tokens, value_tokens):
    return call(
        attention_kernel, [struct(queries.shape, F32)], queries, key_tokens, value_tokens,
        flops=4 * queries.shape[0] * key_tokens.shape[0] * D, name="attention",
    )[0]


def apply_rows(queries, blocks, rows, offsets):
    count = queries.shape[1]
    number = len(blocks)
    aligned = rows % 16 == 0
    if not aligned:
        whole = [jnp.concatenate(chunks, axis=0).reshape(3, rows, D) for chunks in blocks]
        blocks = [[jnp.concatenate(whole, axis=1).reshape(3 * number * rows, D)]]
    chunks = [chunk for block in blocks for chunk in block]
    units = number * rows

    def kernel(gathered_ref, *refs):
        chunk_refs = refs[:len(chunks)]
        out_refs = refs[len(chunks):-3]
        weights, query_ref, sem = refs[-3:]
        fetch = pltpu.make_async_copy(gathered_ref, query_ref, sem)
        fetch.start()
        if aligned:
            for i in range(number):
                for m, row, size, chunk, place in pieces(rows):
                    start = m * units + i * rows + row
                    weights[start:start + size] = chunk_refs[2 * i + chunk][place:place + size]
        else:
            weights[...] = chunk_refs[0][...]
        gx, near = lax.axis_index("gx"), lax.axis_index("near")
        n_gx = query_ref.shape[0] // NEAR
        fetch.wait()
        places = [lax.rem(gx + dx, n_gx) * NEAR + lax.rem(near + dn, NEAR) for dx, dn in [*offsets, (0, 0)]]
        stacked = jnp.concatenate([query_ref[place] for place in places], axis=0)
        gate_act = nt(stacked, weights[:units])
        up_act = nt(stacked, weights[units:2 * units])
        hidden = (jax.nn.silu(gate_act) * up_act).astype(BF)
        result = nn(hidden, weights[2 * units:])
        for i, out in enumerate(out_refs):
            out[...] = result[i * count:(i + 1) * count].astype(out.dtype)

    outs = [struct((count, D), BF) for _ in offsets] + [struct((count, D), F32)]
    return call(
        kernel, outs, queries, *chunks,
        flops=6 * queries.shape[0] * count * units * D,
        scratch=[
            pltpu.VMEM((3 * units, D), BF),
            pltpu.VMEM(queries.shape, BF),
            pltpu.SemaphoreType.DMA(()),
        ],
        in_hbm=(0,),
        name="apply",
    )


def total_kernel(*refs):
    result = refs[0][...] + refs[1][...]
    for ref in refs[2:-1]:
        result = result + ref[...].astype(F32)
    refs[-1][...] = result.astype(BF)


def solution(mesh):
    n_far, along, layer, swap, offsets = moves(mesh)
    bits = [1 << i for i in range(n_far.bit_length() - 1)]

    def line_gather(block):
        blocks = {0: block}
        for bit in reversed(bits):
            for k in list(blocks):
                blocks[k ^ bit] = send(blocks[k], along(bit))
        return [blocks[k] for k in range(n_far)]

    def body(key_tokens, value_tokens, queries, token_rate, fast_weights):
        rows = fast_weights.shape[1]
        blocks = line_gather(fast_weights)

        pair, query_normed = prep(key_tokens, value_tokens, queries, token_rate)
        here = [send(pair, layer(*o)) for o in offsets]
        own_there = send(after(pair, *blocks), swap)
        there = [send(block, swap) for block in here]

        chunks = gradient([own_there] + here + there + [pair], blocks)
        queries_late, keys_late, values_late, query_normed = lax.optimization_barrier(
            (queries, key_tokens, value_tokens, query_normed, chunks[0][0])
        )[:4]
        gathered = lax.all_gather(query_normed, ("gx", "near"), axis=0)
        mixed = attention(queries_late, keys_late, values_late)

        flat = fast_weights.reshape(3 * rows, D)
        olds = flat[:cut(rows)], flat[cut(rows):]
        stepped = []
        for old, (part, keep) in zip(olds, chunks):
            for bit in bits[:-1]:
                part, keep = fold(keep, send(part, along(bit)))
            updated = step(old, keep, send(part, along(bits[-1])))
            stepped.append(line_gather(updated))
        pairs = list(zip(*stepped))
        pairs += [[send(chunk, swap) for chunk in block] for block in pairs]

        outs = apply_rows(gathered, pairs, rows, offsets)
        back = [send(part, layer(*o)) for part, o in zip(outs[:-1], offsets)]
        return call(total_kernel, [struct(queries.shape, BF)], outs[-1], mixed, *back, name="total")[0]

    view = Mesh(mesh.devices.reshape(mesh.shape["grp"] // CORES, CORES, n_far, NEAR), AXES)
    in_specs = (P(AXES, None), P(AXES, None), P(AXES, None), P(AXES), P(None, AXES, None))
    return jax.shard_map(body, mesh=view, in_specs=in_specs, out_specs=P(AXES, None), check_vma=False)
```

```python
import jax
import jax.numpy as jnp
from jax import lax
from jax.experimental import pallas as pl
from jax.experimental.pallas import tpu as pltpu
from jax.sharding import PartitionSpec as P

D = 768
HEADS = 12
HEAD_DIM = 64
CORES = 2
NEAR = 2
BF = jnp.bfloat16
F32 = jnp.float32

epsilon = 1e-06
AXES = ("grp", "dev")


def moves(mesh):
    n_grp, n_dev = mesh.shape["grp"], mesh.shape["dev"]
    n_gx, n_far = n_grp // CORES, n_dev // NEAR

    def build(target):
        pairs = []
        for gx in range(n_gx):
            for core in range(CORES):
                for far in range(n_far):
                    for near in range(NEAR):
                        to = target(gx, core, far, near)
                        source = (gx * CORES + core) * n_dev + far * NEAR + near
                        dest = (to[0] * CORES + to[1]) * n_dev + to[2] * NEAR + to[3]
                        pairs.append((source, dest))
        return pairs

    def along(step):
        return build(lambda gx, core, far, near: (gx, core, far ^ step, near))

    def layer(dx, dn):
        return build(lambda gx, core, far, near: ((gx + dx) % n_gx, core, far, (near + dn) % NEAR))

    swap = build(lambda gx, core, far, near: (gx, 1 - core, far, near))
    offsets = [(dx, dn) for dx in reversed(range(n_gx)) for dn in reversed(range(NEAR))][:-1]
    return n_far, along, layer, swap, offsets


def send(array, pairs):
    return lax.ppermute(array, AXES, pairs)


def after(value, *others):
    return lax.optimization_barrier((value, *others))[0]


def call(kernel, outs, *args, flops=0, scratch=(), space=pltpu.VMEM, limit=32 * 1024 * 1024, name=None):
    vmem = pl.BlockSpec(memory_space=pltpu.VMEM)
    size = sum(a.size * a.dtype.itemsize for a in args) + sum(o.size * o.dtype.itemsize for o in outs)
    result = pl.pallas_call(
        kernel,
        out_shape=list(outs),
        in_specs=[pl.BlockSpec(memory_space=space)] * len(args),
        out_specs=[vmem] * len(outs),
        scratch_shapes=list(scratch),
        compiler_params=pltpu.CompilerParams(vmem_limit_bytes=limit),
        cost_estimate=pl.CostEstimate(flops=flops, bytes_accessed=size, transcendentals=0),
        name=name,
    )(*args)
    return result


def struct(shape, dtype):
    return jax.ShapeDtypeStruct(shape, dtype)


def nt(a, b):
    return lax.dot_general(a, b, (((1,), (1,)), ((), ())), preferred_element_type=F32)


def nn(a, b):
    return lax.dot_general(a, b, (((1,), (0,)), ((), ())), preferred_element_type=F32)


def rms(matrix):
    return matrix / jnp.sqrt(jnp.mean(matrix * matrix, axis=-1, keepdims=True) + epsilon)


def prep_kernel(key_hbm, value_hbm, query_hbm, rate_hbm, pair_ref, query_out, key_ref, value_ref, query_ref, rate_ref, sems):
    count = key_ref.shape[0]
    sources = (key_hbm, rate_hbm, value_hbm, query_hbm)
    targets = (key_ref, rate_ref, value_ref, query_ref)
    copies = [pltpu.make_async_copy(a, b, sems.at[i]) for i, (a, b) in enumerate(zip(sources, targets))]
    for copy in copies:
        copy.start()
    copies[0].wait()
    pair_ref[0] = rms(key_ref[...].astype(F32)).astype(BF)
    copies[1].wait()
    copies[2].wait()
    spread = jnp.broadcast_to(rate_ref[...], (count, count))
    row = lax.broadcasted_iota(jnp.int32, (count, count), 0)
    col = lax.broadcasted_iota(jnp.int32, (count, count), 1)
    rate = jnp.sum(jnp.where(row == col, spread, 0.0), axis=1, keepdims=True)
    pair_ref[1] = (-(rate * value_ref[...].astype(F32))).astype(BF)
    copies[3].wait()
    query_out[...] = rms(query_ref[...].astype(F32)).astype(BF)


def prep(key_tokens, value_tokens, queries, token_rate):
    count = key_tokens.shape[0]
    return call(
        prep_kernel,
        [struct((2, count, D), BF), struct((count, D), BF)],
        key_tokens, value_tokens, queries, token_rate.reshape(1, count),
        scratch=[pltpu.VMEM((count, D), BF)] * 3 + [pltpu.VMEM((1, count), F32), pltpu.SemaphoreType.DMA((4,))],
        space=pltpu.HBM,
        limit=62 * 1024 * 1024,
        name="prep",
    )


def gradient(pairs, blocks, before=None):
    count = pairs[0].shape[1]
    sizes = [b.shape[1] for b in blocks]
    starts = [sum(sizes[:i]) for i in range(len(sizes))]
    units = sum(sizes)
    group = 2 if len(pairs) % 2 == 0 else 1
    given = before is not None

    def kernel(*refs):
        pair_refs = refs[:len(pairs)]
        block_refs = refs[len(pairs):len(pairs) + len(blocks)]
        out_refs = refs[len(pairs) + len(blocks) + given:-1 - given]
        weights = refs[-1]
        total = refs[-2] if given else out_refs[0]
        for ref, start, size in zip(block_refs, starts, sizes):
            for m in range(3):
                weights[m * units + start:m * units + start + size] = ref[m]
        for j in range(0, len(pairs), group):
            keys = jnp.concatenate([pair_refs[j + i][0] for i in range(group)], axis=0)
            signal = jnp.concatenate([pair_refs[j + i][1] for i in range(group)], axis=0)
            acts = nt(weights[:2 * units], keys)
            gate_act, up_act = acts[:units], acts[units:]
            sg = jax.nn.sigmoid(gate_act)
            silu = gate_act * sg
            hidden = (silu * up_act).astype(BF)
            hidden_grad = nt(weights[2 * units:], signal)
            gate_grad = (hidden_grad * up_act * sg * (1.0 + gate_act * (1.0 - sg))).astype(BF)
            up_grad = (hidden_grad * silu).astype(BF)
            first = nn(jnp.concatenate([gate_grad, up_grad], axis=0), keys)
            last = nn(hidden, signal)
            base = refs[len(pairs) + len(blocks)] if j == 0 and given else total if j else None
            total[:2 * units] = first if base is None else base[:2 * units] + first
            total[2 * units:] = last if base is None else base[2 * units:] + last
        if given:
            for out, start, size in zip(out_refs, starts, sizes):
                for m in range(3):
                    out[m] = total[m * units + start:m * units + start + size].astype(out.dtype)

    scratch = [pltpu.VMEM((3 * units, D), BF)]
    if given:
        outs = [struct((3, s, D), F32 if i == 0 else BF) for i, s in enumerate(sizes)]
        scratch = [pltpu.VMEM((3 * units, D), F32), *scratch]
    else:
        outs = [struct((3 * units, D), F32)]
    result = call(
        kernel, outs, *pairs, *blocks, *([before] if given else []),
        flops=12 * count * len(pairs) * units * D,
        scratch=scratch,
        name="gradient" if given else "gradient_part",
    )
    return result if given else result[0]


def step(old, own, others):
    def kernel(old_ref, own_ref, *refs):
        for m in range(3):
            grad = own_ref[m]
            for ref in refs[:-1]:
                grad = grad + ref[m].astype(F32)
            old_rows = old_ref[m].astype(F32)
            stepped = old_rows - grad
            refs[-1][m] = (
                stepped
                * jnp.sqrt(jnp.mean(old_rows * old_rows, axis=-1, keepdims=True) + epsilon)
                / jnp.sqrt(jnp.mean(stepped * stepped, axis=-1, keepdims=True) + epsilon)
            ).astype(BF)

    return call(kernel, [struct(old.shape, BF)], old, own, *others, name="step")[0]


def attention_kernel(query_ref, key_ref, value_ref, out_ref):
    count = key_ref.shape[0]
    width = 2 * HEAD_DIM
    low = lax.broadcasted_iota(jnp.int32, (count, width), 1) < HEAD_DIM
    zero = jnp.zeros((count, width), BF)
    for h in range(HEADS // 2):
        cols = slice(h * width, (h + 1) * width)
        query, key, value = query_ref[:, cols], key_ref[:, cols], value_ref[:, cols]
        probs = []
        for keep in (low, ~low):
            scores = nt(query, jnp.where(keep, key, zero)) * HEAD_DIM ** (-0.5)
            weights = jnp.exp(scores - jnp.max(scores, axis=-1, keepdims=True))
            probs.append((weights / jnp.sum(weights, axis=-1, keepdims=True)).astype(BF))
        values = jnp.concatenate([jnp.where(low, value, zero), jnp.where(low, zero, value)], axis=0)
        out_ref[:, cols] = nn(jnp.concatenate(probs, axis=1), values)


def attention(queries, key_tokens, value_tokens):
    return call(
        attention_kernel, [struct(queries.shape, F32)], queries, key_tokens, value_tokens,
        flops=4 * queries.shape[0] * key_tokens.shape[0] * D, name="attention",
    )[0]


def apply_rows(queries, blocks):
    count = queries[0].shape[0]
    sizes = [b.shape[1] for b in blocks]
    starts = [sum(sizes[:i]) for i in range(len(sizes))]
    units = sum(sizes)

    def kernel(*refs):
        query_refs = refs[:len(queries)]
        block_refs = refs[len(queries):len(queries) + len(blocks)]
        out_refs = refs[len(queries) + len(blocks):-1]
        weights = refs[-1]
        for ref, start, size in zip(block_refs, starts, sizes):
            for m in range(3):
                weights[m * units + start:m * units + start + size] = ref[m]
        rows = jnp.concatenate([ref[...] for ref in query_refs], axis=0)
        gate_act = nt(rows, weights[:units])
        up_act = nt(rows, weights[units:2 * units])
        hidden = (jax.nn.silu(gate_act) * up_act).astype(BF)
        result = nn(hidden, weights[2 * units:])
        for i, out in enumerate(out_refs):
            out[...] = result[i * count:(i + 1) * count].astype(out.dtype)

    outs = [struct((count, D), BF) for _ in queries[:-1]] + [struct((count, D), F32)]
    return call(
        kernel, outs, *queries, *blocks,
        flops=6 * count * len(queries) * units * D,
        scratch=[pltpu.VMEM((3 * units, D), BF)],
        name="apply",
    )


def total_kernel(*refs):
    result = refs[0][...] + refs[1][...]
    for ref in refs[2:-1]:
        result = result + ref[...].astype(F32)
    refs[-1][...] = result.astype(BF)


def solution(mesh):
    n_far, along, layer, swap, offsets = moves(mesh)
    bits = [1 << i for i in range(n_far.bit_length() - 1)]
    steps = [*range(2, n_far), 1]

    def line_gather(block):
        blocks = {0: block}
        for bit in reversed(bits):
            for k in list(blocks):
                blocks[k ^ bit] = send(blocks[k], along(bit))
        return [blocks[k] for k in [0, *steps]]

    def joined(blocks):
        if blocks[0].shape[1] % 16 == 0:
            return blocks
        return [jnp.concatenate(blocks, axis=1)]

    def body(key_tokens, value_tokens, queries, token_rate, fast_weights):
        rows = fast_weights.shape[1]
        line = line_gather(fast_weights)
        blocks = joined(line)

        pair, query_normed = prep(key_tokens, value_tokens, queries, token_rate)
        here = {o: send(pair, layer(*o)) for o in offsets}
        own_there = send(after(pair, *line), swap)
        there = {o: send(here[o], swap) for o in offsets}
        late = [o for o in offsets if o[0] and o[1]]
        early = [o for o in offsets if o not in late]
        part = gradient([pair, own_there] + [source[o] for source in (here, there) for o in early], blocks)
        grads = gradient([source[o] for source in (here, there) for o in late], blocks, part)
        if len(blocks) > 1:
            own_grad, parts = grads[0], grads[1:]
        else:
            own_grad = grads[0][:, :rows]
            parts = [grads[0][:, i * rows:(i + 1) * rows].astype(BF) for i in range(1, n_far)]
        arrived = [send(part, along(k)) for part, k in zip(parts, steps)]

        queries_late, keys_late, values_late, query_normed = lax.optimization_barrier(
            (queries, key_tokens, value_tokens, query_normed, own_grad)
        )[:4]
        all_queries = [send(query_normed, layer(-o[0], -o[1])) for o in offsets[:-1]]
        own_grad = after(own_grad, *all_queries)
        mixed = attention(queries_late, keys_late, values_late)

        updated = step(fast_weights, own_grad, arrived)
        updated, mixed, query_normed = lax.optimization_barrier((updated, mixed, query_normed))
        stepped = [updated] + [send(updated, along(k)) for k in steps]
        all_queries += [send(query_normed, layer(-o[0], -o[1])) for o in offsets[-1:]]
        stepped_there = [send(after(block, all_queries[-1]) if i == 1 else block, swap) for i, block in enumerate(stepped)]

        outs = apply_rows(all_queries + [query_normed], joined(stepped + stepped_there))
        back = [send(part, layer(*o)) for part, o in zip(outs[:-1], offsets)]
        return call(total_kernel, [struct(queries.shape, BF)], outs[-1], mixed, *back, name="total")[0]

    in_specs = (
        P(("grp", "dev"), None),
        P(("grp", "dev"), None),
        P(("grp", "dev"), None),
        P(("grp", "dev")),
        P(None, ("grp", "dev"), None),
    )
    out_specs = P(("grp", "dev"), None)
    return jax.shard_map(body, mesh=mesh, in_specs=in_specs, out_specs=out_specs, check_vma=False)
```

```python
import jax
import jax.numpy as jnp
from jax import lax
from jax.experimental import pallas as pl
from jax.experimental.pallas import tpu as pltpu
from jax.sharding import PartitionSpec as P

D = 768
HEADS = 12
HEAD_DIM = 64
CORES = 2
NEAR = 2
BF = jnp.bfloat16
F32 = jnp.float32

epsilon = 1e-06
AXES = ("grp", "dev")


def moves(mesh):
    n_grp, n_dev = mesh.shape["grp"], mesh.shape["dev"]
    n_gx, n_far = n_grp // CORES, n_dev // NEAR

    def build(target):
        pairs = []
        for gx in range(n_gx):
            for core in range(CORES):
                for far in range(n_far):
                    for near in range(NEAR):
                        to = target(gx, core, far, near)
                        source = (gx * CORES + core) * n_dev + far * NEAR + near
                        dest = (to[0] * CORES + to[1]) * n_dev + to[2] * NEAR + to[3]
                        pairs.append((source, dest))
        return pairs

    def along(step):
        return build(lambda gx, core, far, near: (gx, core, far ^ step, near))

    def layer(dx, dn):
        return build(lambda gx, core, far, near: ((gx + dx) % n_gx, core, far, (near + dn) % NEAR))

    swap = build(lambda gx, core, far, near: (gx, 1 - core, far, near))
    offsets = [(dx, dn) for dx in reversed(range(n_gx)) for dn in range(NEAR) if dx or dn]
    return n_far, along, layer, swap, offsets


def send(array, pairs):
    return lax.ppermute(array, AXES, pairs)


def after(value, *others):
    return lax.optimization_barrier((value, *others))[0]


def call(kernel, outs, *args, flops=0, scratch=(), space=pltpu.VMEM, limit=32 * 1024 * 1024, name=None):
    vmem = pl.BlockSpec(memory_space=pltpu.VMEM)
    size = sum(a.size * a.dtype.itemsize for a in args) + sum(o.size * o.dtype.itemsize for o in outs)
    result = pl.pallas_call(
        kernel,
        out_shape=list(outs),
        in_specs=[pl.BlockSpec(memory_space=space)] * len(args),
        out_specs=[vmem] * len(outs),
        scratch_shapes=list(scratch),
        compiler_params=pltpu.CompilerParams(vmem_limit_bytes=limit),
        cost_estimate=pl.CostEstimate(flops=flops, bytes_accessed=size, transcendentals=0),
        name=name,
    )(*args)
    return result


def struct(shape, dtype):
    return jax.ShapeDtypeStruct(shape, dtype)


def nt(a, b):
    return lax.dot_general(a, b, (((1,), (1,)), ((), ())), preferred_element_type=F32)


def nn(a, b):
    return lax.dot_general(a, b, (((1,), (0,)), ((), ())), preferred_element_type=F32)


def rms(matrix):
    return matrix / jnp.sqrt(jnp.mean(matrix * matrix, axis=-1, keepdims=True) + epsilon)


def prep_kernel(key_hbm, value_hbm, query_hbm, rate_hbm, pair_ref, query_out, key_ref, value_ref, query_ref, rate_ref, sems):
    count = key_ref.shape[0]
    sources = (key_hbm, rate_hbm, value_hbm, query_hbm)
    targets = (key_ref, rate_ref, value_ref, query_ref)
    copies = [pltpu.make_async_copy(a, b, sems.at[i]) for i, (a, b) in enumerate(zip(sources, targets))]
    for copy in copies:
        copy.start()
    copies[0].wait()
    pair_ref[0] = rms(key_ref[...].astype(F32)).astype(BF)
    copies[1].wait()
    copies[2].wait()
    spread = jnp.broadcast_to(rate_ref[...], (count, count))
    row = lax.broadcasted_iota(jnp.int32, (count, count), 0)
    col = lax.broadcasted_iota(jnp.int32, (count, count), 1)
    rate = jnp.sum(jnp.where(row == col, spread, 0.0), axis=1, keepdims=True)
    pair_ref[1] = (-(rate * value_ref[...].astype(F32))).astype(BF)
    copies[3].wait()
    query_out[...] = rms(query_ref[...].astype(F32)).astype(BF)


def prep(key_tokens, value_tokens, queries, token_rate):
    count = key_tokens.shape[0]
    return call(
        prep_kernel,
        [struct((2, count, D), BF), struct((count, D), BF)],
        key_tokens, value_tokens, queries, token_rate.reshape(1, count),
        scratch=[pltpu.VMEM((count, D), BF)] * 3 + [pltpu.VMEM((1, count), F32), pltpu.SemaphoreType.DMA((4,))],
        space=pltpu.HBM,
        limit=62 * 1024 * 1024,
        name="prep",
    )


def stage(*arrays):
    def kernel(*refs):
        for source, target in zip(refs[:len(arrays)], refs[len(arrays):]):
            target[...] = source[...]

    return call(kernel, [struct(a.shape, a.dtype) for a in arrays], *arrays, name="stage")


def gradient(pairs, blocks, before=None):
    count = pairs[0].shape[1]
    sizes = [b.shape[1] for b in blocks]
    starts = [sum(sizes[:i]) for i in range(len(sizes))]
    units = sum(sizes)
    group = 2 if len(pairs) % 2 == 0 else 1
    given = before is not None

    def kernel(*refs):
        pair_refs = refs[:len(pairs)]
        block_refs = refs[len(pairs):len(pairs) + len(blocks)]
        out_refs = refs[len(pairs) + len(blocks) + given:-1 - given]
        weights = refs[-1]
        total = refs[-2] if given else out_refs[0]
        for ref, start, size in zip(block_refs, starts, sizes):
            for m in range(3):
                weights[m * units + start:m * units + start + size] = ref[m]
        for j in range(0, len(pairs), group):
            keys = jnp.concatenate([pair_refs[j + i][0] for i in range(group)], axis=0)
            signal = jnp.concatenate([pair_refs[j + i][1] for i in range(group)], axis=0)
            acts = nt(weights[:2 * units], keys)
            gate_act, up_act = acts[:units], acts[units:]
            sg = jax.nn.sigmoid(gate_act)
            silu = gate_act * sg
            hidden = (silu * up_act).astype(BF)
            hidden_grad = nt(weights[2 * units:], signal)
            gate_grad = (hidden_grad * up_act * sg * (1.0 + gate_act * (1.0 - sg))).astype(BF)
            up_grad = (hidden_grad * silu).astype(BF)
            first = nn(jnp.concatenate([gate_grad, up_grad], axis=0), keys)
            last = nn(hidden, signal)
            base = refs[len(pairs) + len(blocks)] if j == 0 and given else total if j else None
            total[:2 * units] = first if base is None else base[:2 * units] + first
            total[2 * units:] = last if base is None else base[2 * units:] + last
        if given:
            for out, start, size in zip(out_refs, starts, sizes):
                for m in range(3):
                    out[m] = total[m * units + start:m * units + start + size].astype(out.dtype)

    scratch = [pltpu.VMEM((3 * units, D), BF)]
    if given:
        outs = [struct((3, s, D), F32 if i == 0 else BF) for i, s in enumerate(sizes)]
        scratch = [pltpu.VMEM((3 * units, D), F32), *scratch]
    else:
        outs = [struct((3 * units, D), F32)]
    result = call(
        kernel, outs, *pairs, *blocks, *([before] if given else []),
        flops=12 * count * len(pairs) * units * D,
        scratch=scratch,
        name="gradient" if given else "gradient_part",
    )
    return result if given else result[0]


def step(old, own, others):
    def kernel(old_ref, own_ref, *refs):
        for m in range(3):
            grad = own_ref[m]
            for ref in refs[:-1]:
                grad = grad + ref[m].astype(F32)
            old_rows = old_ref[m].astype(F32)
            stepped = old_rows - grad
            refs[-1][m] = (
                stepped
                * jnp.sqrt(jnp.mean(old_rows * old_rows, axis=-1, keepdims=True) + epsilon)
                / jnp.sqrt(jnp.mean(stepped * stepped, axis=-1, keepdims=True) + epsilon)
            ).astype(BF)

    return call(kernel, [struct(old.shape, BF)], old, own, *others, name="step")[0]


def attention_kernel(query_ref, key_ref, value_ref, out_ref):
    count = key_ref.shape[0]
    width = 2 * HEAD_DIM
    low = lax.broadcasted_iota(jnp.int32, (count, width), 1) < HEAD_DIM
    zero = jnp.zeros((count, width), BF)
    for h in range(HEADS // 2):
        cols = slice(h * width, (h + 1) * width)
        query, key, value = query_ref[:, cols], key_ref[:, cols], value_ref[:, cols]
        probs = []
        for keep in (low, ~low):
            scores = nt(query, jnp.where(keep, key, zero)) * HEAD_DIM ** (-0.5)
            weights = jnp.exp(scores - jnp.max(scores, axis=-1, keepdims=True))
            probs.append((weights / jnp.sum(weights, axis=-1, keepdims=True)).astype(BF))
        values = jnp.concatenate([jnp.where(low, value, zero), jnp.where(low, zero, value)], axis=0)
        out_ref[:, cols] = nn(jnp.concatenate(probs, axis=1), values)


def attention(queries, key_tokens, value_tokens):
    return call(
        attention_kernel, [struct(queries.shape, F32)], queries, key_tokens, value_tokens,
        flops=4 * queries.shape[0] * key_tokens.shape[0] * D, name="attention",
    )[0]


def apply_rows(queries, blocks):
    count = queries[0].shape[0]
    sizes = [b.shape[1] for b in blocks]
    starts = [sum(sizes[:i]) for i in range(len(sizes))]
    units = sum(sizes)

    def kernel(*refs):
        query_refs = refs[:len(queries)]
        block_refs = refs[len(queries):len(queries) + len(blocks)]
        out_refs = refs[len(queries) + len(blocks):-1]
        weights = refs[-1]
        for ref, start, size in zip(block_refs, starts, sizes):
            for m in range(3):
                weights[m * units + start:m * units + start + size] = ref[m]
        rows = jnp.concatenate([ref[...] for ref in query_refs], axis=0)
        gate_act = nt(rows, weights[:units])
        up_act = nt(rows, weights[units:2 * units])
        hidden = (jax.nn.silu(gate_act) * up_act).astype(BF)
        result = nn(hidden, weights[2 * units:])
        for i, out in enumerate(out_refs):
            out[...] = result[i * count:(i + 1) * count].astype(out.dtype)

    outs = [struct((count, D), BF) for _ in queries[:-1]] + [struct((count, D), F32)]
    return call(
        kernel, outs, *queries, *blocks,
        flops=6 * count * len(queries) * units * D,
        scratch=[pltpu.VMEM((3 * units, D), BF)],
        name="apply",
    )


def total_kernel(*refs):
    result = refs[0][...] + refs[1][...]
    for ref in refs[2:-1]:
        result = result + ref[...].astype(F32)
    refs[-1][...] = result.astype(BF)


def solution(mesh):
    n_far, along, layer, swap, offsets = moves(mesh)
    bits = [1 << i for i in range(n_far.bit_length() - 1)]
    steps = [*range(2, n_far), 1]

    def line_gather(block):
        blocks = {0: block}
        for bit in reversed(bits):
            for k in list(blocks):
                blocks[k ^ bit] = send(blocks[k], along(bit))
        return [blocks[k] for k in [0, *steps]]

    def joined(blocks):
        if blocks[0].shape[1] % 16 == 0:
            return blocks
        return [jnp.concatenate(blocks, axis=1)]

    def body(key_tokens, value_tokens, queries, token_rate, fast_weights):
        rows = fast_weights.shape[1]
        line = line_gather(fast_weights)
        pair, query_normed = prep(key_tokens, value_tokens, queries, token_rate)
        here = {o: send(pair, layer(*o)) for o in offsets}
        own_weights, own_pair = stage(after(fast_weights, line[1]), pair)
        own_there = send(after(own_pair, here[offsets[0]], *line), swap)
        there = {o: send(here[o], swap) for o in offsets}
        late = [o for o in offsets if o[0] and o[1]]
        early = [o for o in reversed(offsets) if o not in late]
        blocks = joined([own_weights] + line[1:])
        part = gradient([own_pair, own_there] + [source[o] for source in (here, there) for o in early], blocks)
        grads = gradient([source[o] for source in (here, there) for o in late], blocks, part)
        if len(blocks) > 1:
            own_grad, parts = grads[0], grads[1:]
        else:
            own_grad = grads[0][:, :rows]
            parts = [grads[0][:, i * rows:(i + 1) * rows].astype(BF) for i in range(1, n_far)]
        arrived = [send(part, along(k)) for part, k in zip(parts, steps)]

        queries_late, keys_late, values_late, query_normed = lax.optimization_barrier(
            (queries, key_tokens, value_tokens, query_normed, own_grad)
        )[:4]
        all_queries = [send(query_normed, layer(-o[0], -o[1])) for o in offsets[:-1]]
        own_grad = after(own_grad, *all_queries)
        mixed = attention(queries_late, keys_late, values_late)

        updated = step(own_weights, own_grad, arrived)
        updated, mixed, query_normed = lax.optimization_barrier((updated, mixed, query_normed))
        stepped = [updated] + [send(updated, along(k)) for k in steps]
        all_queries += [send(query_normed, layer(-o[0], -o[1])) for o in offsets[-1:]]
        stepped_there = [send(after(block, all_queries[-1]) if i == 1 else block, swap) for i, block in enumerate(stepped)]

        outs = apply_rows(all_queries + [query_normed], joined(stepped + stepped_there))
        back = [send(part, layer(*o)) for part, o in zip(outs[:-1], offsets)]
        return call(total_kernel, [struct(queries.shape, BF)], outs[-1], mixed, *back, name="total")[0]

    in_specs = (
        P(("grp", "dev"), None),
        P(("grp", "dev"), None),
        P(("grp", "dev"), None),
        P(("grp", "dev")),
        P(None, ("grp", "dev"), None),
    )
    out_specs = P(("grp", "dev"), None)
    return jax.shard_map(body, mesh=mesh, in_specs=in_specs, out_specs=out_specs, check_vma=False)
```

```python
import jax
import jax.numpy as jnp
from jax import lax
from jax.experimental import pallas as pl
from jax.experimental.pallas import tpu as pltpu
from jax.sharding import PartitionSpec as P

D = 768
HEADS = 12
HEAD_DIM = 64
CORES = 2
NEAR = 2
BF = jnp.bfloat16
F32 = jnp.float32

epsilon = 1e-06
AXES = ("grp", "dev")


def moves(mesh):
    n_grp, n_dev = mesh.shape["grp"], mesh.shape["dev"]
    n_gx, n_far = n_grp // CORES, n_dev // NEAR

    def build(target):
        pairs = []
        for gx in range(n_gx):
            for core in range(CORES):
                for far in range(n_far):
                    for near in range(NEAR):
                        to = target(gx, core, far, near)
                        source = (gx * CORES + core) * n_dev + far * NEAR + near
                        dest = (to[0] * CORES + to[1]) * n_dev + to[2] * NEAR + to[3]
                        pairs.append((source, dest))
        return pairs

    def along(step):
        return build(lambda gx, core, far, near: (gx, core, far ^ step, near))

    def layer(dx, dn):
        return build(lambda gx, core, far, near: ((gx + dx) % n_gx, core, far, (near + dn) % NEAR))

    swap = build(lambda gx, core, far, near: (gx, 1 - core, far, near))
    offsets = [(dx, dn) for dx in reversed(range(n_gx)) for dn in range(NEAR) if dx or dn]
    return n_far, along, layer, swap, offsets


def send(array, pairs):
    return lax.ppermute(array, AXES, pairs)


def after(value, *others):
    return lax.optimization_barrier((value, *others))[0]


def call(kernel, outs, *args, flops=0, scratch=(), space=pltpu.VMEM, limit=32 * 1024 * 1024, name=None):
    vmem = pl.BlockSpec(memory_space=pltpu.VMEM)
    size = sum(a.size * a.dtype.itemsize for a in args) + sum(o.size * o.dtype.itemsize for o in outs)
    result = pl.pallas_call(
        kernel,
        out_shape=list(outs),
        in_specs=[pl.BlockSpec(memory_space=space)] * len(args),
        out_specs=[vmem] * len(outs),
        scratch_shapes=list(scratch),
        compiler_params=pltpu.CompilerParams(vmem_limit_bytes=limit),
        cost_estimate=pl.CostEstimate(flops=flops, bytes_accessed=size, transcendentals=0),
        name=name,
    )(*args)
    return result


def struct(shape, dtype):
    return jax.ShapeDtypeStruct(shape, dtype)


def nt(a, b):
    return lax.dot_general(a, b, (((1,), (1,)), ((), ())), preferred_element_type=F32)


def nn(a, b):
    return lax.dot_general(a, b, (((1,), (0,)), ((), ())), preferred_element_type=F32)


def rms(matrix):
    return matrix / jnp.sqrt(jnp.mean(matrix * matrix, axis=-1, keepdims=True) + epsilon)


def prep_kernel(key_hbm, value_hbm, query_hbm, rate_hbm, pair_ref, query_out, key_ref, value_ref, query_ref, rate_ref, sems):
    count = key_ref.shape[0]
    sources = (key_hbm, rate_hbm, value_hbm, query_hbm)
    targets = (key_ref, rate_ref, value_ref, query_ref)
    copies = [pltpu.make_async_copy(a, b, sems.at[i]) for i, (a, b) in enumerate(zip(sources, targets))]
    for copy in copies:
        copy.start()
    copies[0].wait()
    pair_ref[0] = rms(key_ref[...].astype(F32)).astype(BF)
    copies[1].wait()
    copies[2].wait()
    spread = jnp.broadcast_to(rate_ref[...], (count, count))
    row = lax.broadcasted_iota(jnp.int32, (count, count), 0)
    col = lax.broadcasted_iota(jnp.int32, (count, count), 1)
    rate = jnp.sum(jnp.where(row == col, spread, 0.0), axis=1, keepdims=True)
    pair_ref[1] = (-(rate * value_ref[...].astype(F32))).astype(BF)
    copies[3].wait()
    query_out[...] = rms(query_ref[...].astype(F32)).astype(BF)


def prep(key_tokens, value_tokens, queries, token_rate):
    count = key_tokens.shape[0]
    return call(
        prep_kernel,
        [struct((2, count, D), BF), struct((count, D), BF)],
        key_tokens, value_tokens, queries, token_rate.reshape(1, count),
        scratch=[pltpu.VMEM((count, D), BF)] * 3 + [pltpu.VMEM((1, count), F32), pltpu.SemaphoreType.DMA((4,))],
        space=pltpu.HBM,
        limit=62 * 1024 * 1024,
        name="prep",
    )


def stage(*arrays):
    def kernel(*refs):
        for source, target in zip(refs[:len(arrays)], refs[len(arrays):]):
            target[...] = source[...]

    return call(kernel, [struct(a.shape, a.dtype) for a in arrays], *arrays, name="stage")


def gradient(pairs, blocks, before=None):
    count = pairs[0].shape[1]
    sizes = [b.shape[1] for b in blocks]
    starts = [sum(sizes[:i]) for i in range(len(sizes))]
    units = sum(sizes)
    group = 2 if len(pairs) % 2 == 0 else 1
    given = before is not None

    def kernel(*refs):
        pair_refs = refs[:len(pairs)]
        block_refs = refs[len(pairs):len(pairs) + len(blocks)]
        out_refs = refs[len(pairs) + len(blocks) + given:-1 - given]
        weights = refs[-1]
        total = refs[-2] if given else out_refs[0]
        for ref, start, size in zip(block_refs, starts, sizes):
            for m in range(3):
                weights[m * units + start:m * units + start + size] = ref[m]
        for j in range(0, len(pairs), group):
            keys = jnp.concatenate([pair_refs[j + i][0] for i in range(group)], axis=0)
            signal = jnp.concatenate([pair_refs[j + i][1] for i in range(group)], axis=0)
            acts = nt(weights[:2 * units], keys)
            gate_act, up_act = acts[:units], acts[units:]
            sg = jax.nn.sigmoid(gate_act)
            silu = gate_act * sg
            hidden = (silu * up_act).astype(BF)
            hidden_grad = nt(weights[2 * units:], signal)
            gate_grad = (hidden_grad * up_act * sg * (1.0 + gate_act * (1.0 - sg))).astype(BF)
            up_grad = (hidden_grad * silu).astype(BF)
            first = nn(jnp.concatenate([gate_grad, up_grad], axis=0), keys)
            last = nn(hidden, signal)
            base = refs[len(pairs) + len(blocks)] if j == 0 and given else total if j else None
            total[:2 * units] = first if base is None else base[:2 * units] + first
            total[2 * units:] = last if base is None else base[2 * units:] + last
        if given:
            for out, start, size in zip(out_refs, starts, sizes):
                for m in range(3):
                    out[m] = total[m * units + start:m * units + start + size].astype(out.dtype)

    scratch = [pltpu.VMEM((3 * units, D), BF)]
    if given:
        outs = [struct((3, s, D), F32 if i == 0 else BF) for i, s in enumerate(sizes)]
        scratch = [pltpu.VMEM((3 * units, D), F32), *scratch]
    else:
        outs = [struct((3 * units, D), F32)]
    result = call(
        kernel, outs, *pairs, *blocks, *([before] if given else []),
        flops=12 * count * len(pairs) * units * D,
        scratch=scratch,
        name="gradient" if given else "gradient_part",
    )
    return result if given else result[0]


def step(old, own, others):
    def kernel(old_ref, own_ref, *refs):
        for m in range(3):
            grad = own_ref[m]
            for ref in refs[:-1]:
                grad = grad + ref[m].astype(F32)
            old_rows = old_ref[m].astype(F32)
            stepped = old_rows - grad
            refs[-1][m] = (
                stepped
                * jnp.sqrt(jnp.mean(old_rows * old_rows, axis=-1, keepdims=True) + epsilon)
                / jnp.sqrt(jnp.mean(stepped * stepped, axis=-1, keepdims=True) + epsilon)
            ).astype(BF)

    return call(kernel, [struct(old.shape, BF)], old, own, *others, name="step")[0]


def attention_kernel(query_ref, key_ref, value_ref, out_ref):
    count = key_ref.shape[0]
    width = 2 * HEAD_DIM
    low = lax.broadcasted_iota(jnp.int32, (count, width), 1) < HEAD_DIM
    zero = jnp.zeros((count, width), BF)
    for h in range(HEADS // 2):
        cols = slice(h * width, (h + 1) * width)
        query, key, value = query_ref[:, cols], key_ref[:, cols], value_ref[:, cols]
        probs = []
        for keep in (low, ~low):
            scores = nt(query, jnp.where(keep, key, zero)) * HEAD_DIM ** (-0.5)
            weights = jnp.exp(scores - jnp.max(scores, axis=-1, keepdims=True))
            probs.append((weights / jnp.sum(weights, axis=-1, keepdims=True)).astype(BF))
        values = jnp.concatenate([jnp.where(low, value, zero), jnp.where(low, zero, value)], axis=0)
        out_ref[:, cols] = nn(jnp.concatenate(probs, axis=1), values)


def attention(queries, key_tokens, value_tokens):
    return call(
        attention_kernel, [struct(queries.shape, F32)], queries, key_tokens, value_tokens,
        flops=4 * queries.shape[0] * key_tokens.shape[0] * D, name="attention",
    )[0]


def apply_rows(queries, blocks):
    count = queries[0].shape[0]
    sizes = [b.shape[1] for b in blocks]
    starts = [sum(sizes[:i]) for i in range(len(sizes))]
    units = sum(sizes)

    def kernel(*refs):
        query_refs = refs[:len(queries)]
        block_refs = refs[len(queries):len(queries) + len(blocks)]
        out_refs = refs[len(queries) + len(blocks):-1]
        weights = refs[-1]
        for ref, start, size in zip(block_refs, starts, sizes):
            for m in range(3):
                weights[m * units + start:m * units + start + size] = ref[m]
        for j in range(0, len(query_refs), 4):
            rows = jnp.concatenate([ref[...] for ref in query_refs[j:j + 4]], axis=0)
            gate_act = nt(rows, weights[:units])
            up_act = nt(rows, weights[units:2 * units])
            hidden = (jax.nn.silu(gate_act) * up_act).astype(BF)
            result = nn(hidden, weights[2 * units:])
            for i, out in enumerate(out_refs[j:j + 4]):
                out[...] = result[i * count:(i + 1) * count].astype(out.dtype)

    outs = [struct((count, D), BF) for _ in queries[:-1]] + [struct((count, D), F32)]
    return call(
        kernel, outs, *queries, *blocks,
        flops=6 * count * len(queries) * units * D,
        scratch=[pltpu.VMEM((3 * units, D), BF)],
        name="apply",
    )


def total_kernel(*refs):
    result = refs[0][...] + refs[1][...]
    for ref in refs[2:-1]:
        result = result + ref[...].astype(F32)
    refs[-1][...] = result.astype(BF)


def solution(mesh):
    n_far, along, layer, swap, offsets = moves(mesh)
    bits = [1 << i for i in range(n_far.bit_length() - 1)]
    steps = [*range(2, n_far), 1]

    def line_gather(block):
        blocks = {0: block}
        for bit in reversed(bits):
            for k in list(blocks):
                blocks[k ^ bit] = send(blocks[k], along(bit))
        return [blocks[k] for k in [0, *steps]]

    def joined(blocks):
        if blocks[0].shape[1] % 16 == 0:
            return blocks
        return [jnp.concatenate(blocks, axis=1)]

    def body(key_tokens, value_tokens, queries, token_rate, fast_weights):
        rows = fast_weights.shape[1]
        line = line_gather(fast_weights)
        pair, query_normed = prep(key_tokens, value_tokens, queries, token_rate)
        first_query = send(after(query_normed, line[1]), along(steps[0]))
        here = {o: send(pair, layer(*o)) for o in offsets}
        own_weights, own_pair = stage(after(fast_weights, first_query), pair)
        own_there = send(after(own_pair, here[offsets[0]], *line), swap)
        there = {o: send(here[o], swap) for o in offsets}
        late = [o for o in offsets if o[0] and o[1]]
        early = [o for o in reversed(offsets) if o not in late]
        blocks = joined([own_weights] + line[1:])
        part = gradient([own_pair, own_there] + [source[o] for source in (here, there) for o in early], blocks)
        grads = gradient([source[o] for source in (here, there) for o in late], blocks, part)
        if len(blocks) > 1:
            own_grad, parts = grads[0], grads[1:]
        else:
            own_grad = grads[0][:, :rows]
            parts = [grads[0][:, i * rows:(i + 1) * rows].astype(BF) for i in range(1, n_far)]
        arrived = [send(part, along(k)) for part, k in zip(parts, steps)]

        queries_late, keys_late, values_late = lax.optimization_barrier(
            (queries, key_tokens, value_tokens, own_grad)
        )[:3]
        mixed = attention(queries_late, keys_late, values_late)

        updated = step(own_weights, own_grad, arrived)
        updated, mixed, query_normed = lax.optimization_barrier((updated, mixed, query_normed))
        stepped = [updated] + [send(updated, layer(-o[0], -o[1])) for o in offsets]
        line_queries = [first_query] + [send(query_normed, along(k)) for k in steps[1:]]
        stepped_there = [send(block, swap) for block in [after(updated, line_queries[-1]), *stepped[1:]]]

        outs = apply_rows(line_queries + [query_normed], joined(stepped + stepped_there))
        back = [send(part, along(k)) for part, k in zip(outs[:-1], steps)]
        return call(total_kernel, [struct(queries.shape, BF)], outs[-1], mixed, *back, name="total")[0]

    in_specs = (
        P(("grp", "dev"), None),
        P(("grp", "dev"), None),
        P(("grp", "dev"), None),
        P(("grp", "dev")),
        P(None, ("grp", "dev"), None),
    )
    out_specs = P(("grp", "dev"), None)
    return jax.shard_map(body, mesh=mesh, in_specs=in_specs, out_specs=out_specs, check_vma=False)
```

```python
import jax
import jax.numpy as jnp
from jax import lax
from jax.experimental import pallas as pl
from jax.experimental.pallas import tpu as pltpu
from jax.sharding import PartitionSpec as P

D = 768
HEADS = 12
HEAD_DIM = 64
CORES = 2
NEAR = 2
BF = jnp.bfloat16
F32 = jnp.float32

epsilon = 1e-06
AXES = ("grp", "dev")


def moves(mesh):
    n_grp, n_dev = mesh.shape["grp"], mesh.shape["dev"]
    n_gx, n_far = n_grp // CORES, n_dev // NEAR

    def build(target):
        pairs = []
        for gx in range(n_gx):
            for core in range(CORES):
                for far in range(n_far):
                    for near in range(NEAR):
                        to = target(gx, core, far, near)
                        source = (gx * CORES + core) * n_dev + far * NEAR + near
                        dest = (to[0] * CORES + to[1]) * n_dev + to[2] * NEAR + to[3]
                        pairs.append((source, dest))
        return pairs

    def along(step):
        return build(lambda gx, core, far, near: (gx, core, far ^ step, near))

    def layer(dx, dn):
        return build(lambda gx, core, far, near: (gx ^ dx, core, far, near ^ dn))

    swap = build(lambda gx, core, far, near: (gx, 1 - core, far, near))
    return n_far, along, layer, swap


def send(array, pairs):
    return lax.ppermute(array, AXES, pairs)


def after(value, *others):
    return lax.optimization_barrier((value, *others))[0]


def call(kernel, outs, *args, flops=0, scratch=(), in_hbm=(), limit=32 * 1024 * 1024, name=None):
    vmem = pl.BlockSpec(memory_space=pltpu.VMEM)
    size = sum(a.size * a.dtype.itemsize for a in args) + sum(o.size * o.dtype.itemsize for o in outs)
    result = pl.pallas_call(
        kernel,
        out_shape=list(outs),
        in_specs=[pl.BlockSpec(memory_space=pltpu.HBM) if i in in_hbm else vmem for i in range(len(args))],
        out_specs=[vmem] * len(outs),
        scratch_shapes=list(scratch),
        compiler_params=pltpu.CompilerParams(vmem_limit_bytes=limit),
        cost_estimate=pl.CostEstimate(flops=flops, bytes_accessed=size, transcendentals=0),
        name=name,
    )(*args)
    return result


def struct(shape, dtype):
    return jax.ShapeDtypeStruct(shape, dtype)


def nt(a, b):
    return lax.dot_general(a, b, (((1,), (1,)), ((), ())), preferred_element_type=F32)


def nn(a, b):
    return lax.dot_general(a, b, (((1,), (0,)), ((), ())), preferred_element_type=F32)


def rms(matrix):
    return matrix / jnp.sqrt(jnp.mean(matrix * matrix, axis=-1, keepdims=True) + epsilon)


def prep_kernel(key_hbm, value_hbm, query_hbm, rate_hbm, pair_ref, query_out, key_ref, value_ref, query_ref, rate_ref, sems):
    count = key_ref.shape[0]
    sources = (key_hbm, rate_hbm, value_hbm, query_hbm)
    targets = (key_ref, rate_ref, value_ref, query_ref)
    copies = [pltpu.make_async_copy(a, b, sems.at[i]) for i, (a, b) in enumerate(zip(sources, targets))]
    for copy in copies:
        copy.start()
    copies[0].wait()
    pair_ref[0] = rms(key_ref[...].astype(F32)).astype(BF)
    copies[1].wait()
    copies[2].wait()
    spread = jnp.broadcast_to(rate_ref[...], (count, count))
    row = lax.broadcasted_iota(jnp.int32, (count, count), 0)
    col = lax.broadcasted_iota(jnp.int32, (count, count), 1)
    rate = jnp.sum(jnp.where(row == col, spread, 0.0), axis=1, keepdims=True)
    pair_ref[1] = (-(rate * value_ref[...].astype(F32))).astype(BF)
    copies[3].wait()
    query_out[...] = rms(query_ref[...].astype(F32)).astype(BF)


def prep(key_tokens, value_tokens, queries, token_rate):
    count = key_tokens.shape[0]
    return call(
        prep_kernel,
        [struct((2, count, D), BF), struct((count, D), BF)],
        key_tokens, value_tokens, queries, token_rate.reshape(1, count),
        scratch=[pltpu.VMEM((count, D), BF)] * 3 + [pltpu.VMEM((1, count), F32), pltpu.SemaphoreType.DMA((4,))],
        in_hbm=(0, 1, 2, 3),
        limit=62 * 1024 * 1024,
        name="prep",
    )


def cut(rows):
    return 16 * ((3 * rows + 31) // 32)


def pieces(rows):
    edge = cut(rows)
    found = []
    for m in range(3):
        for low, high, chunk in ((0, edge, 0), (edge, 3 * rows, 1)):
            first, last = max(low, m * rows), min(high, (m + 1) * rows)
            if first < last:
                found.append((m, first - m * rows, last - first, chunk, first - low))
    return found


def stage(*arrays):
    def kernel(*refs):
        for source, target in zip(refs[:len(arrays)], refs[len(arrays):]):
            target[...] = source[...]

    return call(kernel, [struct(a.shape, a.dtype) for a in arrays], *arrays, name="stage")


def gradient(tokens, blocks, before=None):
    flat = [array for token in tokens for array in token]
    places, at = [], 0
    for token in tokens:
        places.append(((at, 0), (at, 1)) if len(token) == 1 else ((at, None), (at + 1, None)))
        at += len(token)
    count = flat[0].shape[-2]
    number, rows = len(blocks), blocks[0].shape[1]
    aligned = rows % 16 == 0
    if not aligned:
        blocks = [jnp.concatenate(blocks, axis=1)]
    size = blocks[0].shape[1]
    units = number * rows
    given = before is not None

    def kernel(*refs):
        token_refs = refs[:len(flat)]
        block_refs = refs[len(flat):len(flat) + len(blocks)]
        weights = refs[-1]
        total = refs[-2]
        if given:
            base = refs[len(flat) + len(blocks)]
        for i, ref in enumerate(block_refs):
            for m in range(3):
                weights[m * units + i * size:m * units + (i + 1) * size] = ref[m]

        def read(place):
            ref, part = token_refs[place[0]], place[1]
            return ref[...] if part is None else ref[part]

        for j in range(0, len(tokens), 2):
            keys = jnp.concatenate([read(place[0]) for place in places[j:j + 2]], axis=0)
            signal = jnp.concatenate([read(place[1]) for place in places[j:j + 2]], axis=0)
            acts = nt(weights[:2 * units], keys)
            gate_act, up_act = acts[:units], acts[units:]
            sg = jax.nn.sigmoid(gate_act)
            silu = gate_act * sg
            hidden = (silu * up_act).astype(BF)
            hidden_grad = nt(weights[2 * units:], signal)
            gate_grad = (hidden_grad * up_act * sg * (1.0 + gate_act * (1.0 - sg))).astype(BF)
            up_grad = (hidden_grad * silu).astype(BF)
            first = nn(jnp.concatenate([gate_grad, up_grad], axis=0), keys)
            last = nn(hidden, signal)
            if j or given:
                source = total if j else base
                first, last = source[:2 * units] + first, source[2 * units:] + last
            total[:2 * units] = first
            total[2 * units:] = last
        if given and aligned:
            out_refs = refs[len(flat) + len(blocks) + 1:-2]
            for m, row, span, chunk, place in pieces(rows):
                for k in range(number):
                    source = total[m * units + k * rows + row:m * units + k * rows + row + span]
                    out = out_refs[2 * chunk + (k + 1) % 2]
                    out[k // 2, place:place + span] = source.astype(out.dtype)

    edges = (cut(rows), 3 * rows - cut(rows))
    scratch = [pltpu.VMEM((3 * units, D), BF)]
    outs = [struct((3 * units, D), F32)]
    if given and aligned:
        scratch = [pltpu.VMEM((3 * units, D), F32), *scratch]
        outs = [struct((number // 2, edge, D), kind) for edge in edges for kind in (BF, F32)]
    outs = call(
        kernel, outs, *flat, *blocks, *([before] if given else []),
        flops=12 * count * len(tokens) * units * D,
        scratch=scratch,
        name="gradient" if given else "gradient_part",
    )
    if not given:
        return outs[0]
    if aligned:
        return outs[:2], outs[2:]
    total = outs[0].reshape(3, number, rows, D).swapaxes(0, 1).reshape(number, 3 * rows, D)
    parts = total[:, :edges[0]], total[:, edges[0]:]
    return [(part[1::2].astype(BF), part[::2]) for part in parts]


def fold(keep, arrived):
    number, rows = keep.shape[:2]

    def kernel(keep_ref, arrived_ref, send_ref, kept_ref):
        for k in range(number):
            total = keep_ref[k] + arrived_ref[k].astype(F32)
            out = send_ref if k % 2 else kept_ref
            out[k // 2] = total.astype(out.dtype)

    shape = (number // 2, rows, D)
    return call(kernel, [struct(shape, BF), struct(shape, F32)], keep, arrived, name="fold")


def step(old, keep, arrived):
    def kernel(old_ref, keep_ref, arrived_ref, out_ref):
        old_rows = old_ref[...].astype(F32)
        stepped = old_rows - (keep_ref[0] + arrived_ref[0].astype(F32))
        out_ref[...] = (
            stepped
            * jnp.sqrt(jnp.mean(old_rows * old_rows, axis=-1, keepdims=True) + epsilon)
            / jnp.sqrt(jnp.mean(stepped * stepped, axis=-1, keepdims=True) + epsilon)
        ).astype(BF)

    return call(kernel, [struct(old.shape, BF)], old, keep, arrived, name="step")[0]


def attention_kernel(query_ref, key_ref, value_ref, out_ref):
    count = key_ref.shape[0]
    width = 2 * HEAD_DIM
    low = lax.broadcasted_iota(jnp.int32, (count, width), 1) < HEAD_DIM
    zero = jnp.zeros((count, width), BF)
    for h in range(HEADS // 2):
        cols = slice(h * width, (h + 1) * width)
        query, key, value = query_ref[:, cols], key_ref[:, cols], value_ref[:, cols]
        probs = []
        for keep in (low, ~low):
            scores = nt(query, jnp.where(keep, key, zero)) * HEAD_DIM ** (-0.5)
            weights = jnp.exp(scores - jnp.max(scores, axis=-1, keepdims=True))
            probs.append((weights / jnp.sum(weights, axis=-1, keepdims=True)).astype(BF))
        values = jnp.concatenate([jnp.where(low, value, zero), jnp.where(low, zero, value)], axis=0)
        out_ref[:, cols] = nn(jnp.concatenate(probs, axis=1), values)


def attention(queries, key_tokens, value_tokens):
    return call(
        attention_kernel, [struct(queries.shape, F32)], queries, key_tokens, value_tokens,
        flops=4 * queries.shape[0] * key_tokens.shape[0] * D, name="attention",
    )[0]


def apply_rows(queries, blocks, rows):
    count = queries[0].shape[0]
    number = len(blocks)
    aligned = rows % 16 == 0
    if not aligned:
        whole = [jnp.concatenate(chunks, axis=0).reshape(3, rows, D) for chunks in blocks]
        blocks = [[jnp.concatenate(whole, axis=1).reshape(3 * number * rows, D)]]
    chunks = [chunk for block in blocks for chunk in block]
    units = number * rows

    def kernel(*refs):
        query_refs = refs[:len(queries)]
        chunk_refs = list(refs[len(queries):len(queries) + len(chunks)])
        out_refs = refs[len(queries) + len(chunks):-1]
        weights = refs[-1]
        if aligned:
            for i, block in enumerate(blocks):
                own_refs = [chunk_refs.pop(0) for _ in block]
                for m, row, size, chunk, place in pieces(rows):
                    start = m * units + i * rows + row
                    if len(block) == 1:
                        weights[start:start + size] = own_refs[0][m * rows + row:m * rows + row + size]
                    else:
                        weights[start:start + size] = own_refs[chunk][place:place + size]
        else:
            weights[...] = chunk_refs[0][...]
        stacked = jnp.concatenate([ref[...] for ref in query_refs], axis=0)
        gate_act = nt(stacked, weights[:units])
        up_act = nt(stacked, weights[units:2 * units])
        hidden = (jax.nn.silu(gate_act) * up_act).astype(BF)
        result = nn(hidden, weights[2 * units:])
        for i, out in enumerate(out_refs):
            out[...] = result[i * count:(i + 1) * count].astype(out.dtype)

    outs = [struct((count, D), BF) for _ in queries[:-1]] + [struct((count, D), F32)]
    return call(
        kernel, outs, *queries, *chunks,
        flops=6 * count * len(queries) * units * D,
        scratch=[pltpu.VMEM((3 * units, D), BF)],
        name="apply",
    )


def total_kernel(*refs):
    result = refs[0][...] + refs[1][...]
    for ref in refs[2:-1]:
        result = result + ref[...].astype(F32)
    refs[-1][...] = result.astype(BF)


def solution(mesh):
    n_far, along, layer, swap = moves(mesh)
    bits = [1 << i for i in range(n_far.bit_length() - 1)]

    def line_gather(block):
        blocks = {0: block}
        for bit in reversed(bits):
            for k in list(blocks):
                blocks[k ^ bit] = send(blocks[k], along(bit))
        return blocks

    def body(key_tokens, value_tokens, queries, token_rate, fast_weights):
        rows = fast_weights.shape[1]
        pair, query_normed = prep(key_tokens, value_tokens, queries, token_rate)
        at_x, at_y = send(pair, layer(1, 0)), send(pair, layer(0, 1))
        own_there = send(pair, swap)
        line = line_gather(fast_weights)
        own_weights, own_pair = stage(after(fast_weights, line[n_far - 1]), pair)
        corner = (send(at_x[0], layer(0, 1)), send(at_y[1], layer(1, 0)))
        tokens = [(own_pair,), (at_x,), (at_y,)]
        tokens += [(own_there,), (send(after(at_x, at_y, own_there), swap),), (send(after(at_y, at_x), swap),)]
        blocks = [own_weights] + [line[k] for k in range(1, n_far)]
        part = gradient(tokens, blocks)
        late = [corner, tuple(send(array, swap) for array in corner)]
        chunks = gradient(late, blocks, part)

        query_normed = after(query_normed, chunks[0][0])
        all_queries = [send(query_normed, layer(*o)) for o in ((1, 0), (0, 1))]
        mixed = attention(queries, key_tokens, value_tokens)

        flat = own_weights.reshape(3 * rows, D)
        olds = flat[:cut(rows)], flat[cut(rows):]
        stepped = []
        for old, (part, keep) in zip(olds, chunks):
            for bit in bits[:-1]:
                arrived = send(part, along(bit))
                if stepped:
                    keep = after(keep, *all_queries)
                part, keep = fold(keep, arrived)
            updated = step(old, keep, send(part, along(bits[-1])))
            stepped.append(line_gather(updated))
        corner_query = send(after(query_normed, updated), layer(1, 1))
        blocks = [[chunk[k] for chunk in stepped] for k in range(n_far)]
        there = [[send(array, swap) for array in block] for block in blocks[:-1]]
        there.append([send(after(array, corner_query), swap) for array in blocks[-1]])
        blocks += there

        outs = apply_rows(all_queries + [corner_query, query_normed], blocks, rows)
        back = [send(part, layer(*o)) for part, o in zip(outs[:-1], ((1, 0), (0, 1), (1, 1)))]
        return call(total_kernel, [struct(queries.shape, BF)], outs[-1], mixed, *back, name="total")[0]

    in_specs = (
        P(("grp", "dev"), None),
        P(("grp", "dev"), None),
        P(("grp", "dev"), None),
        P(("grp", "dev")),
        P(None, ("grp", "dev"), None),
    )
    out_specs = P(("grp", "dev"), None)
    return jax.shard_map(body, mesh=mesh, in_specs=in_specs, out_specs=out_specs, check_vma=False)
```

```python
import jax
import jax.numpy as jnp
from jax import lax
from jax.experimental import pallas as pl
from jax.experimental.pallas import tpu as pltpu
from jax.sharding import PartitionSpec as P

D = 768
HEADS = 12
HEAD_DIM = 64
CORES = 2
NEAR = 2
BF = jnp.bfloat16
F32 = jnp.float32

epsilon = 1e-06
AXES = ("grp", "dev")


def moves(mesh):
    n_grp, n_dev = mesh.shape["grp"], mesh.shape["dev"]
    n_gx, n_far = n_grp // CORES, n_dev // NEAR

    def build(target):
        pairs = []
        for gx in range(n_gx):
            for core in range(CORES):
                for far in range(n_far):
                    for near in range(NEAR):
                        to = target(gx, core, far, near)
                        source = (gx * CORES + core) * n_dev + far * NEAR + near
                        dest = (to[0] * CORES + to[1]) * n_dev + to[2] * NEAR + to[3]
                        pairs.append((source, dest))
        return pairs

    def along(step):
        return build(lambda gx, core, far, near: (gx, core, far ^ step, near))

    def layer(dx, dn):
        return build(lambda gx, core, far, near: (gx ^ dx, core, far, near ^ dn))

    swap = build(lambda gx, core, far, near: (gx, 1 - core, far, near))
    return n_far, along, layer, swap


def send(array, pairs):
    return lax.ppermute(array, AXES, pairs)


def after(value, *others):
    return lax.optimization_barrier((value, *others))[0]


def call(kernel, outs, *args, flops=0, scratch=(), in_hbm=(), limit=32 * 1024 * 1024, name=None):
    vmem = pl.BlockSpec(memory_space=pltpu.VMEM)
    size = sum(a.size * a.dtype.itemsize for a in args) + sum(o.size * o.dtype.itemsize for o in outs)
    result = pl.pallas_call(
        kernel,
        out_shape=list(outs),
        in_specs=[pl.BlockSpec(memory_space=pltpu.HBM) if i in in_hbm else vmem for i in range(len(args))],
        out_specs=[vmem] * len(outs),
        scratch_shapes=list(scratch),
        compiler_params=pltpu.CompilerParams(vmem_limit_bytes=limit),
        cost_estimate=pl.CostEstimate(flops=flops, bytes_accessed=size, transcendentals=0),
        name=name,
    )(*args)
    return result


def struct(shape, dtype):
    return jax.ShapeDtypeStruct(shape, dtype)


def nt(a, b):
    return lax.dot_general(a, b, (((1,), (1,)), ((), ())), preferred_element_type=F32)


def nn(a, b):
    return lax.dot_general(a, b, (((1,), (0,)), ((), ())), preferred_element_type=F32)


def rms(matrix):
    return matrix / jnp.sqrt(jnp.mean(matrix * matrix, axis=-1, keepdims=True) + epsilon)


def prep_kernel(key_hbm, value_hbm, query_hbm, rate_hbm, pair_ref, query_out, key_ref, value_ref, query_ref, rate_ref, sems):
    count = key_ref.shape[0]
    sources = (key_hbm, rate_hbm, value_hbm, query_hbm)
    targets = (key_ref, rate_ref, value_ref, query_ref)
    copies = [pltpu.make_async_copy(a, b, sems.at[i]) for i, (a, b) in enumerate(zip(sources, targets))]
    for copy in copies:
        copy.start()
    copies[0].wait()
    pair_ref[0] = rms(key_ref[...].astype(F32)).astype(BF)
    copies[1].wait()
    copies[2].wait()
    spread = jnp.broadcast_to(rate_ref[...], (count, count))
    row = lax.broadcasted_iota(jnp.int32, (count, count), 0)
    col = lax.broadcasted_iota(jnp.int32, (count, count), 1)
    rate = jnp.sum(jnp.where(row == col, spread, 0.0), axis=1, keepdims=True)
    pair_ref[1] = (-(rate * value_ref[...].astype(F32))).astype(BF)
    copies[3].wait()
    query_out[...] = rms(query_ref[...].astype(F32)).astype(BF)


def prep(key_tokens, value_tokens, queries, token_rate):
    count = key_tokens.shape[0]
    return call(
        prep_kernel,
        [struct((2, count, D), BF), struct((count, D), BF)],
        key_tokens, value_tokens, queries, token_rate.reshape(1, count),
        scratch=[pltpu.VMEM((count, D), BF)] * 3 + [pltpu.VMEM((1, count), F32), pltpu.SemaphoreType.DMA((4,))],
        in_hbm=(0, 1, 2, 3),
        limit=62 * 1024 * 1024,
        name="prep",
    )


def cut(rows):
    return 16 * ((3 * rows + 31) // 32)


def pieces(rows):
    edge = cut(rows)
    found = []
    for m in range(3):
        for low, high, chunk in ((0, edge, 0), (edge, 3 * rows, 1)):
            first, last = max(low, m * rows), min(high, (m + 1) * rows)
            if first < last:
                found.append((m, first - m * rows, last - first, chunk, first - low))
    return found


def stage(*arrays):
    def kernel(*refs):
        for source, target in zip(refs[:len(arrays)], refs[len(arrays):]):
            target[...] = source[...]

    return call(kernel, [struct(a.shape, a.dtype) for a in arrays], *arrays, name="stage")


def gradient(tokens, blocks, before=None):
    flat = [array for token in tokens for array in token]
    places, at = [], 0
    for token in tokens:
        places.append(((at, 0), (at, 1)) if len(token) == 1 else ((at, None), (at + 1, None)))
        at += len(token)
    count = flat[0].shape[-2]
    number, rows = len(blocks), blocks[0].shape[1]
    aligned = rows % 16 == 0
    if not aligned:
        blocks = [jnp.concatenate(blocks, axis=1)]
    size = blocks[0].shape[1]
    units = number * rows
    given = before is not None

    def kernel(*refs):
        token_refs = refs[:len(flat)]
        block_refs = refs[len(flat):len(flat) + len(blocks)]
        weights = refs[-1]
        total = refs[-2]
        if given:
            base = refs[len(flat) + len(blocks)]
        for i, ref in enumerate(block_refs):
            for m in range(3):
                weights[m * units + i * size:m * units + (i + 1) * size] = ref[m]

        def read(place):
            ref, part = token_refs[place[0]], place[1]
            return ref[...] if part is None else ref[part]

        for j in range(0, len(tokens), 2):
            keys = jnp.concatenate([read(place[0]) for place in places[j:j + 2]], axis=0)
            signal = jnp.concatenate([read(place[1]) for place in places[j:j + 2]], axis=0)
            acts = nt(weights[:2 * units], keys)
            gate_act, up_act = acts[:units], acts[units:]
            sg = jax.nn.sigmoid(gate_act)
            silu = gate_act * sg
            hidden = (silu * up_act).astype(BF)
            hidden_grad = nt(weights[2 * units:], signal)
            gate_grad = (hidden_grad * up_act * sg * (1.0 + gate_act * (1.0 - sg))).astype(BF)
            up_grad = (hidden_grad * silu).astype(BF)
            first = nn(jnp.concatenate([gate_grad, up_grad], axis=0), keys)
            last = nn(hidden, signal)
            if j or given:
                source = total if j else base
                first, last = source[:2 * units] + first, source[2 * units:] + last
            total[:2 * units] = first
            total[2 * units:] = last
        if given and aligned:
            out_refs = refs[len(flat) + len(blocks) + 1:-2]
            for m, row, span, chunk, place in pieces(rows):
                for k in range(number):
                    source = total[m * units + k * rows + row:m * units + k * rows + row + span]
                    out = out_refs[2 * chunk + (k + 1) % 2]
                    out[k // 2, place:place + span] = source.astype(out.dtype)

    edges = (cut(rows), 3 * rows - cut(rows))
    scratch = [pltpu.VMEM((3 * units, D), BF)]
    outs = [struct((3 * units, D), F32)]
    if given and aligned:
        scratch = [pltpu.VMEM((3 * units, D), F32), *scratch]
        outs = [struct((number // 2, edge, D), kind) for edge in edges for kind in (BF, F32)]
    outs = call(
        kernel, outs, *flat, *blocks, *([before] if given else []),
        flops=12 * count * len(tokens) * units * D,
        scratch=scratch,
        name="gradient" if given else "gradient_part",
    )
    if not given:
        return outs[0]
    if aligned:
        return outs[:2], outs[2:]
    total = outs[0].reshape(3, number, rows, D).swapaxes(0, 1).reshape(number, 3 * rows, D)
    parts = total[:, :edges[0]], total[:, edges[0]:]
    return [(part[1::2].astype(BF), part[::2]) for part in parts]


def fold(keep, arrived):
    number, rows = keep.shape[:2]

    def kernel(keep_ref, arrived_ref, send_ref, kept_ref):
        for k in range(number):
            total = keep_ref[k] + arrived_ref[k].astype(F32)
            out = send_ref if k % 2 else kept_ref
            out[k // 2] = total.astype(out.dtype)

    shape = (number // 2, rows, D)
    return call(kernel, [struct(shape, BF), struct(shape, F32)], keep, arrived, name="fold")


def step(old, keep, arrived):
    def kernel(old_ref, keep_ref, arrived_ref, out_ref):
        old_rows = old_ref[...].astype(F32)
        stepped = old_rows - (keep_ref[0] + arrived_ref[0].astype(F32))
        out_ref[...] = (
            stepped
            * jnp.sqrt(jnp.mean(old_rows * old_rows, axis=-1, keepdims=True) + epsilon)
            / jnp.sqrt(jnp.mean(stepped * stepped, axis=-1, keepdims=True) + epsilon)
        ).astype(BF)

    return call(kernel, [struct(old.shape, BF)], old, keep, arrived, name="step")[0]


def attention_kernel(query_ref, key_ref, value_ref, out_ref):
    count = key_ref.shape[0]
    width = 2 * HEAD_DIM
    low = lax.broadcasted_iota(jnp.int32, (count, width), 1) < HEAD_DIM
    zero = jnp.zeros((count, width), BF)
    for h in range(HEADS // 2):
        cols = slice(h * width, (h + 1) * width)
        query, key, value = query_ref[:, cols], key_ref[:, cols], value_ref[:, cols]
        probs = []
        for keep in (low, ~low):
            scores = nt(query, jnp.where(keep, key, zero)) * HEAD_DIM ** (-0.5)
            weights = jnp.exp(scores - jnp.max(scores, axis=-1, keepdims=True))
            probs.append((weights / jnp.sum(weights, axis=-1, keepdims=True)).astype(BF))
        values = jnp.concatenate([jnp.where(low, value, zero), jnp.where(low, zero, value)], axis=0)
        out_ref[:, cols] = nn(jnp.concatenate(probs, axis=1), values)


def attention(queries, key_tokens, value_tokens):
    return call(
        attention_kernel, [struct(queries.shape, F32)], queries, key_tokens, value_tokens,
        flops=4 * queries.shape[0] * key_tokens.shape[0] * D, name="attention",
    )[0]


def apply_rows(queries, blocks, rows):
    count = queries[0].shape[0]
    number = len(blocks)
    aligned = rows % 16 == 0
    if not aligned:
        whole = [jnp.concatenate(chunks, axis=0).reshape(3, rows, D) for chunks in blocks]
        blocks = [[jnp.concatenate(whole, axis=1).reshape(3 * number * rows, D)]]
    chunks = [chunk for block in blocks for chunk in block]
    units = number * rows

    def kernel(*refs):
        query_refs = refs[:len(queries)]
        chunk_refs = list(refs[len(queries):len(queries) + len(chunks)])
        out_refs = refs[len(queries) + len(chunks):-1]
        weights = refs[-1]
        if aligned:
            for i, block in enumerate(blocks):
                own_refs = [chunk_refs.pop(0) for _ in block]
                for m, row, size, chunk, place in pieces(rows):
                    start = m * units + i * rows + row
                    if len(block) == 1:
                        weights[start:start + size] = own_refs[0][m * rows + row:m * rows + row + size]
                    else:
                        weights[start:start + size] = own_refs[chunk][place:place + size]
        else:
            weights[...] = chunk_refs[0][...]
        stacked = jnp.concatenate([ref[...] for ref in query_refs], axis=0)
        gate_act = nt(stacked, weights[:units])
        up_act = nt(stacked, weights[units:2 * units])
        hidden = (jax.nn.silu(gate_act) * up_act).astype(BF)
        result = nn(hidden, weights[2 * units:])
        for i, out in enumerate(out_refs):
            out[...] = result[i * count:(i + 1) * count].astype(out.dtype)

    outs = [struct((count, D), BF) for _ in queries[:-1]] + [struct((count, D), F32)]
    return call(
        kernel, outs, *queries, *chunks,
        flops=6 * count * len(queries) * units * D,
        scratch=[pltpu.VMEM((3 * units, D), BF)],
        name="apply",
    )


def total_kernel(*refs):
    result = refs[0][...] + refs[1][...]
    for ref in refs[2:-1]:
        result = result + ref[...].astype(F32)
    refs[-1][...] = result.astype(BF)


def solution(mesh):
    n_far, along, layer, swap = moves(mesh)
    bits = [1 << i for i in range(n_far.bit_length() - 1)]

    def line_gather(block):
        blocks = {0: block}
        for bit in reversed(bits):
            for k in list(blocks):
                blocks[k ^ bit] = send(blocks[k], along(bit))
        return blocks

    def body(key_tokens, value_tokens, queries, token_rate, fast_weights):
        rows = fast_weights.shape[1]
        pair, query_normed = prep(key_tokens, value_tokens, queries, token_rate)
        at_x, at_y, corner = [send(pair, layer(*o)) for o in ((1, 0), (0, 1), (1, 1))]
        line = line_gather(fast_weights)
        own_weights, own_pair = stage(after(fast_weights, line[bits[-1]]), pair)
        own_there = send(after(own_pair, at_x, *[line[k] for k in range(1, n_far)]), swap)
        blocks = [own_weights] + [line[k] for k in range(1, n_far)]
        tokens = [own_pair, own_there, at_y, at_x, send(at_y, swap), send(at_x, swap)]
        part = gradient([(token,) for token in tokens], blocks)
        chunks = gradient([(corner,), (send(corner, swap),)], blocks, part)

        query_normed = after(query_normed, chunks[0][0])
        all_queries = [send(query_normed, layer(*o)) for o in ((1, 0), (0, 1))]
        mixed = attention(queries, key_tokens, value_tokens)

        flat = own_weights.reshape(3 * rows, D)
        olds = flat[:cut(rows)], flat[cut(rows):]
        stepped = []
        for old, (part, keep) in zip(olds, chunks):
            for bit in bits[:-1]:
                arrived = send(part, along(bit))
                if stepped:
                    keep = after(keep, *all_queries)
                part, keep = fold(keep, arrived)
            updated = step(old, keep, send(part, along(bits[-1])))
            stepped.append(line_gather(updated))
        corner_query = send(after(query_normed, updated), layer(1, 1))
        blocks = [[chunk[k] for chunk in stepped] for k in range(n_far)]
        there = [[send(array, swap) for array in block] for block in blocks[:-1]]
        there.append([send(after(array, corner_query), swap) for array in blocks[-1]])
        blocks += there

        outs = apply_rows(all_queries + [corner_query, query_normed], blocks, rows)
        back = [send(part, layer(*o)) for part, o in zip(outs[:-1], ((1, 0), (0, 1), (1, 1)))]
        return call(total_kernel, [struct(queries.shape, BF)], outs[-1], mixed, *back, name="total")[0]

    in_specs = (
        P(("grp", "dev"), None),
        P(("grp", "dev"), None),
        P(("grp", "dev"), None),
        P(("grp", "dev")),
        P(None, ("grp", "dev"), None),
    )
    out_specs = P(("grp", "dev"), None)
    return jax.shard_map(body, mesh=mesh, in_specs=in_specs, out_specs=out_specs, check_vma=False)
```

```python
import jax
import jax.numpy as jnp
from jax import lax
from jax.experimental import pallas as pl
from jax.experimental.pallas import tpu as pltpu
from jax.sharding import PartitionSpec as P

D = 768
HEADS = 12
HEAD_DIM = 64
CORES = 2
NEAR = 2
BF = jnp.bfloat16
F32 = jnp.float32

epsilon = 1e-06
AXES = ("grp", "dev")


def moves(mesh):
    n_grp, n_dev = mesh.shape["grp"], mesh.shape["dev"]
    n_gx, n_far = n_grp // CORES, n_dev // NEAR

    def build(target):
        pairs = []
        for gx in range(n_gx):
            for core in range(CORES):
                for far in range(n_far):
                    for near in range(NEAR):
                        to = target(gx, core, far, near)
                        source = (gx * CORES + core) * n_dev + far * NEAR + near
                        dest = (to[0] * CORES + to[1]) * n_dev + to[2] * NEAR + to[3]
                        pairs.append((source, dest))
        return pairs

    def along(step):
        return build(lambda gx, core, far, near: (gx, core, far ^ step, near))

    def layer(dx, dn):
        return build(lambda gx, core, far, near: (gx ^ dx, core, far, near ^ dn))

    swap = build(lambda gx, core, far, near: (gx, 1 - core, far, near))
    return n_far, along, layer, swap


def send(array, pairs):
    return lax.ppermute(array, AXES, pairs)


def after(value, *others):
    return lax.optimization_barrier((value, *others))[0]


def call(kernel, outs, *args, flops=0, scratch=(), in_hbm=(), limit=32 * 1024 * 1024, name=None):
    vmem = pl.BlockSpec(memory_space=pltpu.VMEM)
    size = sum(a.size * a.dtype.itemsize for a in args) + sum(o.size * o.dtype.itemsize for o in outs)
    result = pl.pallas_call(
        kernel,
        out_shape=list(outs),
        in_specs=[pl.BlockSpec(memory_space=pltpu.HBM) if i in in_hbm else vmem for i in range(len(args))],
        out_specs=[vmem] * len(outs),
        scratch_shapes=list(scratch),
        compiler_params=pltpu.CompilerParams(vmem_limit_bytes=limit),
        cost_estimate=pl.CostEstimate(flops=flops, bytes_accessed=size, transcendentals=0),
        name=name,
    )(*args)
    return result


def struct(shape, dtype):
    return jax.ShapeDtypeStruct(shape, dtype)


def nt(a, b):
    return lax.dot_general(a, b, (((1,), (1,)), ((), ())), preferred_element_type=F32)


def nn(a, b):
    return lax.dot_general(a, b, (((1,), (0,)), ((), ())), preferred_element_type=F32)


def rms(matrix):
    return matrix / jnp.sqrt(jnp.mean(matrix * matrix, axis=-1, keepdims=True) + epsilon)


def prep_kernel(key_hbm, value_hbm, query_hbm, rate_hbm, pair_ref, query_out, key_ref, value_ref, query_ref, rate_ref, sems):
    count = key_ref.shape[0]
    sources = (key_hbm, rate_hbm, value_hbm, query_hbm)
    targets = (key_ref, rate_ref, value_ref, query_ref)
    copies = [pltpu.make_async_copy(a, b, sems.at[i]) for i, (a, b) in enumerate(zip(sources, targets))]
    for copy in copies:
        copy.start()
    copies[0].wait()
    pair_ref[0] = rms(key_ref[...].astype(F32)).astype(BF)
    copies[1].wait()
    copies[2].wait()
    spread = jnp.broadcast_to(rate_ref[...], (count, count))
    row = lax.broadcasted_iota(jnp.int32, (count, count), 0)
    col = lax.broadcasted_iota(jnp.int32, (count, count), 1)
    rate = jnp.sum(jnp.where(row == col, spread, 0.0), axis=1, keepdims=True)
    pair_ref[1] = (-(rate * value_ref[...].astype(F32))).astype(BF)
    copies[3].wait()
    query_out[...] = rms(query_ref[...].astype(F32)).astype(BF)


def prep(key_tokens, value_tokens, queries, token_rate):
    count = key_tokens.shape[0]
    return call(
        prep_kernel,
        [struct((2, count, D), BF), struct((count, D), BF)],
        key_tokens, value_tokens, queries, token_rate.reshape(1, count),
        scratch=[pltpu.VMEM((count, D), BF)] * 3 + [pltpu.VMEM((1, count), F32), pltpu.SemaphoreType.DMA((4,))],
        in_hbm=(0, 1, 2, 3),
        limit=62 * 1024 * 1024,
        name="prep",
    )


def cut(rows):
    return 16 * ((3 * rows + 31) // 32)


def pieces(rows):
    edge = cut(rows)
    found = []
    for m in range(3):
        for low, high, chunk in ((0, edge, 0), (edge, 3 * rows, 1)):
            first, last = max(low, m * rows), min(high, (m + 1) * rows)
            if first < last:
                found.append((m, first - m * rows, last - first, chunk, first - low))
    return found


def stage(*arrays):
    def kernel(*refs):
        for source, target in zip(refs[:len(arrays)], refs[len(arrays):]):
            target[...] = source[...]

    return call(kernel, [struct(a.shape, a.dtype) for a in arrays], *arrays, name="stage")


def gradient(tokens, blocks, before=None):
    flat = [array for token in tokens for array in token]
    places, at = [], 0
    for token in tokens:
        places.append(((at, 0), (at, 1)) if len(token) == 1 else ((at, None), (at + 1, None)))
        at += len(token)
    count = flat[0].shape[-2]
    number, rows = len(blocks), blocks[0].shape[1]
    aligned = rows % 16 == 0
    if not aligned:
        blocks = [jnp.concatenate(blocks, axis=1)]
    size = blocks[0].shape[1]
    units = number * rows
    given = before is not None

    def kernel(*refs):
        token_refs = refs[:len(flat)]
        block_refs = refs[len(flat):len(flat) + len(blocks)]
        weights = refs[-1]
        total = refs[-2]
        if given:
            base = refs[len(flat) + len(blocks)]
        for i, ref in enumerate(block_refs):
            for m in range(3):
                weights[m * units + i * size:m * units + (i + 1) * size] = ref[m]

        def read(place):
            ref, part = token_refs[place[0]], place[1]
            return ref[...] if part is None else ref[part]

        for j in range(0, len(tokens), 2):
            keys = jnp.concatenate([read(place[0]) for place in places[j:j + 2]], axis=0)
            signal = jnp.concatenate([read(place[1]) for place in places[j:j + 2]], axis=0)
            acts = nt(weights[:2 * units], keys)
            gate_act, up_act = acts[:units], acts[units:]
            sg = jax.nn.sigmoid(gate_act)
            silu = gate_act * sg
            hidden = (silu * up_act).astype(BF)
            hidden_grad = nt(weights[2 * units:], signal)
            gate_grad = (hidden_grad * up_act * sg * (1.0 + gate_act * (1.0 - sg))).astype(BF)
            up_grad = (hidden_grad * silu).astype(BF)
            first = nn(jnp.concatenate([gate_grad, up_grad], axis=0), keys)
            last = nn(hidden, signal)
            if j or given:
                source = total if j else base
                first, last = source[:2 * units] + first, source[2 * units:] + last
            total[:2 * units] = first
            total[2 * units:] = last
        if given and aligned:
            out_refs = refs[len(flat) + len(blocks) + 1:-2]
            for m, row, span, chunk, place in pieces(rows):
                for k in range(number):
                    source = total[m * units + k * rows + row:m * units + k * rows + row + span]
                    out = out_refs[2 * chunk + (k + 1) % 2]
                    out[k // 2, place:place + span] = source.astype(out.dtype)

    edges = (cut(rows), 3 * rows - cut(rows))
    scratch = [pltpu.VMEM((3 * units, D), BF)]
    outs = [struct((3 * units, D), F32)]
    if given and aligned:
        scratch = [pltpu.VMEM((3 * units, D), F32), *scratch]
        outs = [struct((number // 2, edge, D), kind) for edge in edges for kind in (BF, F32)]
    outs = call(
        kernel, outs, *flat, *blocks, *([before] if given else []),
        flops=12 * count * len(tokens) * units * D,
        scratch=scratch,
        name="gradient" if given else "gradient_part",
    )
    if not given:
        return outs[0]
    if aligned:
        return outs[:2], outs[2:]
    total = outs[0].reshape(3, number, rows, D).swapaxes(0, 1).reshape(number, 3 * rows, D)
    parts = total[:, :edges[0]], total[:, edges[0]:]
    return [(part[1::2].astype(BF), part[::2]) for part in parts]


def fold(keep, arrived):
    number, rows = keep.shape[:2]

    def kernel(keep_ref, arrived_ref, send_ref, kept_ref):
        for k in range(number):
            total = keep_ref[k] + arrived_ref[k].astype(F32)
            out = send_ref if k % 2 else kept_ref
            out[k // 2] = total.astype(out.dtype)

    shape = (number // 2, rows, D)
    return call(kernel, [struct(shape, BF), struct(shape, F32)], keep, arrived, name="fold")


def step(old, keep, arrived):
    def kernel(old_ref, keep_ref, arrived_ref, out_ref):
        old_rows = old_ref[...].astype(F32)
        stepped = old_rows - (keep_ref[0] + arrived_ref[0].astype(F32))
        out_ref[...] = (
            stepped
            * jnp.sqrt(jnp.mean(old_rows * old_rows, axis=-1, keepdims=True) + epsilon)
            / jnp.sqrt(jnp.mean(stepped * stepped, axis=-1, keepdims=True) + epsilon)
        ).astype(BF)

    return call(kernel, [struct(old.shape, BF)], old, keep, arrived, name="step")[0]


def attention_kernel(query_ref, key_ref, value_ref, out_ref):
    count = key_ref.shape[0]
    width = 2 * HEAD_DIM
    low = lax.broadcasted_iota(jnp.int32, (count, width), 1) < HEAD_DIM
    zero = jnp.zeros((count, width), BF)
    for h in range(HEADS // 2):
        cols = slice(h * width, (h + 1) * width)
        query, key, value = query_ref[:, cols], key_ref[:, cols], value_ref[:, cols]
        probs = []
        for keep in (low, ~low):
            scores = nt(query, jnp.where(keep, key, zero)) * HEAD_DIM ** (-0.5)
            weights = jnp.exp(scores - jnp.max(scores, axis=-1, keepdims=True))
            probs.append((weights / jnp.sum(weights, axis=-1, keepdims=True)).astype(BF))
        values = jnp.concatenate([jnp.where(low, value, zero), jnp.where(low, zero, value)], axis=0)
        out_ref[:, cols] = nn(jnp.concatenate(probs, axis=1), values)


def attention(queries, key_tokens, value_tokens):
    return call(
        attention_kernel, [struct(queries.shape, F32)], queries, key_tokens, value_tokens,
        flops=4 * queries.shape[0] * key_tokens.shape[0] * D, name="attention",
    )[0]


def apply_rows(queries, blocks, rows):
    count = queries[0].shape[0]
    number = len(blocks)
    aligned = rows % 16 == 0
    if not aligned:
        whole = [jnp.concatenate(chunks, axis=0).reshape(3, rows, D) for chunks in blocks]
        blocks = [[jnp.concatenate(whole, axis=1).reshape(3 * number * rows, D)]]
    chunks = [chunk for block in blocks for chunk in block]
    units = number * rows

    def kernel(*refs):
        query_refs = refs[:len(queries)]
        chunk_refs = list(refs[len(queries):len(queries) + len(chunks)])
        out_refs = refs[len(queries) + len(chunks):-1]
        weights = refs[-1]
        if aligned:
            for i, block in enumerate(blocks):
                own_refs = [chunk_refs.pop(0) for _ in block]
                for m, row, size, chunk, place in pieces(rows):
                    start = m * units + i * rows + row
                    if len(block) == 1:
                        weights[start:start + size] = own_refs[0][m * rows + row:m * rows + row + size]
                    else:
                        weights[start:start + size] = own_refs[chunk][place:place + size]
        else:
            weights[...] = chunk_refs[0][...]
        stacked = jnp.concatenate([ref[...] for ref in query_refs], axis=0)
        gate_act = nt(stacked, weights[:units])
        up_act = nt(stacked, weights[units:2 * units])
        hidden = (jax.nn.silu(gate_act) * up_act).astype(BF)
        result = nn(hidden, weights[2 * units:])
        for i, out in enumerate(out_refs):
            out[...] = result[i * count:(i + 1) * count].astype(out.dtype)

    outs = [struct((count, D), BF) for _ in queries[:-1]] + [struct((count, D), F32)]
    return call(
        kernel, outs, *queries, *chunks,
        flops=6 * count * len(queries) * units * D,
        scratch=[pltpu.VMEM((3 * units, D), BF)],
        name="apply",
    )


def total_kernel(*refs):
    result = refs[0][...] + refs[1][...]
    for ref in refs[2:-1]:
        result = result + ref[...].astype(F32)
    refs[-1][...] = result.astype(BF)


def solution(mesh):
    n_far, along, layer, swap = moves(mesh)
    bits = [1 << i for i in range(n_far.bit_length() - 1)]

    def line_gather(block, near_first=False):
        blocks = {0: block}
        for bit in reversed(bits):
            for k in list(blocks):
                source = after(blocks[k], blocks[1]) if near_first and k and bit == 1 else blocks[k]
                blocks[k ^ bit] = send(source, along(bit))
        return blocks

    def body(key_tokens, value_tokens, queries, token_rate, fast_weights):
        rows = fast_weights.shape[1]
        pair, query_normed = prep(key_tokens, value_tokens, queries, token_rate)
        at_x, at_y, corner = [send(pair, layer(*o)) for o in ((1, 0), (0, 1), (1, 1))]
        line = line_gather(fast_weights)
        own_weights, own_pair = stage(after(fast_weights, line[bits[-1]]), pair)
        own_there = send(after(own_pair, at_x, *[line[k] for k in range(1, n_far)]), swap)
        blocks = [own_weights] + [line[k] for k in range(1, n_far)]
        tokens = [own_pair, own_there, at_y, at_x, send(at_y, swap), send(at_x, swap)]
        part = gradient([(token,) for token in tokens], blocks)
        chunks = gradient([(corner,), (send(corner, swap),)], blocks, part)

        query_normed = after(query_normed, chunks[0][0])
        all_queries = [send(query_normed, layer(*o)) for o in ((1, 0), (0, 1))]
        mixed = attention(queries, key_tokens, value_tokens)

        flat = own_weights.reshape(3 * rows, D)
        olds = flat[:cut(rows)], flat[cut(rows):]
        stepped = []
        for old, (part, keep) in zip(olds, chunks):
            for bit in bits[:-1]:
                arrived = send(part, along(bit))
                if stepped:
                    keep = after(keep, *all_queries)
                part, keep = fold(keep, arrived)
            updated = step(old, keep, send(part, along(bits[-1])))
            stepped.append(line_gather(updated, near_first=not stepped))
        corner_query = send(after(query_normed, all_queries[0]), layer(1, 1))
        blocks = [[chunk[k] for chunk in stepped] for k in range(n_far)]
        there = [[send(array, swap) for array in block] for block in blocks[:-1]]
        there.append([send(after(array, corner_query), swap) for array in blocks[-1]])
        blocks += there

        outs = apply_rows(all_queries + [corner_query, query_normed], blocks, rows)
        back = [send(part, layer(*o)) for part, o in zip(outs[:-1], ((1, 0), (0, 1), (1, 1)))]
        return call(total_kernel, [struct(queries.shape, BF)], outs[-1], mixed, *back, name="total")[0]

    in_specs = (
        P(("grp", "dev"), None),
        P(("grp", "dev"), None),
        P(("grp", "dev"), None),
        P(("grp", "dev")),
        P(None, ("grp", "dev"), None),
    )
    out_specs = P(("grp", "dev"), None)
    return jax.shard_map(body, mesh=mesh, in_specs=in_specs, out_specs=out_specs, check_vma=False)
```

```python
import jax
import jax.numpy as jnp
from jax import lax
from jax.experimental import pallas as pl
from jax.experimental.pallas import tpu as pltpu
from jax.sharding import PartitionSpec as P

D = 768
HEADS = 12
HEAD_DIM = 64
CORES = 2
NEAR = 2
BF = jnp.bfloat16
F32 = jnp.float32

epsilon = 1e-06
AXES = ("grp", "dev")


def moves(mesh):
    n_grp, n_dev = mesh.shape["grp"], mesh.shape["dev"]
    n_gx, n_far = n_grp // CORES, n_dev // NEAR

    def build(target):
        pairs = []
        for gx in range(n_gx):
            for core in range(CORES):
                for far in range(n_far):
                    for near in range(NEAR):
                        to = target(gx, core, far, near)
                        source = (gx * CORES + core) * n_dev + far * NEAR + near
                        dest = (to[0] * CORES + to[1]) * n_dev + to[2] * NEAR + to[3]
                        pairs.append((source, dest))
        return pairs

    def along(step):
        return build(lambda gx, core, far, near: (gx, core, far ^ step, near))

    def layer(dx, dn):
        return build(lambda gx, core, far, near: (gx ^ dx, core, far, near ^ dn))

    swap = build(lambda gx, core, far, near: (gx, 1 - core, far, near))
    return n_far, along, layer, swap


def send(array, pairs):
    return lax.ppermute(array, AXES, pairs)


def after(value, *others):
    return lax.optimization_barrier((value, *others))[0]


def call(kernel, outs, *args, flops=0, scratch=(), in_hbm=(), limit=32 * 1024 * 1024, name=None):
    vmem = pl.BlockSpec(memory_space=pltpu.VMEM)
    size = sum(a.size * a.dtype.itemsize for a in args) + sum(o.size * o.dtype.itemsize for o in outs)
    result = pl.pallas_call(
        kernel,
        out_shape=list(outs),
        in_specs=[pl.BlockSpec(memory_space=pltpu.HBM) if i in in_hbm else vmem for i in range(len(args))],
        out_specs=[vmem] * len(outs),
        scratch_shapes=list(scratch),
        compiler_params=pltpu.CompilerParams(vmem_limit_bytes=limit),
        cost_estimate=pl.CostEstimate(flops=flops, bytes_accessed=size, transcendentals=0),
        name=name,
    )(*args)
    return result


def struct(shape, dtype):
    return jax.ShapeDtypeStruct(shape, dtype)


def nt(a, b):
    return lax.dot_general(a, b, (((1,), (1,)), ((), ())), preferred_element_type=F32)


def nn(a, b):
    return lax.dot_general(a, b, (((1,), (0,)), ((), ())), preferred_element_type=F32)


def rms(matrix):
    return matrix / jnp.sqrt(jnp.mean(matrix * matrix, axis=-1, keepdims=True) + epsilon)


def prep_kernel(key_hbm, value_hbm, query_hbm, rate_hbm, pair_ref, query_out, key_ref, value_ref, query_ref, rate_ref, sems):
    count = key_ref.shape[0]
    sources = (key_hbm, rate_hbm, value_hbm, query_hbm)
    targets = (key_ref, rate_ref, value_ref, query_ref)
    copies = [pltpu.make_async_copy(a, b, sems.at[i]) for i, (a, b) in enumerate(zip(sources, targets))]
    for copy in copies:
        copy.start()
    copies[0].wait()
    pair_ref[0] = rms(key_ref[...].astype(F32)).astype(BF)
    copies[1].wait()
    copies[2].wait()
    spread = jnp.broadcast_to(rate_ref[...], (count, count))
    row = lax.broadcasted_iota(jnp.int32, (count, count), 0)
    col = lax.broadcasted_iota(jnp.int32, (count, count), 1)
    rate = jnp.sum(jnp.where(row == col, spread, 0.0), axis=1, keepdims=True)
    pair_ref[1] = (-(rate * value_ref[...].astype(F32))).astype(BF)
    copies[3].wait()
    query_out[...] = rms(query_ref[...].astype(F32)).astype(BF)


def prep(key_tokens, value_tokens, queries, token_rate):
    count = key_tokens.shape[0]
    return call(
        prep_kernel,
        [struct((2, count, D), BF), struct((count, D), BF)],
        key_tokens, value_tokens, queries, token_rate.reshape(1, count),
        scratch=[pltpu.VMEM((count, D), BF)] * 3 + [pltpu.VMEM((1, count), F32), pltpu.SemaphoreType.DMA((4,))],
        in_hbm=(0, 1, 2, 3),
        limit=62 * 1024 * 1024,
        name="prep",
    )


def cut(rows):
    return 16 * ((3 * rows + 31) // 32)


def pieces(rows):
    edge = cut(rows)
    found = []
    for m in range(3):
        for low, high, chunk in ((0, edge, 0), (edge, 3 * rows, 1)):
            first, last = max(low, m * rows), min(high, (m + 1) * rows)
            if first < last:
                found.append((m, first - m * rows, last - first, chunk, first - low))
    return found


def stage(*arrays):
    def kernel(*refs):
        for source, target in zip(refs[:len(arrays)], refs[len(arrays):]):
            target[...] = source[...]

    return call(kernel, [struct(a.shape, a.dtype) for a in arrays], *arrays, name="stage")


def gradient(tokens, blocks, before=None):
    flat = [array for token in tokens for array in token]
    places, at = [], 0
    for token in tokens:
        places.append(((at, 0), (at, 1)) if len(token) == 1 else ((at, None), (at + 1, None)))
        at += len(token)
    count = flat[0].shape[-2]
    number, rows = len(blocks), blocks[0].shape[1]
    aligned = rows % 16 == 0
    if not aligned:
        blocks = [jnp.concatenate(blocks, axis=1)]
    size = blocks[0].shape[1]
    units = number * rows
    given = before is not None

    def kernel(*refs):
        token_refs = refs[:len(flat)]
        block_refs = refs[len(flat):len(flat) + len(blocks)]
        weights = refs[-1]
        total = refs[-2]
        if given:
            base = refs[len(flat) + len(blocks)]
        for i, ref in enumerate(block_refs):
            for m in range(3):
                weights[m * units + i * size:m * units + (i + 1) * size] = ref[m]

        def read(place):
            ref, part = token_refs[place[0]], place[1]
            return ref[...] if part is None else ref[part]

        for j in range(0, len(tokens), 2):
            keys = jnp.concatenate([read(place[0]) for place in places[j:j + 2]], axis=0)
            signal = jnp.concatenate([read(place[1]) for place in places[j:j + 2]], axis=0)
            acts = nt(weights[:2 * units], keys)
            gate_act, up_act = acts[:units], acts[units:]
            sg = jax.nn.sigmoid(gate_act)
            silu = gate_act * sg
            hidden = (silu * up_act).astype(BF)
            hidden_grad = nt(weights[2 * units:], signal)
            gate_grad = (hidden_grad * up_act * sg * (1.0 + gate_act * (1.0 - sg))).astype(BF)
            up_grad = (hidden_grad * silu).astype(BF)
            first = nn(jnp.concatenate([gate_grad, up_grad], axis=0), keys)
            last = nn(hidden, signal)
            if j or given:
                source = total if j else base
                first, last = source[:2 * units] + first, source[2 * units:] + last
            total[:2 * units] = first
            total[2 * units:] = last
        if given and aligned:
            out_refs = refs[len(flat) + len(blocks) + 1:-2]
            for m, row, span, chunk, place in pieces(rows):
                for k in range(number):
                    source = total[m * units + k * rows + row:m * units + k * rows + row + span]
                    out = out_refs[2 * chunk + (k + 1) % 2]
                    out[k // 2, place:place + span] = source.astype(out.dtype)

    edges = (cut(rows), 3 * rows - cut(rows))
    scratch = [pltpu.VMEM((3 * units, D), BF)]
    outs = [struct((3 * units, D), F32)]
    if given and aligned:
        scratch = [pltpu.VMEM((3 * units, D), F32), *scratch]
        outs = [struct((number // 2, edge, D), kind) for edge in edges for kind in (BF, F32)]
    outs = call(
        kernel, outs, *flat, *blocks, *([before] if given else []),
        flops=12 * count * len(tokens) * units * D,
        scratch=scratch,
        name="gradient" if given else "gradient_part",
    )
    if not given:
        return outs[0]
    if aligned:
        return outs[:2], outs[2:]
    total = outs[0].reshape(3, number, rows, D).swapaxes(0, 1).reshape(number, 3 * rows, D)
    parts = total[:, :edges[0]], total[:, edges[0]:]
    return [(part[1::2].astype(BF), part[::2]) for part in parts]


def fold(keep, arrived):
    number, rows = keep.shape[:2]

    def kernel(keep_ref, arrived_ref, send_ref, kept_ref):
        for k in range(number):
            total = keep_ref[k] + arrived_ref[k].astype(F32)
            out = send_ref if k % 2 else kept_ref
            out[k // 2] = total.astype(out.dtype)

    shape = (number // 2, rows, D)
    return call(kernel, [struct(shape, BF), struct(shape, F32)], keep, arrived, name="fold")


def step(old, keep, arrived):
    def kernel(old_ref, keep_ref, arrived_ref, out_ref):
        old_rows = old_ref[...].astype(F32)
        stepped = old_rows - (keep_ref[0] + arrived_ref[0].astype(F32))
        out_ref[...] = (
            stepped
            * jnp.sqrt(jnp.mean(old_rows * old_rows, axis=-1, keepdims=True) + epsilon)
            / jnp.sqrt(jnp.mean(stepped * stepped, axis=-1, keepdims=True) + epsilon)
        ).astype(BF)

    return call(kernel, [struct(old.shape, BF)], old, keep, arrived, name="step")[0]


def attention_kernel(query_ref, key_ref, value_ref, out_ref):
    count = key_ref.shape[0]
    width = 2 * HEAD_DIM
    low = lax.broadcasted_iota(jnp.int32, (count, width), 1) < HEAD_DIM
    zero = jnp.zeros((count, width), BF)
    for h in range(HEADS // 2):
        cols = slice(h * width, (h + 1) * width)
        query, key, value = query_ref[:, cols], key_ref[:, cols], value_ref[:, cols]
        probs = []
        for keep in (low, ~low):
            scores = nt(query, jnp.where(keep, key, zero)) * HEAD_DIM ** (-0.5)
            weights = jnp.exp(scores - jnp.max(scores, axis=-1, keepdims=True))
            probs.append((weights / jnp.sum(weights, axis=-1, keepdims=True)).astype(BF))
        values = jnp.concatenate([jnp.where(low, value, zero), jnp.where(low, zero, value)], axis=0)
        out_ref[:, cols] = nn(jnp.concatenate(probs, axis=1), values)


def attention(queries, key_tokens, value_tokens):
    return call(
        attention_kernel, [struct(queries.shape, F32)], queries, key_tokens, value_tokens,
        flops=4 * queries.shape[0] * key_tokens.shape[0] * D, name="attention",
    )[0]


def apply_rows(queries, blocks, rows):
    count = queries[0].shape[0]
    number = len(blocks)
    aligned = rows % 16 == 0
    if not aligned:
        whole = [jnp.concatenate(chunks, axis=0).reshape(3, rows, D) for chunks in blocks]
        blocks = [[jnp.concatenate(whole, axis=1).reshape(3 * number * rows, D)]]
    chunks = [chunk for block in blocks for chunk in block]
    units = number * rows

    def kernel(*refs):
        query_refs = refs[:len(queries)]
        chunk_refs = list(refs[len(queries):len(queries) + len(chunks)])
        out_refs = refs[len(queries) + len(chunks):-1]
        weights = refs[-1]
        if aligned:
            for i, block in enumerate(blocks):
                own_refs = [chunk_refs.pop(0) for _ in block]
                for m, row, size, chunk, place in pieces(rows):
                    start = m * units + i * rows + row
                    if len(block) == 1:
                        weights[start:start + size] = own_refs[0][m * rows + row:m * rows + row + size]
                    else:
                        weights[start:start + size] = own_refs[chunk][place:place + size]
        else:
            weights[...] = chunk_refs[0][...]
        stacked = jnp.concatenate([ref[...] for ref in query_refs], axis=0)
        gate_act = nt(stacked, weights[:units])
        up_act = nt(stacked, weights[units:2 * units])
        hidden = (jax.nn.silu(gate_act) * up_act).astype(BF)
        result = nn(hidden, weights[2 * units:])
        for i, out in enumerate(out_refs):
            out[...] = result[i * count:(i + 1) * count].astype(out.dtype)

    outs = [struct((count, D), BF) for _ in queries[:-1]] + [struct((count, D), F32)]
    return call(
        kernel, outs, *queries, *chunks,
        flops=6 * count * len(queries) * units * D,
        scratch=[pltpu.VMEM((3 * units, D), BF)],
        name="apply",
    )


def total_kernel(*refs):
    result = refs[0][...] + refs[1][...]
    for ref in refs[2:-1]:
        result = result + ref[...].astype(F32)
    refs[-1][...] = result.astype(BF)


def solution(mesh):
    n_far, along, layer, swap = moves(mesh)
    bits = [1 << i for i in range(n_far.bit_length() - 1)]

    def line_gather(block, near_first=False):
        blocks = {0: block}
        for bit in reversed(bits):
            for k in list(blocks):
                source = after(blocks[k], blocks[1]) if near_first and k and bit == 1 else blocks[k]
                blocks[k ^ bit] = send(source, along(bit))
        return blocks

    def body(key_tokens, value_tokens, queries, token_rate, fast_weights):
        rows = fast_weights.shape[1]
        pair, query_normed = prep(key_tokens, value_tokens, queries, token_rate)
        at_x, at_y, corner = [send(pair, layer(*o)) for o in ((1, 0), (0, 1), (1, 1))]
        line = line_gather(fast_weights)
        own_weights, own_pair = stage(after(fast_weights, line[bits[-1]]), pair)
        own_there = send(after(own_pair, at_x, *[line[k] for k in range(1, n_far)]), swap)
        blocks = [own_weights] + [line[k] for k in range(1, n_far)]
        tokens = [own_pair, own_there, at_y, at_x, send(at_y, swap), send(at_x, swap)]
        part = gradient([(token,) for token in tokens], blocks)
        chunks = gradient([(corner,), (send(corner, swap),)], blocks, part)

        query_normed = after(query_normed, chunks[0][0])
        all_queries = [send(query_normed, layer(*o)) for o in ((1, 0), (0, 1))]
        mixed = attention(queries, key_tokens, value_tokens)

        flat = own_weights.reshape(3 * rows, D)
        olds = flat[:cut(rows)], flat[cut(rows):]
        stepped = []
        for old, (part, keep) in zip(olds, chunks):
            for bit in bits[:-1]:
                arrived = send(part, along(bit))
                part, keep = fold(keep, arrived)
            updated = step(old, keep, send(part, along(bits[-1])))
            stepped.append(line_gather(updated, near_first=not stepped))
        corner_query = send(after(query_normed, *all_queries), layer(1, 1))
        blocks = [[chunk[k] for chunk in stepped] for k in range(n_far)]
        there = [[send(array, swap) for array in block] for block in blocks[:-1]]
        there.append([send(after(array, corner_query), swap) for array in blocks[-1]])
        blocks += there

        outs = apply_rows([corner_query, *all_queries, query_normed], blocks, rows)
        back = [send(part, layer(*o)) for part, o in zip(outs[:-1], ((1, 1), (1, 0), (0, 1)))]
        return call(total_kernel, [struct(queries.shape, BF)], outs[-1], mixed, *back, name="total")[0]

    in_specs = (
        P(("grp", "dev"), None),
        P(("grp", "dev"), None),
        P(("grp", "dev"), None),
        P(("grp", "dev")),
        P(None, ("grp", "dev"), None),
    )
    out_specs = P(("grp", "dev"), None)
    return jax.shard_map(body, mesh=mesh, in_specs=in_specs, out_specs=out_specs, check_vma=False)
```

```python
import jax
import jax.numpy as jnp
from jax import lax
from jax.experimental import pallas as pl
from jax.experimental.pallas import tpu as pltpu
from jax.sharding import PartitionSpec as P

D = 768
HEADS = 12
HEAD_DIM = 64
CORES = 2
NEAR = 2
BF = jnp.bfloat16
F32 = jnp.float32

epsilon = 1e-06
AXES = ("grp", "dev")


def moves(mesh):
    n_grp, n_dev = mesh.shape["grp"], mesh.shape["dev"]
    n_gx, n_far = n_grp // CORES, n_dev // NEAR

    def build(target):
        pairs = []
        for gx in range(n_gx):
            for core in range(CORES):
                for far in range(n_far):
                    for near in range(NEAR):
                        to = target(gx, core, far, near)
                        source = (gx * CORES + core) * n_dev + far * NEAR + near
                        dest = (to[0] * CORES + to[1]) * n_dev + to[2] * NEAR + to[3]
                        pairs.append((source, dest))
        return pairs

    def along(step):
        return build(lambda gx, core, far, near: (gx, core, far ^ step, near))

    def layer(dx, dn):
        return build(lambda gx, core, far, near: (gx ^ dx, core, far, near ^ dn))

    swap = build(lambda gx, core, far, near: (gx, 1 - core, far, near))
    return n_far, along, layer, swap


def send(array, pairs):
    return lax.ppermute(array, AXES, pairs)


def after(value, *others):
    return lax.optimization_barrier((value, *others))[0]


def call(kernel, outs, *args, flops=0, scratch=(), in_hbm=(), limit=32 * 1024 * 1024, name=None):
    vmem = pl.BlockSpec(memory_space=pltpu.VMEM)
    size = sum(a.size * a.dtype.itemsize for a in args) + sum(o.size * o.dtype.itemsize for o in outs)
    result = pl.pallas_call(
        kernel,
        out_shape=list(outs),
        in_specs=[pl.BlockSpec(memory_space=pltpu.HBM) if i in in_hbm else vmem for i in range(len(args))],
        out_specs=[vmem] * len(outs),
        scratch_shapes=list(scratch),
        compiler_params=pltpu.CompilerParams(vmem_limit_bytes=limit),
        cost_estimate=pl.CostEstimate(flops=flops, bytes_accessed=size, transcendentals=0),
        name=name,
    )(*args)
    return result


def struct(shape, dtype):
    return jax.ShapeDtypeStruct(shape, dtype)


def nt(a, b):
    return lax.dot_general(a, b, (((1,), (1,)), ((), ())), preferred_element_type=F32)


def nn(a, b):
    return lax.dot_general(a, b, (((1,), (0,)), ((), ())), preferred_element_type=F32)


def rms(matrix):
    return matrix / jnp.sqrt(jnp.mean(matrix * matrix, axis=-1, keepdims=True) + epsilon)


def prep_kernel(key_hbm, value_hbm, rate_hbm, pair_ref, key_ref, value_ref, rate_ref, sems):
    count = key_ref.shape[0]
    sources = (key_hbm, rate_hbm, value_hbm)
    targets = (key_ref, rate_ref, value_ref)
    copies = [pltpu.make_async_copy(a, b, sems.at[i]) for i, (a, b) in enumerate(zip(sources, targets))]
    for copy in copies:
        copy.start()
    copies[0].wait()
    pair_ref[0] = rms(key_ref[...].astype(F32)).astype(BF)
    copies[1].wait()
    copies[2].wait()
    spread = jnp.broadcast_to(rate_ref[...], (count, count))
    row = lax.broadcasted_iota(jnp.int32, (count, count), 0)
    col = lax.broadcasted_iota(jnp.int32, (count, count), 1)
    rate = jnp.sum(jnp.where(row == col, spread, 0.0), axis=1, keepdims=True)
    pair_ref[1] = (-(rate * value_ref[...].astype(F32))).astype(BF)


def prep(key_tokens, value_tokens, token_rate):
    count = key_tokens.shape[0]
    return call(
        prep_kernel,
        [struct((2, count, D), BF)],
        key_tokens, value_tokens, token_rate.reshape(1, count),
        scratch=[pltpu.VMEM((count, D), BF)] * 2 + [pltpu.VMEM((1, count), F32), pltpu.SemaphoreType.DMA((3,))],
        in_hbm=(0, 1, 2),
        limit=62 * 1024 * 1024,
        name="prep",
    )[0]


def cut(rows):
    return 16 * ((3 * rows + 31) // 32)


def pieces(rows):
    edge = cut(rows)
    found = []
    for m in range(3):
        for low, high, chunk in ((0, edge, 0), (edge, 3 * rows, 1)):
            first, last = max(low, m * rows), min(high, (m + 1) * rows)
            if first < last:
                found.append((m, first - m * rows, last - first, chunk, first - low))
    return found


def stage(weights, pair, queries):
    def kernel(weights_ref, pair_ref, query_ref, weights_out, pair_out, query_out):
        weights_out[...] = weights_ref[...]
        pair_out[...] = pair_ref[...]
        query_out[...] = rms(query_ref[...].astype(F32)).astype(BF)

    return call(kernel, [struct(a.shape, BF) for a in (weights, pair, queries)], weights, pair, queries, name="stage")


def gradient(tokens, blocks, before=None):
    flat = [array for token in tokens for array in token]
    places, at = [], 0
    for token in tokens:
        places.append(((at, 0), (at, 1)) if len(token) == 1 else ((at, None), (at + 1, None)))
        at += len(token)
    count = flat[0].shape[-2]
    number, rows = len(blocks), blocks[0].shape[1]
    aligned = rows % 16 == 0
    if not aligned:
        blocks = [jnp.concatenate(blocks, axis=1)]
    size = blocks[0].shape[1]
    units = number * rows
    given = before is not None

    def kernel(*refs):
        token_refs = refs[:len(flat)]
        block_refs = refs[len(flat):len(flat) + len(blocks)]
        weights = refs[-1]
        total = refs[-2]
        if given:
            base = refs[len(flat) + len(blocks)]
        for i, ref in enumerate(block_refs):
            for m in range(3):
                weights[m * units + i * size:m * units + (i + 1) * size] = ref[m]

        def read(place):
            ref, part = token_refs[place[0]], place[1]
            return ref[...] if part is None else ref[part]

        for j in range(0, len(tokens), 2):
            keys = jnp.concatenate([read(place[0]) for place in places[j:j + 2]], axis=0)
            signal = jnp.concatenate([read(place[1]) for place in places[j:j + 2]], axis=0)
            acts = nt(weights[:2 * units], keys)
            gate_act, up_act = acts[:units], acts[units:]
            sg = jax.nn.sigmoid(gate_act)
            silu = gate_act * sg
            hidden = (silu * up_act).astype(BF)
            hidden_grad = nt(weights[2 * units:], signal)
            gate_grad = (hidden_grad * up_act * sg * (1.0 + gate_act * (1.0 - sg))).astype(BF)
            up_grad = (hidden_grad * silu).astype(BF)
            first = nn(jnp.concatenate([gate_grad, up_grad], axis=0), keys)
            last = nn(hidden, signal)
            if j or given:
                source = total if j else base
                first, last = source[:2 * units] + first, source[2 * units:] + last
            total[:2 * units] = first
            total[2 * units:] = last
        if given and aligned:
            out_refs = refs[len(flat) + len(blocks) + 1:-2]
            for m, row, span, chunk, place in pieces(rows):
                for k in range(number):
                    source = total[m * units + k * rows + row:m * units + k * rows + row + span]
                    out = out_refs[2 * chunk + (k + 1) % 2]
                    out[k // 2, place:place + span] = source.astype(out.dtype)

    edges = (cut(rows), 3 * rows - cut(rows))
    scratch = [pltpu.VMEM((3 * units, D), BF)]
    outs = [struct((3 * units, D), F32)]
    if given and aligned:
        scratch = [pltpu.VMEM((3 * units, D), F32), *scratch]
        outs = [struct((number // 2, edge, D), kind) for edge in edges for kind in (BF, F32)]
    outs = call(
        kernel, outs, *flat, *blocks, *([before] if given else []),
        flops=12 * count * len(tokens) * units * D,
        scratch=scratch,
        name="gradient" if given else "gradient_part",
    )
    if not given:
        return outs[0]
    if aligned:
        return outs[:2], outs[2:]
    total = outs[0].reshape(3, number, rows, D).swapaxes(0, 1).reshape(number, 3 * rows, D)
    parts = total[:, :edges[0]], total[:, edges[0]:]
    return [(part[1::2].astype(BF), part[::2]) for part in parts]


def fold(keep, arrived):
    number, rows = keep.shape[:2]

    def kernel(keep_ref, arrived_ref, send_ref, kept_ref):
        for k in range(number):
            total = keep_ref[k] + arrived_ref[k].astype(F32)
            out = send_ref if k % 2 else kept_ref
            out[k // 2] = total.astype(out.dtype)

    shape = (number // 2, rows, D)
    return call(kernel, [struct(shape, BF), struct(shape, F32)], keep, arrived, name="fold")


def step(old, keep, arrived):
    def kernel(old_ref, keep_ref, arrived_ref, out_ref):
        old_rows = old_ref[...].astype(F32)
        stepped = old_rows - (keep_ref[0] + arrived_ref[0].astype(F32))
        out_ref[...] = (
            stepped
            * jnp.sqrt(jnp.mean(old_rows * old_rows, axis=-1, keepdims=True) + epsilon)
            / jnp.sqrt(jnp.mean(stepped * stepped, axis=-1, keepdims=True) + epsilon)
        ).astype(BF)

    return call(kernel, [struct(old.shape, BF)], old, keep, arrived, name="step")[0]


def attention_kernel(query_ref, key_ref, value_ref, out_ref):
    count = key_ref.shape[0]
    width = 2 * HEAD_DIM
    low = lax.broadcasted_iota(jnp.int32, (count, width), 1) < HEAD_DIM
    zero = jnp.zeros((count, width), BF)
    for h in range(HEADS // 2):
        cols = slice(h * width, (h + 1) * width)
        query, key, value = query_ref[:, cols], key_ref[:, cols], value_ref[:, cols]
        probs = []
        for keep in (low, ~low):
            scores = nt(query, jnp.where(keep, key, zero)) * HEAD_DIM ** (-0.5)
            weights = jnp.exp(scores - jnp.max(scores, axis=-1, keepdims=True))
            probs.append((weights / jnp.sum(weights, axis=-1, keepdims=True)).astype(BF))
        values = jnp.concatenate([jnp.where(low, value, zero), jnp.where(low, zero, value)], axis=0)
        out_ref[:, cols] = nn(jnp.concatenate(probs, axis=1), values)


def attention(queries, key_tokens, value_tokens):
    return call(
        attention_kernel, [struct(queries.shape, F32)], queries, key_tokens, value_tokens,
        flops=4 * queries.shape[0] * key_tokens.shape[0] * D, name="attention",
    )[0]


def apply_rows(queries, blocks, rows, last):
    count = queries[0].shape[0]
    number = len(blocks)
    aligned = rows % 16 == 0
    if not aligned:
        whole = [jnp.concatenate(chunks, axis=0).reshape(3, rows, D) for chunks in blocks]
        blocks = [[jnp.concatenate(whole, axis=1).reshape(3 * number * rows, D)]]
    chunks = [chunk for block in blocks for chunk in block]
    units = number * rows

    def kernel(*refs):
        query_refs = refs[:len(queries)]
        chunk_refs = list(refs[len(queries):len(queries) + len(chunks)])
        out_refs = refs[len(queries) + len(chunks):-1]
        weights = refs[-1]
        if aligned:
            for i, block in enumerate(blocks):
                own_refs = [chunk_refs.pop(0) for _ in block]
                for m, row, size, chunk, place in pieces(rows):
                    start = m * units + i * rows + row
                    if len(block) == 1:
                        weights[start:start + size] = own_refs[0][m * rows + row:m * rows + row + size]
                    else:
                        weights[start:start + size] = own_refs[chunk][place:place + size]
        else:
            weights[...] = chunk_refs[0][...]
        stacked = jnp.concatenate([ref[...] for ref in query_refs], axis=0)
        gate_act = nt(stacked, weights[:units])
        up_act = nt(stacked, weights[units:2 * units])
        hidden = (jax.nn.silu(gate_act) * up_act).astype(BF)
        result = nn(hidden, weights[2 * units:])
        for i, out in enumerate(out_refs):
            out[...] = result[i * count:(i + 1) * count].astype(out.dtype)

    outs = [struct((count, D), BF) for _ in queries[:-1]] + [struct((count, D), last)]
    return call(
        kernel, outs, *queries, *chunks,
        flops=6 * count * len(queries) * units * D,
        scratch=[pltpu.VMEM((3 * units, D), BF)],
        name="apply",
    )


def total_kernel(*refs):
    result = refs[0][...] + refs[1][...]
    for ref in refs[2:-1]:
        result = result + ref[...].astype(F32)
    refs[-1][...] = result.astype(BF)


def solution(mesh):
    n_far, along, layer, swap = moves(mesh)
    bits = [1 << i for i in range(n_far.bit_length() - 1)]

    def line_gather(block, near_first=False):
        blocks = {0: block}
        for bit in reversed(bits):
            for k in list(blocks):
                source = after(blocks[k], blocks[1]) if near_first and k and bit == 1 else blocks[k]
                blocks[k ^ bit] = send(source, along(bit))
        return blocks

    def body(key_tokens, value_tokens, queries, token_rate, fast_weights):
        rows = fast_weights.shape[1]
        pair = prep(key_tokens, value_tokens, token_rate)
        at_x, at_y, corner = [send(pair, layer(*o)) for o in ((1, 0), (0, 1), (1, 1))]
        line = line_gather(fast_weights)
        own_weights, own_pair, query_normed = stage(after(fast_weights, line[bits[-1]]), pair, queries)
        own_there = send(after(own_pair, at_x, *[line[k] for k in range(1, n_far)]), swap)
        blocks = [own_weights] + [line[k] for k in range(1, n_far)]
        tokens = [own_pair, own_there, at_y, at_x, send(at_y, swap), send(at_x, swap)]
        part = gradient([(token,) for token in tokens], blocks)
        chunks = gradient([(corner,), (send(corner, swap),)], blocks, part)

        query_normed = after(query_normed, chunks[0][0])
        all_queries = [send(query_normed, layer(*o)) for o in ((1, 0), (0, 1))]
        mixed = attention(queries, key_tokens, value_tokens)

        flat = own_weights.reshape(3 * rows, D)
        olds = flat[:cut(rows)], flat[cut(rows):]
        stepped = []
        for old, (part, keep) in zip(olds, chunks):
            for bit in bits[:-1]:
                arrived = send(part, along(bit))
                part, keep = fold(keep, arrived)
            updated = step(old, keep, send(part, along(bits[-1])))
            stepped.append(line_gather(updated, near_first=not stepped))
        corner_query = send(after(query_normed, *all_queries), layer(1, 1))
        blocks = [[chunk[k] for chunk in stepped] for k in range(n_far)]
        there = [[send(array, swap) for array in block] for block in blocks[:-1]]
        there.append([send(after(array, corner_query), swap) for array in blocks[-1]])
        blocks += there

        outs = apply_rows([corner_query, all_queries[0]], blocks, rows, BF)
        outs += apply_rows([all_queries[1], query_normed], blocks, rows, F32)
        back = [send(part, layer(*o)) for part, o in zip(outs[:-1], ((1, 1), (1, 0), (0, 1)))]
        return call(total_kernel, [struct(queries.shape, BF)], outs[-1], mixed, *back, name="total")[0]

    in_specs = (
        P(("grp", "dev"), None),
        P(("grp", "dev"), None),
        P(("grp", "dev"), None),
        P(("grp", "dev")),
        P(None, ("grp", "dev"), None),
    )
    out_specs = P(("grp", "dev"), None)
    return jax.shard_map(body, mesh=mesh, in_specs=in_specs, out_specs=out_specs, check_vma=False)
```

```python
import jax
import jax.numpy as jnp
from jax import lax
from jax.experimental import pallas as pl
from jax.experimental.pallas import tpu as pltpu
from jax.sharding import PartitionSpec as P

D = 768
HEADS = 12
HEAD_DIM = 64
CORES = 2
NEAR = 2
BF = jnp.bfloat16
F32 = jnp.float32

epsilon = 1e-06
AXES = ("grp", "dev")


def moves(mesh):
    n_grp, n_dev = mesh.shape["grp"], mesh.shape["dev"]
    n_gx, n_far = n_grp // CORES, n_dev // NEAR

    def build(target):
        pairs = []
        for gx in range(n_gx):
            for core in range(CORES):
                for far in range(n_far):
                    for near in range(NEAR):
                        to = target(gx, core, far, near)
                        source = (gx * CORES + core) * n_dev + far * NEAR + near
                        dest = (to[0] * CORES + to[1]) * n_dev + to[2] * NEAR + to[3]
                        pairs.append((source, dest))
        return pairs

    def along(step):
        return build(lambda gx, core, far, near: (gx, core, far ^ step, near))

    def layer(dx, dn):
        return build(lambda gx, core, far, near: (gx ^ dx, core, far, near ^ dn))

    swap = build(lambda gx, core, far, near: (gx, 1 - core, far, near))
    return n_far, along, layer, swap


def send(array, pairs):
    return lax.ppermute(array, AXES, pairs)


def after(value, *others):
    return lax.optimization_barrier((value, *others))[0]


def call(kernel, outs, *args, flops=0, scratch=(), in_hbm=(), limit=32 * 1024 * 1024, name=None):
    vmem = pl.BlockSpec(memory_space=pltpu.VMEM)
    size = sum(a.size * a.dtype.itemsize for a in args) + sum(o.size * o.dtype.itemsize for o in outs)
    result = pl.pallas_call(
        kernel,
        out_shape=list(outs),
        in_specs=[pl.BlockSpec(memory_space=pltpu.HBM) if i in in_hbm else vmem for i in range(len(args))],
        out_specs=[vmem] * len(outs),
        scratch_shapes=list(scratch),
        compiler_params=pltpu.CompilerParams(vmem_limit_bytes=limit),
        cost_estimate=pl.CostEstimate(flops=flops, bytes_accessed=size, transcendentals=0),
        name=name,
    )(*args)
    return result


def struct(shape, dtype):
    return jax.ShapeDtypeStruct(shape, dtype)


def nt(a, b):
    return lax.dot_general(a, b, (((1,), (1,)), ((), ())), preferred_element_type=F32)


def nn(a, b):
    return lax.dot_general(a, b, (((1,), (0,)), ((), ())), preferred_element_type=F32)


def rms(matrix):
    return matrix / jnp.sqrt(jnp.mean(matrix * matrix, axis=-1, keepdims=True) + epsilon)


def prep_kernel(key_hbm, value_hbm, rate_hbm, pair_ref, key_ref, value_ref, rate_ref, sems):
    count = key_ref.shape[0]
    sources = (key_hbm, rate_hbm, value_hbm)
    targets = (key_ref, rate_ref, value_ref)
    copies = [pltpu.make_async_copy(a, b, sems.at[i]) for i, (a, b) in enumerate(zip(sources, targets))]
    for copy in copies:
        copy.start()
    copies[0].wait()
    pair_ref[0] = rms(key_ref[...].astype(F32)).astype(BF)
    copies[1].wait()
    copies[2].wait()
    spread = jnp.broadcast_to(rate_ref[...], (count, count))
    row = lax.broadcasted_iota(jnp.int32, (count, count), 0)
    col = lax.broadcasted_iota(jnp.int32, (count, count), 1)
    rate = jnp.sum(jnp.where(row == col, spread, 0.0), axis=1, keepdims=True)
    pair_ref[1] = (-(rate * value_ref[...].astype(F32))).astype(BF)


def prep(key_tokens, value_tokens, token_rate):
    count = key_tokens.shape[0]
    return call(
        prep_kernel,
        [struct((2, count, D), BF)],
        key_tokens, value_tokens, token_rate.reshape(1, count),
        scratch=[pltpu.VMEM((count, D), BF)] * 2 + [pltpu.VMEM((1, count), F32), pltpu.SemaphoreType.DMA((3,))],
        in_hbm=(0, 1, 2),
        limit=62 * 1024 * 1024,
        name="prep",
    )[0]


def cut(rows):
    return 16 * ((3 * rows + 31) // 32)


def pieces(rows):
    edge = cut(rows)
    found = []
    for m in range(3):
        for low, high, chunk in ((0, edge, 0), (edge, 3 * rows, 1)):
            first, last = max(low, m * rows), min(high, (m + 1) * rows)
            if first < last:
                found.append((m, first - m * rows, last - first, chunk, first - low))
    return found


def stage(weights, pair, queries):
    def kernel(weights_ref, pair_ref, query_ref, weights_out, pair_out, query_out):
        weights_out[...] = weights_ref[...]
        pair_out[...] = pair_ref[...]
        query_out[...] = rms(query_ref[...].astype(F32)).astype(BF)

    return call(kernel, [struct(a.shape, BF) for a in (weights, pair, queries)], weights, pair, queries, name="stage")


def gradient(tokens, blocks, before=None):
    flat = [array for token in tokens for array in token]
    places, at = [], 0
    for token in tokens:
        places.append(((at, 0), (at, 1)) if len(token) == 1 else ((at, None), (at + 1, None)))
        at += len(token)
    count = flat[0].shape[-2]
    number, rows = len(blocks), blocks[0].shape[1]
    aligned = rows % 16 == 0
    if not aligned:
        blocks = [jnp.concatenate(blocks, axis=1)]
    size = blocks[0].shape[1]
    units = number * rows
    given = before is not None

    def kernel(*refs):
        token_refs = refs[:len(flat)]
        block_refs = refs[len(flat):len(flat) + len(blocks)]
        weights = refs[-1]
        total = refs[-2]
        if given:
            base = refs[len(flat) + len(blocks)]
        for i, ref in enumerate(block_refs):
            for m in range(3):
                weights[m * units + i * size:m * units + (i + 1) * size] = ref[m]

        def read(place):
            ref, part = token_refs[place[0]], place[1]
            return ref[...] if part is None else ref[part]

        for j in range(0, len(tokens), 2):
            keys = jnp.concatenate([read(place[0]) for place in places[j:j + 2]], axis=0)
            signal = jnp.concatenate([read(place[1]) for place in places[j:j + 2]], axis=0)
            acts = nt(weights[:2 * units], keys)
            gate_act, up_act = acts[:units], acts[units:]
            sg = jax.nn.sigmoid(gate_act)
            silu = gate_act * sg
            hidden = (silu * up_act).astype(BF)
            hidden_grad = nt(weights[2 * units:], signal)
            gate_grad = (hidden_grad * up_act * sg * (1.0 + gate_act * (1.0 - sg))).astype(BF)
            up_grad = (hidden_grad * silu).astype(BF)
            first = nn(jnp.concatenate([gate_grad, up_grad], axis=0), keys)
            last = nn(hidden, signal)
            if j or given:
                source = total if j else base
                first, last = source[:2 * units] + first, source[2 * units:] + last
            total[:2 * units] = first
            total[2 * units:] = last
        if given and aligned:
            out_refs = refs[len(flat) + len(blocks) + 1:-2]
            for m, row, span, chunk, place in pieces(rows):
                for k in range(number):
                    source = total[m * units + k * rows + row:m * units + k * rows + row + span]
                    out = out_refs[2 * chunk + (k + 1) % 2]
                    out[k // 2, place:place + span] = source.astype(out.dtype)

    edges = (cut(rows), 3 * rows - cut(rows))
    scratch = [pltpu.VMEM((3 * units, D), BF)]
    outs = [struct((3 * units, D), F32)]
    if given and aligned:
        scratch = [pltpu.VMEM((3 * units, D), F32), *scratch]
        outs = [struct((number // 2, edge, D), kind) for edge in edges for kind in (BF, F32)]
    outs = call(
        kernel, outs, *flat, *blocks, *([before] if given else []),
        flops=12 * count * len(tokens) * units * D,
        scratch=scratch,
        name="gradient" if given else "gradient_part",
    )
    if not given:
        return outs[0]
    if aligned:
        return outs[:2], outs[2:]
    total = outs[0].reshape(3, number, rows, D).swapaxes(0, 1).reshape(number, 3 * rows, D)
    parts = total[:, :edges[0]], total[:, edges[0]:]
    return [(part[1::2].astype(BF), part[::2]) for part in parts]


def fold(keep, arrived):
    number, rows = keep.shape[:2]

    def kernel(keep_ref, arrived_ref, send_ref, kept_ref):
        for k in range(number):
            total = keep_ref[k] + arrived_ref[k].astype(F32)
            out = send_ref if k % 2 else kept_ref
            out[k // 2] = total.astype(out.dtype)

    shape = (number // 2, rows, D)
    return call(kernel, [struct(shape, BF), struct(shape, F32)], keep, arrived, name="fold")


def step(old, keep, arrived):
    def kernel(old_ref, keep_ref, arrived_ref, out_ref):
        old_rows = old_ref[...].astype(F32)
        stepped = old_rows - (keep_ref[0] + arrived_ref[0].astype(F32))
        out_ref[...] = (
            stepped
            * jnp.sqrt(jnp.mean(old_rows * old_rows, axis=-1, keepdims=True) + epsilon)
            / jnp.sqrt(jnp.mean(stepped * stepped, axis=-1, keepdims=True) + epsilon)
        ).astype(BF)

    return call(kernel, [struct(old.shape, BF)], old, keep, arrived, name="step")[0]


def attention_kernel(query_ref, key_ref, value_ref, out_ref):
    count = key_ref.shape[0]
    width = 2 * HEAD_DIM
    low = lax.broadcasted_iota(jnp.int32, (count, width), 1) < HEAD_DIM
    zero = jnp.zeros((count, width), BF)
    for h in range(HEADS // 2):
        cols = slice(h * width, (h + 1) * width)
        query, key, value = query_ref[:, cols], key_ref[:, cols], value_ref[:, cols]
        probs = []
        for keep in (low, ~low):
            scores = nt(query, jnp.where(keep, key, zero)) * HEAD_DIM ** (-0.5)
            weights = jnp.exp(scores - jnp.max(scores, axis=-1, keepdims=True))
            probs.append((weights / jnp.sum(weights, axis=-1, keepdims=True)).astype(BF))
        values = jnp.concatenate([jnp.where(low, value, zero), jnp.where(low, zero, value)], axis=0)
        out_ref[:, cols] = nn(jnp.concatenate(probs, axis=1), values)


def attention(queries, key_tokens, value_tokens):
    return call(
        attention_kernel, [struct(queries.shape, F32)], queries, key_tokens, value_tokens,
        flops=4 * queries.shape[0] * key_tokens.shape[0] * D, name="attention",
    )[0]


def apply_rows(queries, blocks, rows, last):
    count = queries[0].shape[0]
    number = len(blocks)
    aligned = rows % 16 == 0
    if not aligned:
        whole = [jnp.concatenate(chunks, axis=0).reshape(3, rows, D) for chunks in blocks]
        blocks = [[jnp.concatenate(whole, axis=1).reshape(3 * number * rows, D)]]
    chunks = [chunk for block in blocks for chunk in block]
    units = number * rows

    def kernel(*refs):
        query_refs = refs[:len(queries)]
        chunk_refs = list(refs[len(queries):len(queries) + len(chunks)])
        out_refs = refs[len(queries) + len(chunks):-1]
        weights = refs[-1]
        if aligned:
            for i, block in enumerate(blocks):
                own_refs = [chunk_refs.pop(0) for _ in block]
                for m, row, size, chunk, place in pieces(rows):
                    start = m * units + i * rows + row
                    if len(block) == 1:
                        weights[start:start + size] = own_refs[0][m * rows + row:m * rows + row + size]
                    else:
                        weights[start:start + size] = own_refs[chunk][place:place + size]
        else:
            weights[...] = chunk_refs[0][...]
        stacked = jnp.concatenate([ref[...] for ref in query_refs], axis=0)
        gate_act = nt(stacked, weights[:units])
        up_act = nt(stacked, weights[units:2 * units])
        hidden = (jax.nn.silu(gate_act) * up_act).astype(BF)
        result = nn(hidden, weights[2 * units:])
        for i, out in enumerate(out_refs):
            out[...] = result[i * count:(i + 1) * count].astype(out.dtype)

    outs = [struct((count, D), BF) for _ in queries[:-1]] + [struct((count, D), last)]
    return call(
        kernel, outs, *queries, *chunks,
        flops=6 * count * len(queries) * units * D,
        scratch=[pltpu.VMEM((3 * units, D), BF)],
        name="apply",
    )


def total_kernel(*refs):
    result = refs[0][...] + refs[1][...]
    for ref in refs[2:-1]:
        result = result + ref[...].astype(F32)
    refs[-1][...] = result.astype(BF)


def solution(mesh):
    n_far, along, layer, swap = moves(mesh)
    bits = [1 << i for i in range(n_far.bit_length() - 1)]

    def line_gather(block, near_first=False):
        blocks = {0: block}
        for bit in reversed(bits):
            for k in list(blocks):
                source = after(blocks[k], blocks[1]) if near_first and k and bit == 1 else blocks[k]
                blocks[k ^ bit] = send(source, along(bit))
        return blocks

    def body(key_tokens, value_tokens, queries, token_rate, fast_weights):
        rows = fast_weights.shape[1]
        pair = prep(key_tokens, value_tokens, token_rate)
        at_x, at_y, corner = [send(pair, layer(*o)) for o in ((1, 0), (0, 1), (1, 1))]
        line = line_gather(fast_weights)
        own_weights, own_pair, query_normed = stage(after(fast_weights, line[bits[-1]]), pair, queries)
        own_there = send(after(own_pair, at_x, *[line[k] for k in range(1, n_far)]), swap)
        blocks = [own_weights] + [line[k] for k in range(1, n_far)]
        part = gradient([(token,) for token in (own_pair, own_there, at_x, send(at_x, swap))], blocks)
        late = [at_y, corner, send(at_y, swap), send(corner, swap)]
        chunks = gradient([(token,) for token in late], blocks, part)

        query_normed = after(query_normed, chunks[0][0])
        all_queries = [send(query_normed, layer(*o)) for o in ((1, 0), (0, 1))]
        mixed = attention(queries, key_tokens, value_tokens)

        flat = own_weights.reshape(3 * rows, D)
        olds = flat[:cut(rows)], flat[cut(rows):]
        stepped = []
        for old, (part, keep) in zip(olds, chunks):
            for bit in bits[:-1]:
                arrived = send(part, along(bit))
                part, keep = fold(keep, arrived)
            updated = step(old, keep, send(part, along(bits[-1])))
            stepped.append(line_gather(updated, near_first=not stepped))
        corner_query = send(after(query_normed, *all_queries), layer(1, 1))
        blocks = [[chunk[k] for chunk in stepped] for k in range(n_far)]
        there = [[send(array, swap) for array in block] for block in blocks[:-1]]
        there.append([send(after(array, corner_query), swap) for array in blocks[-1]])
        blocks += there

        outs = apply_rows([corner_query, all_queries[0]], blocks, rows, BF)
        outs += apply_rows([all_queries[1], query_normed], blocks, rows, F32)
        back = [send(part, layer(*o)) for part, o in zip(outs[:-1], ((1, 1), (1, 0), (0, 1)))]
        return call(total_kernel, [struct(queries.shape, BF)], outs[-1], mixed, *back, name="total")[0]

    in_specs = (
        P(("grp", "dev"), None),
        P(("grp", "dev"), None),
        P(("grp", "dev"), None),
        P(("grp", "dev")),
        P(None, ("grp", "dev"), None),
    )
    out_specs = P(("grp", "dev"), None)
    return jax.shard_map(body, mesh=mesh, in_specs=in_specs, out_specs=out_specs, check_vma=False)
```

```python
import jax
import jax.numpy as jnp
from jax import lax
from jax.experimental import pallas as pl
from jax.experimental.pallas import tpu as pltpu
from jax.sharding import PartitionSpec as P

D = 768
HEADS = 12
HEAD_DIM = 64
CORES = 2
NEAR = 2
BF = jnp.bfloat16
F32 = jnp.float32

epsilon = 1e-06
AXES = ("grp", "dev")


def moves(mesh):
    n_grp, n_dev = mesh.shape["grp"], mesh.shape["dev"]
    n_gx, n_far = n_grp // CORES, n_dev // NEAR

    def build(target):
        pairs = []
        for gx in range(n_gx):
            for core in range(CORES):
                for far in range(n_far):
                    for near in range(NEAR):
                        to = target(gx, core, far, near)
                        source = (gx * CORES + core) * n_dev + far * NEAR + near
                        dest = (to[0] * CORES + to[1]) * n_dev + to[2] * NEAR + to[3]
                        pairs.append((source, dest))
        return pairs

    def along(step):
        return build(lambda gx, core, far, near: (gx, core, far ^ step, near))

    def layer(dx, dn):
        return build(lambda gx, core, far, near: (gx ^ dx, core, far, near ^ dn))

    swap = build(lambda gx, core, far, near: (gx, 1 - core, far, near))
    return n_far, along, layer, swap


def send(array, pairs):
    return lax.ppermute(array, AXES, pairs)


def after(value, *others):
    return lax.optimization_barrier((value, *others))[0]


def call(kernel, outs, *args, flops=0, scratch=(), in_hbm=(), limit=32 * 1024 * 1024, name=None):
    vmem = pl.BlockSpec(memory_space=pltpu.VMEM)
    size = sum(a.size * a.dtype.itemsize for a in args) + sum(o.size * o.dtype.itemsize for o in outs)
    result = pl.pallas_call(
        kernel,
        out_shape=list(outs),
        in_specs=[pl.BlockSpec(memory_space=pltpu.HBM) if i in in_hbm else vmem for i in range(len(args))],
        out_specs=[vmem] * len(outs),
        scratch_shapes=list(scratch),
        compiler_params=pltpu.CompilerParams(vmem_limit_bytes=limit),
        cost_estimate=pl.CostEstimate(flops=flops, bytes_accessed=size, transcendentals=0),
        name=name,
    )(*args)
    return result


def struct(shape, dtype):
    return jax.ShapeDtypeStruct(shape, dtype)


def nt(a, b):
    return lax.dot_general(a, b, (((1,), (1,)), ((), ())), preferred_element_type=F32)


def nn(a, b):
    return lax.dot_general(a, b, (((1,), (0,)), ((), ())), preferred_element_type=F32)


def rms(matrix):
    return matrix / jnp.sqrt(jnp.mean(matrix * matrix, axis=-1, keepdims=True) + epsilon)


def prep_kernel(key_hbm, value_hbm, rate_hbm, pair_ref, key_ref, value_ref, rate_ref, sems):
    count = key_ref.shape[0]
    sources = (key_hbm, rate_hbm, value_hbm)
    targets = (key_ref, rate_ref, value_ref)
    copies = [pltpu.make_async_copy(a, b, sems.at[i]) for i, (a, b) in enumerate(zip(sources, targets))]
    for copy in copies:
        copy.start()
    copies[0].wait()
    pair_ref[0] = rms(key_ref[...].astype(F32)).astype(BF)
    copies[1].wait()
    copies[2].wait()
    spread = jnp.broadcast_to(rate_ref[...], (count, count))
    row = lax.broadcasted_iota(jnp.int32, (count, count), 0)
    col = lax.broadcasted_iota(jnp.int32, (count, count), 1)
    rate = jnp.sum(jnp.where(row == col, spread, 0.0), axis=1, keepdims=True)
    pair_ref[1] = (-(rate * value_ref[...].astype(F32))).astype(BF)


def prep(key_tokens, value_tokens, token_rate):
    count = key_tokens.shape[0]
    return call(
        prep_kernel,
        [struct((2, count, D), BF)],
        key_tokens, value_tokens, token_rate.reshape(1, count),
        scratch=[pltpu.VMEM((count, D), BF)] * 2 + [pltpu.VMEM((1, count), F32), pltpu.SemaphoreType.DMA((3,))],
        in_hbm=(0, 1, 2),
        limit=62 * 1024 * 1024,
        name="prep",
    )[0]


def cut(rows):
    return 16 * ((3 * rows + 31) // 32)


def pieces(rows):
    edge = cut(rows)
    found = []
    for m in range(3):
        for low, high, chunk in ((0, edge, 0), (edge, 3 * rows, 1)):
            first, last = max(low, m * rows), min(high, (m + 1) * rows)
            if first < last:
                found.append((m, first - m * rows, last - first, chunk, first - low))
    return found


def stage(weights, pair, queries):
    def kernel(weights_ref, pair_ref, query_ref, weights_out, pair_out, query_out):
        weights_out[...] = weights_ref[...]
        pair_out[...] = pair_ref[...]
        query_out[...] = rms(query_ref[...].astype(F32)).astype(BF)

    return call(kernel, [struct(a.shape, BF) for a in (weights, pair, queries)], weights, pair, queries, name="stage")


def gradient(tokens, blocks, before=None):
    flat = [array for token in tokens for array in token]
    places, at = [], 0
    for token in tokens:
        places.append(((at, 0), (at, 1)) if len(token) == 1 else ((at, None), (at + 1, None)))
        at += len(token)
    count = flat[0].shape[-2]
    number, rows = len(blocks), blocks[0].shape[1]
    aligned = rows % 16 == 0
    if not aligned:
        blocks = [jnp.concatenate(blocks, axis=1)]
    size = blocks[0].shape[1]
    units = number * rows
    given = before is not None

    def kernel(*refs):
        token_refs = refs[:len(flat)]
        block_refs = refs[len(flat):len(flat) + len(blocks)]
        weights = refs[-1]
        total = refs[-2]
        if given:
            base = refs[len(flat) + len(blocks)]
        for i, ref in enumerate(block_refs):
            for m in range(3):
                weights[m * units + i * size:m * units + (i + 1) * size] = ref[m]

        def read(place):
            ref, part = token_refs[place[0]], place[1]
            return ref[...] if part is None else ref[part]

        for j in range(0, len(tokens), 2):
            keys = jnp.concatenate([read(place[0]) for place in places[j:j + 2]], axis=0)
            signal = jnp.concatenate([read(place[1]) for place in places[j:j + 2]], axis=0)
            acts = nt(weights[:2 * units], keys)
            gate_act, up_act = acts[:units], acts[units:]
            sg = jax.nn.sigmoid(gate_act)
            silu = gate_act * sg
            hidden = (silu * up_act).astype(BF)
            hidden_grad = nt(weights[2 * units:], signal)
            gate_grad = (hidden_grad * up_act * sg * (1.0 + gate_act * (1.0 - sg))).astype(BF)
            up_grad = (hidden_grad * silu).astype(BF)
            first = nn(jnp.concatenate([gate_grad, up_grad], axis=0), keys)
            last = nn(hidden, signal)
            if j or given:
                source = total if j else base
                first, last = source[:2 * units] + first, source[2 * units:] + last
            total[:2 * units] = first
            total[2 * units:] = last
        if given and aligned:
            out_refs = refs[len(flat) + len(blocks) + 1:-2]
            for m, row, span, chunk, place in pieces(rows):
                for k in range(number):
                    source = total[m * units + k * rows + row:m * units + k * rows + row + span]
                    out = out_refs[2 * chunk + (k + 1) % 2]
                    out[k // 2, place:place + span] = source.astype(out.dtype)

    edges = (cut(rows), 3 * rows - cut(rows))
    scratch = [pltpu.VMEM((3 * units, D), BF)]
    outs = [struct((3 * units, D), F32)]
    if given and aligned:
        scratch = [pltpu.VMEM((3 * units, D), F32), *scratch]
        outs = [struct((number // 2, edge, D), kind) for edge in edges for kind in (BF, F32)]
    outs = call(
        kernel, outs, *flat, *blocks, *([before] if given else []),
        flops=12 * count * len(tokens) * units * D,
        scratch=scratch,
        name="gradient" if given else "gradient_part",
    )
    if not given:
        return outs[0]
    if aligned:
        return outs[:2], outs[2:]
    total = outs[0].reshape(3, number, rows, D).swapaxes(0, 1).reshape(number, 3 * rows, D)
    parts = total[:, :edges[0]], total[:, edges[0]:]
    return [(part[1::2].astype(BF), part[::2]) for part in parts]


def fold(keep, arrived):
    number, rows = keep.shape[:2]

    def kernel(keep_ref, arrived_ref, send_ref, kept_ref):
        for k in range(number):
            total = keep_ref[k] + arrived_ref[k].astype(F32)
            out = send_ref if k % 2 else kept_ref
            out[k // 2] = total.astype(out.dtype)

    shape = (number // 2, rows, D)
    return call(kernel, [struct(shape, BF), struct(shape, F32)], keep, arrived, name="fold")


def step(old, keep, arrived):
    def kernel(old_ref, keep_ref, arrived_ref, out_ref):
        old_rows = old_ref[...].astype(F32)
        stepped = old_rows - (keep_ref[0] + arrived_ref[0].astype(F32))
        out_ref[...] = (
            stepped
            * jnp.sqrt(jnp.mean(old_rows * old_rows, axis=-1, keepdims=True) + epsilon)
            / jnp.sqrt(jnp.mean(stepped * stepped, axis=-1, keepdims=True) + epsilon)
        ).astype(BF)

    return call(kernel, [struct(old.shape, BF)], old, keep, arrived, name="step")[0]


def attention_kernel(query_ref, key_ref, value_ref, out_ref):
    count = key_ref.shape[0]
    width = 2 * HEAD_DIM
    low = lax.broadcasted_iota(jnp.int32, (count, width), 1) < HEAD_DIM
    zero = jnp.zeros((count, width), BF)
    for h in range(HEADS // 2):
        cols = slice(h * width, (h + 1) * width)
        query, key, value = query_ref[:, cols], key_ref[:, cols], value_ref[:, cols]
        probs = []
        for keep in (low, ~low):
            scores = nt(query, jnp.where(keep, key, zero)) * HEAD_DIM ** (-0.5)
            weights = jnp.exp(scores - jnp.max(scores, axis=-1, keepdims=True))
            probs.append((weights / jnp.sum(weights, axis=-1, keepdims=True)).astype(BF))
        values = jnp.concatenate([jnp.where(low, value, zero), jnp.where(low, zero, value)], axis=0)
        out_ref[:, cols] = nn(jnp.concatenate(probs, axis=1), values)


def attention(queries, key_tokens, value_tokens):
    return call(
        attention_kernel, [struct(queries.shape, F32)], queries, key_tokens, value_tokens,
        flops=4 * queries.shape[0] * key_tokens.shape[0] * D, name="attention",
    )[0]


def apply_rows(queries, blocks, rows, last):
    count = queries[0].shape[0]
    number = len(blocks)
    aligned = rows % 16 == 0
    if not aligned:
        whole = [jnp.concatenate(chunks, axis=0).reshape(3, rows, D) for chunks in blocks]
        blocks = [[jnp.concatenate(whole, axis=1).reshape(3 * number * rows, D)]]
    chunks = [chunk for block in blocks for chunk in block]
    units = number * rows

    def kernel(*refs):
        query_refs = refs[:len(queries)]
        chunk_refs = list(refs[len(queries):len(queries) + len(chunks)])
        out_refs = refs[len(queries) + len(chunks):-1]
        weights = refs[-1]
        if aligned:
            for i, block in enumerate(blocks):
                own_refs = [chunk_refs.pop(0) for _ in block]
                for m, row, size, chunk, place in pieces(rows):
                    start = m * units + i * rows + row
                    if len(block) == 1:
                        weights[start:start + size] = own_refs[0][m * rows + row:m * rows + row + size]
                    else:
                        weights[start:start + size] = own_refs[chunk][place:place + size]
        else:
            weights[...] = chunk_refs[0][...]
        stacked = jnp.concatenate([ref[...] for ref in query_refs], axis=0)
        gate_act = nt(stacked, weights[:units])
        up_act = nt(stacked, weights[units:2 * units])
        hidden = (jax.nn.silu(gate_act) * up_act).astype(BF)
        result = nn(hidden, weights[2 * units:])
        for i, out in enumerate(out_refs):
            out[...] = result[i * count:(i + 1) * count].astype(out.dtype)

    outs = [struct((count, D), BF) for _ in queries[:-1]] + [struct((count, D), last)]
    return call(
        kernel, outs, *queries, *chunks,
        flops=6 * count * len(queries) * units * D,
        scratch=[pltpu.VMEM((3 * units, D), BF)],
        name="apply",
    )


def total_kernel(*refs):
    result = refs[0][...] + refs[1][...]
    for ref in refs[2:-1]:
        result = result + ref[...].astype(F32)
    refs[-1][...] = result.astype(BF)


def solution(mesh):
    n_far, along, layer, swap = moves(mesh)
    bits = [1 << i for i in range(n_far.bit_length() - 1)]

    def line_gather(block, *first):
        blocks = {0: block}
        for bit in reversed(bits):
            for k in list(blocks):
                source = after(blocks[k], *first) if first and k and bit == 1 else blocks[k]
                blocks[k ^ bit] = send(source, along(bit))
        return blocks

    def body(key_tokens, value_tokens, queries, token_rate, fast_weights):
        rows = fast_weights.shape[1]
        pair = prep(key_tokens, value_tokens, token_rate)
        at_x, at_y, corner = [send(pair, layer(*o)) for o in ((1, 0), (0, 1), (1, 1))]
        line = line_gather(fast_weights)
        own_weights, own_pair, query_normed = stage(after(fast_weights, line[bits[-1]]), pair, queries)
        own_there = send(after(own_pair, at_x, *[line[k] for k in range(1, n_far)]), swap)
        blocks = [own_weights] + [line[k] for k in range(1, n_far)]
        part = gradient([(token,) for token in (own_pair, own_there, at_x, send(at_x, swap))], blocks)
        late = [at_y, corner, send(at_y, swap), send(corner, swap)]
        chunks = gradient([(token,) for token in late], blocks, part)

        query_normed = after(query_normed, chunks[0][0])
        all_queries = [send(query_normed, layer(*o)) for o in ((1, 0), (0, 1))]
        mixed = attention(queries, key_tokens, value_tokens)

        flat = own_weights.reshape(3 * rows, D)
        olds = flat[:cut(rows)], flat[cut(rows):]
        stepped = []
        for old, (part, keep) in zip(olds, chunks):
            for bit in bits[:-1]:
                arrived = send(part, along(bit))
                part, keep = fold(keep, arrived)
            updated = step(old, keep, send(part, along(bits[-1])))
            stepped.append(line_gather(updated, *[chunk[1] for chunk in stepped]))
        corner_query = send(after(query_normed, *all_queries), layer(1, 1))
        blocks = [[chunk[k] for chunk in stepped] for k in range(n_far)]
        there = [[send(array, swap) for array in block] for block in blocks[:-1]]
        there.append([send(after(array, corner_query), swap) for array in blocks[-1]])
        blocks += there

        outs = apply_rows([corner_query, all_queries[0]], blocks, rows, BF)
        outs += apply_rows([all_queries[1], query_normed], blocks, rows, F32)
        back = [send(part, layer(*o)) for part, o in zip(outs[:-1], ((1, 1), (1, 0), (0, 1)))]
        return call(total_kernel, [struct(queries.shape, BF)], outs[-1], mixed, *back, name="total")[0]

    in_specs = (
        P(("grp", "dev"), None),
        P(("grp", "dev"), None),
        P(("grp", "dev"), None),
        P(("grp", "dev")),
        P(None, ("grp", "dev"), None),
    )
    out_specs = P(("grp", "dev"), None)
    return jax.shard_map(body, mesh=mesh, in_specs=in_specs, out_specs=out_specs, check_vma=False)
```

```python
import jax
import jax.numpy as jnp
from jax import lax
from jax.experimental import pallas as pl
from jax.experimental.pallas import tpu as pltpu
from jax.sharding import PartitionSpec as P

D = 768
HEADS = 12
HEAD_DIM = 64
CORES = 2
NEAR = 2
BF = jnp.bfloat16
F32 = jnp.float32

epsilon = 1e-06
AXES = ("grp", "dev")


def moves(mesh):
    n_grp, n_dev = mesh.shape["grp"], mesh.shape["dev"]
    n_gx, n_far = n_grp // CORES, n_dev // NEAR

    def build(target):
        pairs = []
        for gx in range(n_gx):
            for core in range(CORES):
                for far in range(n_far):
                    for near in range(NEAR):
                        to = target(gx, core, far, near)
                        source = (gx * CORES + core) * n_dev + far * NEAR + near
                        dest = (to[0] * CORES + to[1]) * n_dev + to[2] * NEAR + to[3]
                        pairs.append((source, dest))
        return pairs

    def along(step):
        return build(lambda gx, core, far, near: (gx, core, far ^ step, near))

    def layer(dx, dn):
        return build(lambda gx, core, far, near: (gx ^ dx, core, far, near ^ dn))

    swap = build(lambda gx, core, far, near: (gx, 1 - core, far, near))
    return n_far, along, layer, swap


def send(array, pairs):
    return lax.ppermute(array, AXES, pairs)


def after(value, *others):
    return lax.optimization_barrier((value, *others))[0]


def call(kernel, outs, *args, flops=0, scratch=(), in_hbm=(), limit=32 * 1024 * 1024, name=None):
    vmem = pl.BlockSpec(memory_space=pltpu.VMEM)
    size = sum(a.size * a.dtype.itemsize for a in args) + sum(o.size * o.dtype.itemsize for o in outs)
    result = pl.pallas_call(
        kernel,
        out_shape=list(outs),
        in_specs=[pl.BlockSpec(memory_space=pltpu.HBM) if i in in_hbm else vmem for i in range(len(args))],
        out_specs=[vmem] * len(outs),
        scratch_shapes=list(scratch),
        compiler_params=pltpu.CompilerParams(vmem_limit_bytes=limit),
        cost_estimate=pl.CostEstimate(flops=flops, bytes_accessed=size, transcendentals=0),
        name=name,
    )(*args)
    return result


def struct(shape, dtype):
    return jax.ShapeDtypeStruct(shape, dtype)


def nt(a, b):
    return lax.dot_general(a, b, (((1,), (1,)), ((), ())), preferred_element_type=F32)


def nn(a, b):
    return lax.dot_general(a, b, (((1,), (0,)), ((), ())), preferred_element_type=F32)


def rms(matrix):
    return matrix / jnp.sqrt(jnp.mean(matrix * matrix, axis=-1, keepdims=True) + epsilon)


def prep_kernel(key_hbm, value_hbm, rate_hbm, pair_ref, key_ref, value_ref, rate_ref, sems):
    count = key_ref.shape[0]
    sources = (key_hbm, rate_hbm, value_hbm)
    targets = (key_ref, rate_ref, value_ref)
    copies = [pltpu.make_async_copy(a, b, sems.at[i]) for i, (a, b) in enumerate(zip(sources, targets))]
    for copy in copies:
        copy.start()
    copies[0].wait()
    pair_ref[0] = rms(key_ref[...].astype(F32)).astype(BF)
    copies[1].wait()
    copies[2].wait()
    spread = jnp.broadcast_to(rate_ref[...], (count, count))
    row = lax.broadcasted_iota(jnp.int32, (count, count), 0)
    col = lax.broadcasted_iota(jnp.int32, (count, count), 1)
    rate = jnp.sum(jnp.where(row == col, spread, 0.0), axis=1, keepdims=True)
    pair_ref[1] = (-(rate * value_ref[...].astype(F32))).astype(BF)


def prep(key_tokens, value_tokens, token_rate):
    count = key_tokens.shape[0]
    return call(
        prep_kernel,
        [struct((2, count, D), BF)],
        key_tokens, value_tokens, token_rate.reshape(1, count),
        scratch=[pltpu.VMEM((count, D), BF)] * 2 + [pltpu.VMEM((1, count), F32), pltpu.SemaphoreType.DMA((3,))],
        in_hbm=(0, 1, 2),
        limit=62 * 1024 * 1024,
        name="prep",
    )[0]


def cut(rows):
    return 16 * ((3 * rows + 31) // 32)


def pieces(rows):
    edge = cut(rows)
    found = []
    for m in range(3):
        for low, high, chunk in ((0, edge, 0), (edge, 3 * rows, 1)):
            first, last = max(low, m * rows), min(high, (m + 1) * rows)
            if first < last:
                found.append((m, first - m * rows, last - first, chunk, first - low))
    return found


def stage(weights, pair, queries):
    def kernel(weights_ref, pair_ref, query_ref, weights_out, pair_out, query_out):
        weights_out[...] = weights_ref[...]
        pair_out[...] = pair_ref[...]
        query_out[...] = rms(query_ref[...].astype(F32)).astype(BF)

    return call(kernel, [struct(a.shape, BF) for a in (weights, pair, queries)], weights, pair, queries, name="stage")


def gradient(tokens, blocks, before=None):
    flat = [array for token in tokens for array in token]
    places, at = [], 0
    for token in tokens:
        places.append(((at, 0), (at, 1)) if len(token) == 1 else ((at, None), (at + 1, None)))
        at += len(token)
    count = flat[0].shape[-2]
    number, rows = len(blocks), blocks[0].shape[1]
    aligned = rows % 16 == 0
    if not aligned:
        blocks = [jnp.concatenate(blocks, axis=1)]
    size = blocks[0].shape[1]
    units = number * rows
    given = before is not None

    def kernel(*refs):
        token_refs = refs[:len(flat)]
        block_refs = refs[len(flat):len(flat) + len(blocks)]
        weights = refs[-1]
        total = refs[-2]
        if given:
            base = refs[len(flat) + len(blocks)]
        for i, ref in enumerate(block_refs):
            for m in range(3):
                weights[m * units + i * size:m * units + (i + 1) * size] = ref[m]

        def read(place):
            ref, part = token_refs[place[0]], place[1]
            return ref[...] if part is None else ref[part]

        for j in range(0, len(tokens), 2):
            keys = jnp.concatenate([read(place[0]) for place in places[j:j + 2]], axis=0)
            signal = jnp.concatenate([read(place[1]) for place in places[j:j + 2]], axis=0)
            acts = nt(weights[:2 * units], keys)
            gate_act, up_act = acts[:units], acts[units:]
            sg = jax.nn.sigmoid(gate_act)
            silu = gate_act * sg
            hidden = (silu * up_act).astype(BF)
            hidden_grad = nt(weights[2 * units:], signal)
            gate_grad = (hidden_grad * up_act * sg * (1.0 + gate_act * (1.0 - sg))).astype(BF)
            up_grad = (hidden_grad * silu).astype(BF)
            first = nn(jnp.concatenate([gate_grad, up_grad], axis=0), keys)
            last = nn(hidden, signal)
            if j or given:
                source = total if j else base
                first, last = source[:2 * units] + first, source[2 * units:] + last
            total[:2 * units] = first
            total[2 * units:] = last
        if given and aligned:
            out_refs = refs[len(flat) + len(blocks) + 1:-2]
            for m, row, span, chunk, place in pieces(rows):
                for k in range(number):
                    source = total[m * units + k * rows + row:m * units + k * rows + row + span]
                    out = out_refs[2 * chunk + (k + 1) % 2]
                    out[k // 2, place:place + span] = source.astype(out.dtype)

    edges = (cut(rows), 3 * rows - cut(rows))
    scratch = [pltpu.VMEM((3 * units, D), BF)]
    outs = [struct((3 * units, D), F32)]
    if given and aligned:
        scratch = [pltpu.VMEM((3 * units, D), F32), *scratch]
        outs = [struct((number // 2, edge, D), kind) for edge in edges for kind in (BF, F32)]
    outs = call(
        kernel, outs, *flat, *blocks, *([before] if given else []),
        flops=12 * count * len(tokens) * units * D,
        scratch=scratch,
        name="gradient" if given else "gradient_part",
    )
    if not given:
        return outs[0]
    if aligned:
        return outs[:2], outs[2:]
    total = outs[0].reshape(3, number, rows, D).swapaxes(0, 1).reshape(number, 3 * rows, D)
    parts = total[:, :edges[0]], total[:, edges[0]:]
    return [(part[1::2].astype(BF), part[::2]) for part in parts]


def fold(keep, arrived):
    number, rows = keep.shape[:2]

    def kernel(keep_ref, arrived_ref, send_ref, kept_ref):
        for k in range(number):
            total = keep_ref[k] + arrived_ref[k].astype(F32)
            out = send_ref if k % 2 else kept_ref
            out[k // 2] = total.astype(out.dtype)

    shape = (number // 2, rows, D)
    return call(kernel, [struct(shape, BF), struct(shape, F32)], keep, arrived, name="fold")


def step(old, keep, arrived):
    def kernel(old_ref, keep_ref, arrived_ref, out_ref):
        old_rows = old_ref[...].astype(F32)
        stepped = old_rows - (keep_ref[0] + arrived_ref[0].astype(F32))
        out_ref[...] = (
            stepped
            * jnp.sqrt(jnp.mean(old_rows * old_rows, axis=-1, keepdims=True) + epsilon)
            / jnp.sqrt(jnp.mean(stepped * stepped, axis=-1, keepdims=True) + epsilon)
        ).astype(BF)

    return call(kernel, [struct(old.shape, BF)], old, keep, arrived, name="step")[0]


def attention_kernel(query_ref, key_ref, value_ref, out_ref):
    count = key_ref.shape[0]
    width = 2 * HEAD_DIM
    low = lax.broadcasted_iota(jnp.int32, (count, width), 1) < HEAD_DIM
    zero = jnp.zeros((count, width), BF)
    for h in range(HEADS // 2):
        cols = slice(h * width, (h + 1) * width)
        query, key, value = query_ref[:, cols], key_ref[:, cols], value_ref[:, cols]
        probs = []
        for keep in (low, ~low):
            scores = nt(query, jnp.where(keep, key, zero)) * HEAD_DIM ** (-0.5)
            weights = jnp.exp(scores - jnp.max(scores, axis=-1, keepdims=True))
            probs.append((weights / jnp.sum(weights, axis=-1, keepdims=True)).astype(BF))
        values = jnp.concatenate([jnp.where(low, value, zero), jnp.where(low, zero, value)], axis=0)
        out_ref[:, cols] = nn(jnp.concatenate(probs, axis=1), values)


def attention(queries, key_tokens, value_tokens):
    return call(
        attention_kernel, [struct(queries.shape, F32)], queries, key_tokens, value_tokens,
        flops=4 * queries.shape[0] * key_tokens.shape[0] * D, name="attention",
    )[0]


def apply_rows(queries, blocks, rows, last):
    count = queries[0].shape[0]
    number = len(blocks)
    aligned = rows % 16 == 0
    if not aligned:
        whole = [jnp.concatenate(chunks, axis=0).reshape(3, rows, D) for chunks in blocks]
        blocks = [[jnp.concatenate(whole, axis=1).reshape(3 * number * rows, D)]]
    chunks = [chunk for block in blocks for chunk in block]
    units = number * rows

    def kernel(*refs):
        query_refs = refs[:len(queries)]
        chunk_refs = list(refs[len(queries):len(queries) + len(chunks)])
        out_refs = refs[len(queries) + len(chunks):-1]
        weights = refs[-1]
        if aligned:
            for i, block in enumerate(blocks):
                own_refs = [chunk_refs.pop(0) for _ in block]
                for m, row, size, chunk, place in pieces(rows):
                    start = m * units + i * rows + row
                    if len(block) == 1:
                        weights[start:start + size] = own_refs[0][m * rows + row:m * rows + row + size]
                    else:
                        weights[start:start + size] = own_refs[chunk][place:place + size]
        else:
            weights[...] = chunk_refs[0][...]
        stacked = jnp.concatenate([ref[...] for ref in query_refs], axis=0)
        gate_act = nt(stacked, weights[:units])
        up_act = nt(stacked, weights[units:2 * units])
        hidden = (jax.nn.silu(gate_act) * up_act).astype(BF)
        result = nn(hidden, weights[2 * units:])
        for i, out in enumerate(out_refs):
            out[...] = result[i * count:(i + 1) * count].astype(out.dtype)

    outs = [struct((count, D), BF) for _ in queries[:-1]] + [struct((count, D), last)]
    return call(
        kernel, outs, *queries, *chunks,
        flops=6 * count * len(queries) * units * D,
        scratch=[pltpu.VMEM((3 * units, D), BF)],
        name="apply",
    )


def total_kernel(*refs):
    result = refs[0][...] + refs[1][...]
    for ref in refs[2:-1]:
        result = result + ref[...].astype(F32)
    refs[-1][...] = result.astype(BF)


def solution(mesh):
    n_far, along, layer, swap = moves(mesh)
    bits = [1 << i for i in range(n_far.bit_length() - 1)]

    def line_gather(block, *first):
        blocks = {0: block}
        for bit in reversed(bits):
            for k in list(blocks):
                source = after(blocks[k], *first) if first and k and bit == 1 else blocks[k]
                blocks[k ^ bit] = send(source, along(bit))
        return blocks

    def body(key_tokens, value_tokens, queries, token_rate, fast_weights):
        rows = fast_weights.shape[1]
        pair = prep(key_tokens, value_tokens, token_rate)
        at_x, at_y, corner = [send(pair, layer(*o)) for o in ((1, 0), (0, 1), (1, 1))]
        line = line_gather(fast_weights)
        own_weights, own_pair, query_normed = stage(after(fast_weights, line[bits[-1]]), pair, queries)
        own_there = send(after(own_pair, at_x, *[line[k] for k in range(1, n_far)]), swap)
        blocks = [own_weights] + [line[k] for k in range(1, n_far)]
        part = gradient([(token,) for token in (own_pair, own_there, at_x, send(at_x, swap))], blocks)
        late = [at_y, corner, send(at_y, swap), send(corner, swap)]
        chunks = gradient([(token,) for token in late], blocks, part)

        query_normed = after(query_normed, chunks[0][0])
        all_queries = [send(query_normed, layer(*o)) for o in ((1, 0), (0, 1))]
        mixed = attention(queries, key_tokens, value_tokens)

        flat = own_weights.reshape(3 * rows, D)
        olds = flat[:cut(rows)], flat[cut(rows):]
        stepped = []
        for old, (part, keep) in zip(olds, chunks):
            for bit in bits[:-1]:
                arrived = send(part, along(bit))
                part, keep = fold(keep, arrived)
            updated = step(old, keep, send(part, along(bits[-1])))
            stepped.append(line_gather(updated, *[chunk[1] for chunk in stepped]))
        corner_query = send(after(query_normed, *all_queries), layer(1, 1))
        blocks = [[chunk[k] for chunk in stepped] for k in range(n_far)]
        there = [[send(array, swap) for array in block] for block in blocks[:-1]]
        there.append([send(after(blocks[-1][0], corner_query), swap), send(blocks[-1][1], swap)])
        blocks += there

        outs = apply_rows([corner_query, all_queries[0]], blocks, rows, BF)
        outs += apply_rows([all_queries[1], query_normed], blocks, rows, F32)
        back = [send(part, layer(*o)) for part, o in zip(outs[:-1], ((1, 1), (1, 0), (0, 1)))]
        return call(total_kernel, [struct(queries.shape, BF)], outs[-1], mixed, *back, name="total")[0]

    in_specs = (
        P(("grp", "dev"), None),
        P(("grp", "dev"), None),
        P(("grp", "dev"), None),
        P(("grp", "dev")),
        P(None, ("grp", "dev"), None),
    )
    out_specs = P(("grp", "dev"), None)
    return jax.shard_map(body, mesh=mesh, in_specs=in_specs, out_specs=out_specs, check_vma=False)
```

```python
import jax
import jax.numpy as jnp
from jax import lax
from jax.experimental import pallas as pl
from jax.experimental.pallas import tpu as pltpu
from jax.sharding import PartitionSpec as P

D = 768
HEADS = 12
HEAD_DIM = 64
CORES = 2
NEAR = 2
BF = jnp.bfloat16
F32 = jnp.float32

epsilon = 1e-06
AXES = ("grp", "dev")


def moves(mesh):
    n_grp, n_dev = mesh.shape["grp"], mesh.shape["dev"]
    n_gx, n_far = n_grp // CORES, n_dev // NEAR

    def build(target):
        pairs = []
        for gx in range(n_gx):
            for core in range(CORES):
                for far in range(n_far):
                    for near in range(NEAR):
                        to = target(gx, core, far, near)
                        source = (gx * CORES + core) * n_dev + far * NEAR + near
                        dest = (to[0] * CORES + to[1]) * n_dev + to[2] * NEAR + to[3]
                        pairs.append((source, dest))
        return pairs

    def along(step):
        return build(lambda gx, core, far, near: (gx, core, far ^ step, near))

    def layer(dx, dn):
        return build(lambda gx, core, far, near: (gx ^ dx, core, far, near ^ dn))

    swap = build(lambda gx, core, far, near: (gx, 1 - core, far, near))
    return n_far, along, layer, swap


def send(array, pairs):
    return lax.ppermute(array, AXES, pairs)


def after(value, *others):
    return lax.optimization_barrier((value, *others))[0]


def call(kernel, outs, *args, flops=0, scratch=(), in_hbm=(), limit=32 * 1024 * 1024, name=None):
    vmem = pl.BlockSpec(memory_space=pltpu.VMEM)
    size = sum(a.size * a.dtype.itemsize for a in args) + sum(o.size * o.dtype.itemsize for o in outs)
    result = pl.pallas_call(
        kernel,
        out_shape=list(outs),
        in_specs=[pl.BlockSpec(memory_space=pltpu.HBM) if i in in_hbm else vmem for i in range(len(args))],
        out_specs=[vmem] * len(outs),
        scratch_shapes=list(scratch),
        compiler_params=pltpu.CompilerParams(vmem_limit_bytes=limit),
        cost_estimate=pl.CostEstimate(flops=flops, bytes_accessed=size, transcendentals=0),
        name=name,
    )(*args)
    return result


def struct(shape, dtype):
    return jax.ShapeDtypeStruct(shape, dtype)


def nt(a, b):
    return lax.dot_general(a, b, (((1,), (1,)), ((), ())), preferred_element_type=F32)


def nn(a, b):
    return lax.dot_general(a, b, (((1,), (0,)), ((), ())), preferred_element_type=F32)


def rms(matrix):
    return matrix / jnp.sqrt(jnp.mean(matrix * matrix, axis=-1, keepdims=True) + epsilon)


def prep_kernel(key_hbm, value_hbm, rate_hbm, pair_ref, key_ref, value_ref, rate_ref, sems):
    count = key_ref.shape[0]
    sources = (key_hbm, rate_hbm, value_hbm)
    targets = (key_ref, rate_ref, value_ref)
    copies = [pltpu.make_async_copy(a, b, sems.at[i]) for i, (a, b) in enumerate(zip(sources, targets))]
    for copy in copies:
        copy.start()
    copies[0].wait()
    pair_ref[0] = rms(key_ref[...].astype(F32)).astype(BF)
    copies[1].wait()
    copies[2].wait()
    spread = jnp.broadcast_to(rate_ref[...], (count, count))
    row = lax.broadcasted_iota(jnp.int32, (count, count), 0)
    col = lax.broadcasted_iota(jnp.int32, (count, count), 1)
    rate = jnp.sum(jnp.where(row == col, spread, 0.0), axis=1, keepdims=True)
    pair_ref[1] = (-(rate * value_ref[...].astype(F32))).astype(BF)


def prep(key_tokens, value_tokens, token_rate):
    count = key_tokens.shape[0]
    return call(
        prep_kernel,
        [struct((2, count, D), BF)],
        key_tokens, value_tokens, token_rate.reshape(1, count),
        scratch=[pltpu.VMEM((count, D), BF)] * 2 + [pltpu.VMEM((1, count), F32), pltpu.SemaphoreType.DMA((3,))],
        in_hbm=(0, 1, 2),
        limit=62 * 1024 * 1024,
        name="prep",
    )[0]


def cut(rows):
    return 16 * ((3 * rows + 31) // 32)


def pieces(rows):
    edge = cut(rows)
    found = []
    for m in range(3):
        for low, high, chunk in ((0, edge, 0), (edge, 3 * rows, 1)):
            first, last = max(low, m * rows), min(high, (m + 1) * rows)
            if first < last:
                found.append((m, first - m * rows, last - first, chunk, first - low))
    return found


def stage(weights, pair, queries):
    def kernel(weights_ref, pair_ref, query_ref, weights_out, pair_out, query_out):
        weights_out[...] = weights_ref[...]
        pair_out[...] = pair_ref[...]
        query_out[...] = rms(query_ref[...].astype(F32)).astype(BF)

    return call(kernel, [struct(a.shape, BF) for a in (weights, pair, queries)], weights, pair, queries, name="stage")


def gradient(tokens, blocks, before=None):
    flat = [array for token in tokens for array in token]
    places, at = [], 0
    for token in tokens:
        places.append(((at, 0), (at, 1)) if len(token) == 1 else ((at, None), (at + 1, None)))
        at += len(token)
    count = flat[0].shape[-2]
    number, rows = len(blocks), blocks[0].shape[1]
    aligned = rows % 16 == 0
    if not aligned:
        blocks = [jnp.concatenate(blocks, axis=1)]
    size = blocks[0].shape[1]
    units = number * rows
    given = before is not None

    def kernel(*refs):
        token_refs = refs[:len(flat)]
        block_refs = refs[len(flat):len(flat) + len(blocks)]
        weights = refs[-1]
        total = refs[-2]
        if given:
            base = refs[len(flat) + len(blocks)]
        for i, ref in enumerate(block_refs):
            for m in range(3):
                weights[m * units + i * size:m * units + (i + 1) * size] = ref[m]

        def read(place):
            ref, part = token_refs[place[0]], place[1]
            return ref[...] if part is None else ref[part]

        for j in range(0, len(tokens), 2):
            keys = jnp.concatenate([read(place[0]) for place in places[j:j + 2]], axis=0)
            signal = jnp.concatenate([read(place[1]) for place in places[j:j + 2]], axis=0)
            acts = nt(weights[:2 * units], keys)
            gate_act, up_act = acts[:units], acts[units:]
            sg = jax.nn.sigmoid(gate_act)
            silu = gate_act * sg
            hidden = (silu * up_act).astype(BF)
            hidden_grad = nt(weights[2 * units:], signal)
            gate_grad = (hidden_grad * up_act * sg * (1.0 + gate_act * (1.0 - sg))).astype(BF)
            up_grad = (hidden_grad * silu).astype(BF)
            first = nn(jnp.concatenate([gate_grad, up_grad], axis=0), keys)
            last = nn(hidden, signal)
            if j or given:
                source = total if j else base
                first, last = source[:2 * units] + first, source[2 * units:] + last
            total[:2 * units] = first
            total[2 * units:] = last
        if given and aligned:
            out_refs = refs[len(flat) + len(blocks) + 1:-2]
            for m, row, span, chunk, place in pieces(rows):
                for k in range(number):
                    source = total[m * units + k * rows + row:m * units + k * rows + row + span]
                    out = out_refs[2 * chunk + (k + 1) % 2]
                    out[k // 2, place:place + span] = source.astype(out.dtype)

    edges = (cut(rows), 3 * rows - cut(rows))
    scratch = [pltpu.VMEM((3 * units, D), BF)]
    outs = [struct((3 * units, D), F32)]
    if given and aligned:
        scratch = [pltpu.VMEM((3 * units, D), F32), *scratch]
        outs = [struct((number // 2, edge, D), kind) for edge in edges for kind in (BF, F32)]
    outs = call(
        kernel, outs, *flat, *blocks, *([before] if given else []),
        flops=12 * count * len(tokens) * units * D,
        scratch=scratch,
        name="gradient" if given else "gradient_part",
    )
    if not given:
        return outs[0]
    if aligned:
        return outs[:2], outs[2:]
    total = outs[0].reshape(3, number, rows, D).swapaxes(0, 1).reshape(number, 3 * rows, D)
    parts = total[:, :edges[0]], total[:, edges[0]:]
    return [(part[1::2].astype(BF), part[::2]) for part in parts]


def fold(keep, arrived):
    number, rows = keep.shape[:2]

    def kernel(keep_ref, arrived_ref, send_ref, kept_ref):
        for k in range(number):
            total = keep_ref[k] + arrived_ref[k].astype(F32)
            out = send_ref if k % 2 else kept_ref
            out[k // 2] = total.astype(out.dtype)

    shape = (number // 2, rows, D)
    return call(kernel, [struct(shape, BF), struct(shape, F32)], keep, arrived, name="fold")


def step(old, keep, arrived):
    def kernel(old_ref, keep_ref, arrived_ref, out_ref):
        old_rows = old_ref[...].astype(F32)
        stepped = old_rows - (keep_ref[0] + arrived_ref[0].astype(F32))
        out_ref[...] = (
            stepped
            * jnp.sqrt(jnp.mean(old_rows * old_rows, axis=-1, keepdims=True) + epsilon)
            / jnp.sqrt(jnp.mean(stepped * stepped, axis=-1, keepdims=True) + epsilon)
        ).astype(BF)

    return call(kernel, [struct(old.shape, BF)], old, keep, arrived, name="step")[0]


def attention_kernel(query_ref, key_ref, value_ref, out_ref):
    count = key_ref.shape[0]
    width = 2 * HEAD_DIM
    low = lax.broadcasted_iota(jnp.int32, (count, width), 1) < HEAD_DIM
    zero = jnp.zeros((count, width), BF)
    for h in range(HEADS // 2):
        cols = slice(h * width, (h + 1) * width)
        query, key, value = query_ref[:, cols], key_ref[:, cols], value_ref[:, cols]
        probs = []
        for keep in (low, ~low):
            scores = nt(query, jnp.where(keep, key, zero)) * HEAD_DIM ** (-0.5)
            weights = jnp.exp(scores - jnp.max(scores, axis=-1, keepdims=True))
            probs.append((weights / jnp.sum(weights, axis=-1, keepdims=True)).astype(BF))
        values = jnp.concatenate([jnp.where(low, value, zero), jnp.where(low, zero, value)], axis=0)
        out_ref[:, cols] = nn(jnp.concatenate(probs, axis=1), values)


def attention(queries, key_tokens, value_tokens):
    return call(
        attention_kernel, [struct(queries.shape, F32)], queries, key_tokens, value_tokens,
        flops=4 * queries.shape[0] * key_tokens.shape[0] * D, name="attention",
    )[0]


def apply_rows(queries, blocks, rows, last):
    count = queries[0].shape[0]
    number = len(blocks)
    aligned = rows % 16 == 0
    if not aligned:
        whole = [jnp.concatenate(chunks, axis=0).reshape(3, rows, D) for chunks in blocks]
        blocks = [[jnp.concatenate(whole, axis=1).reshape(3 * number * rows, D)]]
    chunks = [chunk for block in blocks for chunk in block]
    units = number * rows

    def kernel(*refs):
        query_refs = refs[:len(queries)]
        chunk_refs = list(refs[len(queries):len(queries) + len(chunks)])
        out_refs = refs[len(queries) + len(chunks):-1]
        weights = refs[-1]
        if aligned:
            for i, block in enumerate(blocks):
                own_refs = [chunk_refs.pop(0) for _ in block]
                for m, row, size, chunk, place in pieces(rows):
                    start = m * units + i * rows + row
                    if len(block) == 1:
                        weights[start:start + size] = own_refs[0][m * rows + row:m * rows + row + size]
                    else:
                        weights[start:start + size] = own_refs[chunk][place:place + size]
        else:
            weights[...] = chunk_refs[0][...]
        stacked = jnp.concatenate([ref[...] for ref in query_refs], axis=0)
        gate_act = nt(stacked, weights[:units])
        up_act = nt(stacked, weights[units:2 * units])
        hidden = (jax.nn.silu(gate_act) * up_act).astype(BF)
        result = nn(hidden, weights[2 * units:])
        for i, out in enumerate(out_refs):
            out[...] = result[i * count:(i + 1) * count].astype(out.dtype)

    outs = [struct((count, D), BF) for _ in queries[:-1]] + [struct((count, D), last)]
    return call(
        kernel, outs, *queries, *chunks,
        flops=6 * count * len(queries) * units * D,
        scratch=[pltpu.VMEM((3 * units, D), BF)],
        name="apply",
    )


def total_kernel(*refs):
    result = refs[0][...] + refs[1][...]
    for ref in refs[2:-1]:
        result = result + ref[...].astype(F32)
    refs[-1][...] = result.astype(BF)


def solution(mesh):
    n_far, along, layer, swap = moves(mesh)
    bits = [1 << i for i in range(n_far.bit_length() - 1)]

    def line_gather(block, *first):
        blocks = {0: block}
        for bit in reversed(bits):
            for k in list(blocks):
                source = after(blocks[k], *first) if first and k and bit == 1 else blocks[k]
                blocks[k ^ bit] = send(source, along(bit))
        return blocks

    def body(key_tokens, value_tokens, queries, token_rate, fast_weights):
        rows = fast_weights.shape[1]
        pair = prep(key_tokens, value_tokens, token_rate)
        at_x, at_y, corner = [send(pair, layer(*o)) for o in ((1, 0), (0, 1), (1, 1))]
        line = line_gather(fast_weights)
        own_weights, own_pair, query_normed = stage(after(fast_weights, line[bits[-1]]), pair, queries)
        own_there = send(after(own_pair, at_x, *[line[k] for k in range(1, n_far)]), swap)
        blocks = [own_weights] + [line[k] for k in range(1, n_far)]
        part = gradient([(token,) for token in (own_pair, own_there, at_x, send(at_x, swap))], blocks)
        late = [at_y, corner, send(at_y, swap), send(corner, swap)]
        chunks = gradient([(token,) for token in late], blocks, part)

        query_normed = after(query_normed, chunks[0][0])
        all_queries = [send(query_normed, layer(*o)) for o in ((1, 0), (0, 1))]
        mixed = attention(queries, key_tokens, value_tokens)

        flat = own_weights.reshape(3 * rows, D)
        olds = flat[:cut(rows)], flat[cut(rows):]
        stepped = []
        for old, (part, keep) in zip(olds, chunks):
            for bit in bits[:-1]:
                arrived = send(part, along(bit))
                part, keep = fold(keep, arrived)
            updated = step(old, keep, send(part, along(bits[-1])))
            stepped.append(line_gather(updated, *[chunk[1] for chunk in stepped]))
        corner_query = send(after(query_normed, *all_queries), layer(1, 1))
        blocks = [[chunk[k] for chunk in stepped] for k in range(n_far)]
        there = [[send(array, swap) for array in block] for block in blocks[:-1]]
        there.append([send(after(array, corner_query), swap) for array in blocks[-1]])
        blocks += there

        outs = apply_rows([corner_query, *all_queries], blocks, rows, BF)
        back = [send(part, layer(*o)) for part, o in zip(outs, ((1, 1), (1, 0), (0, 1)))]
        outs += apply_rows([query_normed], blocks, rows, F32)
        return call(total_kernel, [struct(queries.shape, BF)], outs[-1], mixed, *back, name="total")[0]

    in_specs = (
        P(("grp", "dev"), None),
        P(("grp", "dev"), None),
        P(("grp", "dev"), None),
        P(("grp", "dev")),
        P(None, ("grp", "dev"), None),
    )
    out_specs = P(("grp", "dev"), None)
    return jax.shard_map(body, mesh=mesh, in_specs=in_specs, out_specs=out_specs, check_vma=False)
```

```python
import jax
import jax.numpy as jnp
from jax import lax
from jax.experimental import pallas as pl
from jax.experimental.pallas import tpu as pltpu
from jax.sharding import PartitionSpec as P

D = 768
HEADS = 12
HEAD_DIM = 64
CORES = 2
NEAR = 2
BF = jnp.bfloat16
F32 = jnp.float32

epsilon = 1e-06
AXES = ("grp", "dev")


def moves(mesh):
    n_grp, n_dev = mesh.shape["grp"], mesh.shape["dev"]
    n_gx, n_far = n_grp // CORES, n_dev // NEAR

    def build(target):
        pairs = []
        for gx in range(n_gx):
            for core in range(CORES):
                for far in range(n_far):
                    for near in range(NEAR):
                        to = target(gx, core, far, near)
                        source = (gx * CORES + core) * n_dev + far * NEAR + near
                        dest = (to[0] * CORES + to[1]) * n_dev + to[2] * NEAR + to[3]
                        pairs.append((source, dest))
        return pairs

    def along(step):
        return build(lambda gx, core, far, near: (gx, core, far ^ step, near))

    def layer(dx, dn):
        return build(lambda gx, core, far, near: (gx ^ dx, core, far, near ^ dn))

    swap = build(lambda gx, core, far, near: (gx, 1 - core, far, near))
    return n_far, along, layer, swap


def send(array, pairs):
    return lax.ppermute(array, AXES, pairs)


def after(value, *others):
    return lax.optimization_barrier((value, *others))[0]


def call(kernel, outs, *args, flops=0, scratch=(), in_hbm=(), limit=32 * 1024 * 1024, name=None):
    vmem = pl.BlockSpec(memory_space=pltpu.VMEM)
    size = sum(a.size * a.dtype.itemsize for a in args) + sum(o.size * o.dtype.itemsize for o in outs)
    result = pl.pallas_call(
        kernel,
        out_shape=list(outs),
        in_specs=[pl.BlockSpec(memory_space=pltpu.HBM) if i in in_hbm else vmem for i in range(len(args))],
        out_specs=[vmem] * len(outs),
        scratch_shapes=list(scratch),
        compiler_params=pltpu.CompilerParams(vmem_limit_bytes=limit),
        cost_estimate=pl.CostEstimate(flops=flops, bytes_accessed=size, transcendentals=0),
        name=name,
    )(*args)
    return result


def struct(shape, dtype):
    return jax.ShapeDtypeStruct(shape, dtype)


def nt(a, b):
    return lax.dot_general(a, b, (((1,), (1,)), ((), ())), preferred_element_type=F32)


def nn(a, b):
    return lax.dot_general(a, b, (((1,), (0,)), ((), ())), preferred_element_type=F32)


def rms(matrix):
    return matrix / jnp.sqrt(jnp.mean(matrix * matrix, axis=-1, keepdims=True) + epsilon)


def prep_kernel(key_hbm, value_hbm, rate_hbm, pair_ref, key_ref, value_ref, rate_ref, sems):
    count = key_ref.shape[0]
    sources = (key_hbm, rate_hbm, value_hbm)
    targets = (key_ref, rate_ref, value_ref)
    copies = [pltpu.make_async_copy(a, b, sems.at[i]) for i, (a, b) in enumerate(zip(sources, targets))]
    for copy in copies:
        copy.start()
    copies[0].wait()
    pair_ref[0] = rms(key_ref[...].astype(F32)).astype(BF)
    copies[1].wait()
    copies[2].wait()
    spread = jnp.broadcast_to(rate_ref[...], (count, count))
    row = lax.broadcasted_iota(jnp.int32, (count, count), 0)
    col = lax.broadcasted_iota(jnp.int32, (count, count), 1)
    rate = jnp.sum(jnp.where(row == col, spread, 0.0), axis=1, keepdims=True)
    pair_ref[1] = (-(rate * value_ref[...].astype(F32))).astype(BF)


def prep(key_tokens, value_tokens, token_rate):
    count = key_tokens.shape[0]
    return call(
        prep_kernel,
        [struct((2, count, D), BF)],
        key_tokens, value_tokens, token_rate.reshape(1, count),
        scratch=[pltpu.VMEM((count, D), BF)] * 2 + [pltpu.VMEM((1, count), F32), pltpu.SemaphoreType.DMA((3,))],
        in_hbm=(0, 1, 2),
        limit=62 * 1024 * 1024,
        name="prep",
    )[0]


def cut(rows):
    return 16 * ((3 * rows + 31) // 32)


def pieces(rows):
    edge = cut(rows)
    found = []
    for m in range(3):
        for low, high, chunk in ((0, edge, 0), (edge, 3 * rows, 1)):
            first, last = max(low, m * rows), min(high, (m + 1) * rows)
            if first < last:
                found.append((m, first - m * rows, last - first, chunk, first - low))
    return found


def stage(weights, pair, queries):
    def kernel(weights_ref, pair_ref, query_ref, weights_out, pair_out, query_out):
        weights_out[...] = weights_ref[...]
        pair_out[...] = pair_ref[...]
        query_out[...] = rms(query_ref[...].astype(F32)).astype(BF)

    return call(kernel, [struct(a.shape, BF) for a in (weights, pair, queries)], weights, pair, queries, name="stage")


def gradient(tokens, blocks, before=None):
    flat = [array for token in tokens for array in token]
    places, at = [], 0
    for token in tokens:
        places.append(((at, 0), (at, 1)) if len(token) == 1 else ((at, None), (at + 1, None)))
        at += len(token)
    count = flat[0].shape[-2]
    number, rows = len(blocks), blocks[0].shape[1]
    aligned = rows % 16 == 0
    units = number * rows
    given = before is not None
    if given:
        blocks = before
    elif not aligned:
        blocks = [jnp.concatenate(blocks, axis=1)]
    size = blocks[0].shape[1]

    def kernel(*refs):
        token_refs = refs[:len(flat)]
        block_refs = refs[len(flat):len(flat) + len(blocks)]
        if given:
            weights, base = block_refs
            total = refs[-1]
        else:
            total, weights = refs[-2:]
            for i, ref in enumerate(block_refs):
                for m in range(3):
                    weights[m * units + i * size:m * units + (i + 1) * size] = ref[m]

        def read(place):
            ref, part = token_refs[place[0]], place[1]
            return ref[...] if part is None else ref[part]

        for j in range(0, len(tokens), 2):
            keys = jnp.concatenate([read(place[0]) for place in places[j:j + 2]], axis=0)
            signal = jnp.concatenate([read(place[1]) for place in places[j:j + 2]], axis=0)
            acts = nt(weights[:2 * units], keys)
            gate_act, up_act = acts[:units], acts[units:]
            sg = jax.nn.sigmoid(gate_act)
            silu = gate_act * sg
            hidden = (silu * up_act).astype(BF)
            hidden_grad = nt(weights[2 * units:], signal)
            gate_grad = (hidden_grad * up_act * sg * (1.0 + gate_act * (1.0 - sg))).astype(BF)
            up_grad = (hidden_grad * silu).astype(BF)
            first = nn(jnp.concatenate([gate_grad, up_grad], axis=0), keys)
            last = nn(hidden, signal)
            if j or given:
                source = total if j else base
                first, last = source[:2 * units] + first, source[2 * units:] + last
            total[:2 * units] = first
            total[2 * units:] = last
        if given and aligned:
            out_refs = refs[len(flat) + len(blocks):-1]
            for m, row, span, chunk, place in pieces(rows):
                for k in range(number):
                    source = total[m * units + k * rows + row:m * units + k * rows + row + span]
                    out = out_refs[2 * chunk + (k + 1) % 2]
                    out[k // 2, place:place + span] = source.astype(out.dtype)

    edges = (cut(rows), 3 * rows - cut(rows))
    scratch = []
    outs = [struct((3 * units, D), F32)]
    if not given:
        outs.append(struct((3 * units, D), BF))
    elif aligned:
        scratch = [pltpu.VMEM((3 * units, D), F32)]
        outs = [struct((number // 2, edge, D), kind) for edge in edges for kind in (BF, F32)]
    outs = call(
        kernel, outs, *flat, *blocks,
        flops=12 * count * len(tokens) * units * D,
        scratch=scratch,
        name="gradient" if given else "gradient_part",
    )
    if not given:
        return outs[1], outs[0]
    if aligned:
        return outs[:2], outs[2:]
    total = outs[0].reshape(3, number, rows, D).swapaxes(0, 1).reshape(number, 3 * rows, D)
    parts = total[:, :edges[0]], total[:, edges[0]:]
    return [(part[1::2].astype(BF), part[::2]) for part in parts]


def fold(keep, arrived):
    number, rows = keep.shape[:2]

    def kernel(keep_ref, arrived_ref, send_ref, kept_ref):
        for k in range(number):
            total = keep_ref[k] + arrived_ref[k].astype(F32)
            out = send_ref if k % 2 else kept_ref
            out[k // 2] = total.astype(out.dtype)

    shape = (number // 2, rows, D)
    return call(kernel, [struct(shape, BF), struct(shape, F32)], keep, arrived, name="fold")


def step(old, keep, arrived):
    def kernel(old_ref, keep_ref, arrived_ref, out_ref):
        old_rows = old_ref[...].astype(F32)
        stepped = old_rows - (keep_ref[0] + arrived_ref[0].astype(F32))
        out_ref[...] = (
            stepped
            * jnp.sqrt(jnp.mean(old_rows * old_rows, axis=-1, keepdims=True) + epsilon)
            / jnp.sqrt(jnp.mean(stepped * stepped, axis=-1, keepdims=True) + epsilon)
        ).astype(BF)

    return call(kernel, [struct(old.shape, BF)], old, keep, arrived, name="step")[0]


def attention_kernel(query_ref, key_ref, value_ref, out_ref):
    count = key_ref.shape[0]
    width = 2 * HEAD_DIM
    low = lax.broadcasted_iota(jnp.int32, (count, width), 1) < HEAD_DIM
    zero = jnp.zeros((count, width), BF)
    for h in range(HEADS // 2):
        cols = slice(h * width, (h + 1) * width)
        query, key, value = query_ref[:, cols], key_ref[:, cols], value_ref[:, cols]
        probs = []
        for keep in (low, ~low):
            scores = nt(query, jnp.where(keep, key, zero)) * HEAD_DIM ** (-0.5)
            weights = jnp.exp(scores - jnp.max(scores, axis=-1, keepdims=True))
            probs.append((weights / jnp.sum(weights, axis=-1, keepdims=True)).astype(BF))
        values = jnp.concatenate([jnp.where(low, value, zero), jnp.where(low, zero, value)], axis=0)
        out_ref[:, cols] = nn(jnp.concatenate(probs, axis=1), values)


def attention(queries, key_tokens, value_tokens):
    return call(
        attention_kernel, [struct(queries.shape, F32)], queries, key_tokens, value_tokens,
        flops=4 * queries.shape[0] * key_tokens.shape[0] * D, name="attention",
    )[0]


def apply_rows(queries, blocks, rows, last):
    count = queries[0].shape[0]
    number = len(blocks)
    aligned = rows % 16 == 0
    if not aligned:
        whole = [jnp.concatenate(chunks, axis=0).reshape(3, rows, D) for chunks in blocks]
        blocks = [[jnp.concatenate(whole, axis=1).reshape(3 * number * rows, D)]]
    chunks = [chunk for block in blocks for chunk in block]
    units = number * rows

    def kernel(*refs):
        query_refs = refs[:len(queries)]
        chunk_refs = list(refs[len(queries):len(queries) + len(chunks)])
        out_refs = refs[len(queries) + len(chunks):-1]
        weights = refs[-1]
        if aligned:
            for i, block in enumerate(blocks):
                own_refs = [chunk_refs.pop(0) for _ in block]
                for m, row, size, chunk, place in pieces(rows):
                    start = m * units + i * rows + row
                    if len(block) == 1:
                        weights[start:start + size] = own_refs[0][m * rows + row:m * rows + row + size]
                    else:
                        weights[start:start + size] = own_refs[chunk][place:place + size]
        else:
            weights[...] = chunk_refs[0][...]
        stacked = jnp.concatenate([ref[...] for ref in query_refs], axis=0)
        gate_act = nt(stacked, weights[:units])
        up_act = nt(stacked, weights[units:2 * units])
        hidden = (jax.nn.silu(gate_act) * up_act).astype(BF)
        result = nn(hidden, weights[2 * units:])
        for i, out in enumerate(out_refs):
            out[...] = result[i * count:(i + 1) * count].astype(out.dtype)

    outs = [struct((count, D), BF) for _ in queries[:-1]] + [struct((count, D), last)]
    return call(
        kernel, outs, *queries, *chunks,
        flops=6 * count * len(queries) * units * D,
        scratch=[pltpu.VMEM((3 * units, D), BF)],
        name="apply",
    )


def total_kernel(*refs):
    result = refs[0][...] + refs[1][...]
    for ref in refs[2:-1]:
        result = result + ref[...].astype(F32)
    refs[-1][...] = result.astype(BF)


def solution(mesh):
    n_far, along, layer, swap = moves(mesh)
    bits = [1 << i for i in range(n_far.bit_length() - 1)]

    def line_gather(block, *first):
        blocks = {0: block}
        for bit in reversed(bits):
            for k in list(blocks):
                source = after(blocks[k], *first) if first and k and bit == 1 else blocks[k]
                blocks[k ^ bit] = send(source, along(bit))
        return blocks

    def body(key_tokens, value_tokens, queries, token_rate, fast_weights):
        rows = fast_weights.shape[1]
        pair = prep(key_tokens, value_tokens, token_rate)
        at_x, at_y, corner = [send(pair, layer(*o)) for o in ((1, 0), (0, 1), (1, 1))]
        line = line_gather(fast_weights)
        own_weights, own_pair, query_normed = stage(after(fast_weights, line[bits[-1]]), pair, queries)
        own_there = send(after(own_pair, at_x, *[line[k] for k in range(1, n_far)]), swap)
        blocks = [own_weights] + [line[k] for k in range(1, n_far)]
        part = gradient([(token,) for token in (own_pair, own_there, at_x, send(at_x, swap))], blocks)
        late = [at_y, corner, send(at_y, swap), send(corner, swap)]
        chunks = gradient([(token,) for token in late], blocks, part)

        query_normed = after(query_normed, chunks[0][0])
        all_queries = [send(query_normed, layer(*o)) for o in ((1, 0), (0, 1))]
        mixed = attention(queries, key_tokens, value_tokens)

        flat = own_weights.reshape(3 * rows, D)
        olds = flat[:cut(rows)], flat[cut(rows):]
        stepped = []
        for old, (part, keep) in zip(olds, chunks):
            for bit in bits[:-1]:
                arrived = send(part, along(bit))
                part, keep = fold(keep, arrived)
            updated = step(old, keep, send(part, along(bits[-1])))
            stepped.append(line_gather(updated, *[chunk[1] for chunk in stepped]))
        corner_query = send(after(query_normed, *all_queries), layer(1, 1))
        blocks = [[chunk[k] for chunk in stepped] for k in range(n_far)]
        there = [[send(array, swap) for array in block] for block in blocks[:-1]]
        there.append([send(after(array, corner_query), swap) for array in blocks[-1]])
        blocks += there

        outs = apply_rows([*all_queries, corner_query], blocks, rows, BF)
        back = [send(part, layer(*o)) for part, o in zip(outs, ((1, 0), (0, 1), (1, 1)))]
        outs += apply_rows([query_normed], blocks, rows, F32)
        return call(total_kernel, [struct(queries.shape, BF)], outs[-1], mixed, *back, name="total")[0]

    in_specs = (
        P(("grp", "dev"), None),
        P(("grp", "dev"), None),
        P(("grp", "dev"), None),
        P(("grp", "dev")),
        P(None, ("grp", "dev"), None),
    )
    out_specs = P(("grp", "dev"), None)
    return jax.shard_map(body, mesh=mesh, in_specs=in_specs, out_specs=out_specs, check_vma=False)
```

```python
import jax
import jax.numpy as jnp
from jax import lax
from jax.experimental import pallas as pl
from jax.experimental.pallas import tpu as pltpu
from jax.sharding import PartitionSpec as P

D = 768
HEADS = 12
HEAD_DIM = 64
CORES = 2
NEAR = 2
BF = jnp.bfloat16
F32 = jnp.float32

epsilon = 1e-06
AXES = ("grp", "dev")


def moves(mesh):
    n_grp, n_dev = mesh.shape["grp"], mesh.shape["dev"]
    n_gx, n_far = n_grp // CORES, n_dev // NEAR

    def build(target):
        pairs = []
        for gx in range(n_gx):
            for core in range(CORES):
                for far in range(n_far):
                    for near in range(NEAR):
                        to = target(gx, core, far, near)
                        source = (gx * CORES + core) * n_dev + far * NEAR + near
                        dest = (to[0] * CORES + to[1]) * n_dev + to[2] * NEAR + to[3]
                        pairs.append((source, dest))
        return pairs

    def along(step):
        return build(lambda gx, core, far, near: (gx, core, far ^ step, near))

    def layer(dx, dn):
        return build(lambda gx, core, far, near: (gx ^ dx, core, far, near ^ dn))

    swap = build(lambda gx, core, far, near: (gx, 1 - core, far, near))
    return n_far, along, layer, swap


def send(array, pairs):
    return lax.ppermute(array, AXES, pairs)


def after(value, *others):
    return lax.optimization_barrier((value, *others))[0]


def call(kernel, outs, *args, flops=0, scratch=(), in_hbm=(), limit=32 * 1024 * 1024, name=None):
    vmem = pl.BlockSpec(memory_space=pltpu.VMEM)
    size = sum(a.size * a.dtype.itemsize for a in args) + sum(o.size * o.dtype.itemsize for o in outs)
    result = pl.pallas_call(
        kernel,
        out_shape=list(outs),
        in_specs=[pl.BlockSpec(memory_space=pltpu.HBM) if i in in_hbm else vmem for i in range(len(args))],
        out_specs=[vmem] * len(outs),
        scratch_shapes=list(scratch),
        compiler_params=pltpu.CompilerParams(vmem_limit_bytes=limit),
        cost_estimate=pl.CostEstimate(flops=flops, bytes_accessed=size, transcendentals=0),
        name=name,
    )(*args)
    return result


def struct(shape, dtype):
    return jax.ShapeDtypeStruct(shape, dtype)


def nt(a, b):
    return lax.dot_general(a, b, (((1,), (1,)), ((), ())), preferred_element_type=F32)


def nn(a, b):
    return lax.dot_general(a, b, (((1,), (0,)), ((), ())), preferred_element_type=F32)


def rms(matrix):
    return matrix / jnp.sqrt(jnp.mean(matrix * matrix, axis=-1, keepdims=True) + epsilon)


def prep_kernel(key_hbm, value_hbm, rate_hbm, pair_ref, key_ref, value_ref, rate_ref, sems):
    count = key_ref.shape[0]
    sources = (key_hbm, rate_hbm, value_hbm)
    targets = (key_ref, rate_ref, value_ref)
    copies = [pltpu.make_async_copy(a, b, sems.at[i]) for i, (a, b) in enumerate(zip(sources, targets))]
    for copy in copies:
        copy.start()
    copies[0].wait()
    pair_ref[0] = rms(key_ref[...].astype(F32)).astype(BF)
    copies[1].wait()
    copies[2].wait()
    spread = jnp.broadcast_to(rate_ref[...], (count, count))
    row = lax.broadcasted_iota(jnp.int32, (count, count), 0)
    col = lax.broadcasted_iota(jnp.int32, (count, count), 1)
    rate = jnp.sum(jnp.where(row == col, spread, 0.0), axis=1, keepdims=True)
    pair_ref[1] = (-(rate * value_ref[...].astype(F32))).astype(BF)


def prep(key_tokens, value_tokens, token_rate):
    count = key_tokens.shape[0]
    return call(
        prep_kernel,
        [struct((2, count, D), BF)],
        key_tokens, value_tokens, token_rate.reshape(1, count),
        scratch=[pltpu.VMEM((count, D), BF)] * 2 + [pltpu.VMEM((1, count), F32), pltpu.SemaphoreType.DMA((3,))],
        in_hbm=(0, 1, 2),
        limit=62 * 1024 * 1024,
        name="prep",
    )[0]


def cut(rows):
    return 16 * ((3 * rows + 31) // 32)


def pieces(rows):
    edge = cut(rows)
    found = []
    for m in range(3):
        for low, high, chunk in ((0, edge, 0), (edge, 3 * rows, 1)):
            first, last = max(low, m * rows), min(high, (m + 1) * rows)
            if first < last:
                found.append((m, first - m * rows, last - first, chunk, first - low))
    return found


def stage(weights, pair, queries):
    def kernel(weights_ref, pair_ref, query_ref, weights_out, pair_out, query_out):
        weights_out[...] = weights_ref[...]
        pair_out[...] = pair_ref[...]
        query_out[...] = rms(query_ref[...].astype(F32)).astype(BF)

    return call(kernel, [struct(a.shape, BF) for a in (weights, pair, queries)], weights, pair, queries, name="stage")


def gradient(tokens, blocks, before=None):
    flat = [array for token in tokens for array in token]
    places, at = [], 0
    for token in tokens:
        places.append(((at, 0), (at, 1)) if len(token) == 1 else ((at, None), (at + 1, None)))
        at += len(token)
    count = flat[0].shape[-2]
    number, rows = len(blocks), blocks[0].shape[1]
    aligned = rows % 16 == 0
    units = number * rows
    given = before is not None
    if given:
        blocks = before
    elif not aligned:
        blocks = [jnp.concatenate(blocks, axis=1)]
    size = blocks[0].shape[1]

    def kernel(*refs):
        token_refs = refs[:len(flat)]
        block_refs = refs[len(flat):len(flat) + len(blocks)]
        if given:
            weights, base = block_refs
            total = refs[-1]
        else:
            total, weights = refs[-2:]
            for i, ref in enumerate(block_refs):
                for m in range(3):
                    weights[m * units + i * size:m * units + (i + 1) * size] = ref[m]

        def read(place):
            ref, part = token_refs[place[0]], place[1]
            return ref[...] if part is None else ref[part]

        for j in range(0, len(tokens), 2):
            keys = jnp.concatenate([read(place[0]) for place in places[j:j + 2]], axis=0)
            signal = jnp.concatenate([read(place[1]) for place in places[j:j + 2]], axis=0)
            acts = nt(weights[:2 * units], keys)
            gate_act, up_act = acts[:units], acts[units:]
            sg = jax.nn.sigmoid(gate_act)
            silu = gate_act * sg
            hidden = (silu * up_act).astype(BF)
            hidden_grad = nt(weights[2 * units:], signal)
            gate_grad = (hidden_grad * up_act * sg * (1.0 + gate_act * (1.0 - sg))).astype(BF)
            up_grad = (hidden_grad * silu).astype(BF)
            first = nn(jnp.concatenate([gate_grad, up_grad], axis=0), keys)
            last = nn(hidden, signal)
            if j or given:
                source = total if j else base
                first, last = source[:2 * units] + first, source[2 * units:] + last
            total[:2 * units] = first
            total[2 * units:] = last
        if given and aligned:
            out_refs = refs[len(flat) + len(blocks):-1]
            for m, row, span, chunk, place in pieces(rows):
                for k in range(number):
                    source = total[m * units + k * rows + row:m * units + k * rows + row + span]
                    out = out_refs[2 * chunk + (k + 1) % 2]
                    out[k // 2, place:place + span] = source.astype(out.dtype)

    edges = (cut(rows), 3 * rows - cut(rows))
    scratch = []
    outs = [struct((3 * units, D), F32)]
    if not given:
        outs.append(struct((3 * units, D), BF))
    elif aligned:
        scratch = [pltpu.VMEM((3 * units, D), F32)]
        outs = [struct((number // 2, edge, D), kind) for edge in edges for kind in (BF, F32)]
    outs = call(
        kernel, outs, *flat, *blocks,
        flops=12 * count * len(tokens) * units * D,
        scratch=scratch,
        name="gradient" if given else "gradient_part",
    )
    if not given:
        return outs[1], outs[0]
    if aligned:
        return outs[:2], outs[2:]
    total = outs[0].reshape(3, number, rows, D).swapaxes(0, 1).reshape(number, 3 * rows, D)
    parts = total[:, :edges[0]], total[:, edges[0]:]
    return [(part[1::2].astype(BF), part[::2]) for part in parts]


def fold(keep, arrived):
    number, rows = keep.shape[:2]

    def kernel(keep_ref, arrived_ref, send_ref, kept_ref):
        for k in range(number):
            total = keep_ref[k] + arrived_ref[k].astype(F32)
            out = send_ref if k % 2 else kept_ref
            out[k // 2] = total.astype(out.dtype)

    shape = (number // 2, rows, D)
    return call(kernel, [struct(shape, BF), struct(shape, F32)], keep, arrived, name="fold")


def step(old, keep, arrived):
    def kernel(old_ref, keep_ref, arrived_ref, out_ref):
        old_rows = old_ref[...].astype(F32)
        stepped = old_rows - (keep_ref[0] + arrived_ref[0].astype(F32))
        out_ref[...] = (
            stepped
            * jnp.sqrt(jnp.mean(old_rows * old_rows, axis=-1, keepdims=True) + epsilon)
            / jnp.sqrt(jnp.mean(stepped * stepped, axis=-1, keepdims=True) + epsilon)
        ).astype(BF)

    return call(kernel, [struct(old.shape, BF)], old, keep, arrived, name="step")[0]


def attention_kernel(query_ref, key_ref, value_ref, out_ref):
    count = key_ref.shape[0]
    width = 2 * HEAD_DIM
    low = lax.broadcasted_iota(jnp.int32, (count, width), 1) < HEAD_DIM
    zero = jnp.zeros((count, width), BF)
    for h in range(HEADS // 2):
        cols = slice(h * width, (h + 1) * width)
        query, key, value = query_ref[:, cols], key_ref[:, cols], value_ref[:, cols]
        probs = []
        for keep in (low, ~low):
            scores = nt(query, jnp.where(keep, key, zero)) * HEAD_DIM ** (-0.5)
            weights = jnp.exp(scores - jnp.max(scores, axis=-1, keepdims=True))
            probs.append((weights / jnp.sum(weights, axis=-1, keepdims=True)).astype(BF))
        values = jnp.concatenate([jnp.where(low, value, zero), jnp.where(low, zero, value)], axis=0)
        out_ref[:, cols] = nn(jnp.concatenate(probs, axis=1), values)


def attention(queries, key_tokens, value_tokens):
    return call(
        attention_kernel, [struct(queries.shape, F32)], queries, key_tokens, value_tokens,
        flops=4 * queries.shape[0] * key_tokens.shape[0] * D, name="attention",
    )[0]


def apply_rows(queries, blocks, rows, last):
    count = queries[0].shape[0]
    number = len(blocks)
    aligned = rows % 16 == 0
    if not aligned:
        whole = [jnp.concatenate(chunks, axis=0).reshape(3, rows, D) for chunks in blocks]
        blocks = [[jnp.concatenate(whole, axis=1).reshape(3 * number * rows, D)]]
    chunks = [chunk for block in blocks for chunk in block]
    units = number * rows

    def kernel(*refs):
        query_refs = refs[:len(queries)]
        chunk_refs = list(refs[len(queries):len(queries) + len(chunks)])
        out_refs = refs[len(queries) + len(chunks):-1]
        weights = refs[-1]
        if aligned:
            for i, block in enumerate(blocks):
                own_refs = [chunk_refs.pop(0) for _ in block]
                for m, row, size, chunk, place in pieces(rows):
                    start = m * units + i * rows + row
                    if len(block) == 1:
                        weights[start:start + size] = own_refs[0][m * rows + row:m * rows + row + size]
                    else:
                        weights[start:start + size] = own_refs[chunk][place:place + size]
        else:
            weights[...] = chunk_refs[0][...]
        stacked = jnp.concatenate([ref[...] for ref in query_refs], axis=0)
        gate_act = nt(stacked, weights[:units])
        up_act = nt(stacked, weights[units:2 * units])
        hidden = (jax.nn.silu(gate_act) * up_act).astype(BF)
        result = nn(hidden, weights[2 * units:])
        for i, out in enumerate(out_refs):
            out[...] = result[i * count:(i + 1) * count].astype(out.dtype)

    outs = [struct((count, D), BF) for _ in queries[:-1]] + [struct((count, D), last)]
    return call(
        kernel, outs, *queries, *chunks,
        flops=6 * count * len(queries) * units * D,
        scratch=[pltpu.VMEM((3 * units, D), BF)],
        name="apply",
    )


def total_kernel(*refs):
    result = refs[0][...] + refs[1][...]
    for ref in refs[2:-1]:
        result = result + ref[...].astype(F32)
    refs[-1][...] = result.astype(BF)


def solution(mesh):
    n_far, along, layer, swap = moves(mesh)
    bits = [1 << i for i in range(n_far.bit_length() - 1)]

    def line_gather(block, *first):
        blocks = {0: block}
        for bit in reversed(bits):
            for k in list(blocks):
                source = after(blocks[k], *first) if first and k and bit == 1 else blocks[k]
                blocks[k ^ bit] = send(source, along(bit))
        return blocks

    def body(key_tokens, value_tokens, queries, token_rate, fast_weights):
        rows = fast_weights.shape[1]
        pair = prep(key_tokens, value_tokens, token_rate)
        at_x, at_y, corner = [send(pair, layer(*o)) for o in ((1, 0), (0, 1), (1, 1))]
        line = line_gather(fast_weights)
        own_weights, own_pair, query_normed = stage(after(fast_weights, line[bits[-1]]), pair, queries)
        own_there = send(after(own_pair, at_x, *[line[k] for k in range(1, n_far)]), swap)
        blocks = [own_weights] + [line[k] for k in range(1, n_far)]
        part = gradient([(token,) for token in (own_pair, own_there, at_x, send(at_x, swap))], blocks)
        late = [at_y, corner, send(at_y, swap), send(corner, swap)]
        chunks = gradient([(token,) for token in late], blocks, part)

        query_normed = after(query_normed, chunks[0][0])
        all_queries = [send(query_normed, layer(*o)) for o in ((1, 0), (0, 1))]
        mixed = attention(queries, key_tokens, value_tokens)

        flat = own_weights.reshape(3 * rows, D)
        olds = flat[:cut(rows)], flat[cut(rows):]
        stepped = []
        for old, (part, keep) in zip(olds, chunks):
            for bit in bits[:-1]:
                arrived = send(part, along(bit))
                part, keep = fold(keep, arrived)
            updated = step(old, keep, send(part, along(bits[-1])))
            stepped.append(line_gather(updated, *[chunk[1] for chunk in stepped]))
        corner_query = send(after(query_normed, *all_queries), layer(1, 1))
        blocks = [[chunk[k] for chunk in stepped] for k in range(n_far)]
        there = [[send(array, swap) for array in block] for block in blocks[:-1]]
        there.append([send(after(array, corner_query), swap) for array in blocks[-1]])
        blocks += there

        outs = apply_rows(all_queries, blocks, rows, BF)
        outs += apply_rows([corner_query, query_normed], blocks, rows, F32)
        back = [send(part, layer(*o)) for part, o in zip(outs, ((1, 0), (0, 1), (1, 1)))]
        return call(total_kernel, [struct(queries.shape, BF)], outs[-1], mixed, *back, name="total")[0]

    in_specs = (
        P(("grp", "dev"), None),
        P(("grp", "dev"), None),
        P(("grp", "dev"), None),
        P(("grp", "dev")),
        P(None, ("grp", "dev"), None),
    )
    out_specs = P(("grp", "dev"), None)
    return jax.shard_map(body, mesh=mesh, in_specs=in_specs, out_specs=out_specs, check_vma=False)
```
